32 devices in a mesh: section: 2 (over x), edge: 8 (over z, y), mp: 2 (over core).
Axes of the slice: x: 2, y: 2, z: 4, core: 2. Of those that a mesh axis runs over, the one named last changes fastest.
Arguments:
- edge_vectors: float32 [3, 3, 3072], P(None, None, 'edge'), as said below
- edge_species: int32 [3, 2, 3072], P(None, None, 'edge'), may hold values from 0 to 3
- centres: int32 [3, 3072], P(None, 'edge'), may hold values from 0 to 319, as said below
- edge_mask: int32 [3, 3072], P(None, 'edge'), may hold values 0 or 1
- structures: int32 [3, 3072], P(None, 'edge'), may hold values from 0 to 15, never falling along the last dimension, each value on 1 to 384 neighbouring positions
- energy_cot: float32 [3, 16], replicated, may hold values from -6 to 6
- embed_in: float32 [16, 1024], replicated, may hold values from -1.5 to 1.5
- section_head: float32 [2, 1024, 1024], P('section', None, 'mp'), may hold values from -0.5 to 0.5
- env_weight: float32 [2, 1024, 64], P('section'), may hold values from -0.375 to 0.375
- mix_weight: float32 [3, 64, 64], replicated, may hold values from -0.75 to 0.75
- w_in: float32 [2, 1216, 1024], P('section', None, 'mp'), may hold values from -0.15625 to 0.15625
- w_out: float32 [2, 1024, 1024], P('section', 'mp'), may hold values from -0.1875 to 0.1875
- read_weight: float32 [1024], replicated, may hold values from -0.046875 to 0.046875
Outputs:
- energies: float32 [3, 16], replicated
- edge_forces: float32 [3, 3, 3072], P(None, None, 'edge')
- embed_grad: float32 [16, 1024], replicated
- head_grad: float32 [2, 1024, 1024], P('section', None, 'mp')
- env_grad: float32 [2, 1024, 64], P('section')
- mix_grad: float32 [3, 64, 64], replicated
- w_in_grad: float32 [2, 1216, 1024], P('section', None, 'mp')
- w_out_grad: float32 [2, 1024, 1024], P('section', 'mp')
- read_grad: float32 [1024], replicated
The draws below stay inside these ranges and needn't reach their ends.
Inputs may be any that keep to these rules, and one draw needn't show every extreme that they name: `edge_vectors`: every edge vector is 0.4 to 5.3 long. `centres`: an edge in the block b of 384 edges of a micro-batch has its centre among atoms (b - 1) * 40 to (b + 2) * 40 - 1.
All inputs are finite; a program needn't handle non-finite values. No bound on the sum of `edge_mask` on one device may be relied on, other than what follows from the above.
Results may differ from the reference program's by a relative error of at most 0.0003.
Values sent between devices are 32-bit elements; how exact they have to be, the bound alone decides.
No kernel may reach another device: no remote copies, remote signals or barrier semaphores. Data moves between devices by JAX's collectives and lax.ppermute only.
A program may use at most 192 MiB of HBM per device.

```python
import math
import jax
import jax.numpy as jnp
import numpy as np
from jax import lax

D = 1024
CH = 64
NBES = 8
NSPEC = 4
EDGE_DEV = 384
ATOM_DEV = 40
MICRO = 3
STRUCTS = 16
EDGES_MB = 3072
ATOMS = 320
FEAT = 16
N_SECTION = 2


def draw_edge_vectors(key, part):
    key = jax.random.fold_in(key, 5)
    direction_key, length_key = jax.random.split(key)
    direction = jax.random.normal(direction_key, (MICRO, 3, EDGES_MB), jnp.float32)
    norm_value = jnp.sqrt(jnp.sum(direction * direction, axis=1, keepdims=True) + 1e-06)
    uniform_value = jax.random.uniform(length_key, (MICRO, 1, EDGES_MB), jnp.float32)
    length = 0.4 + 4.9 * uniform_value
    return direction / norm_value * length


def draw_centres(key, part):
    key = jax.random.fold_in(key, 11)
    position = jnp.arange(EDGES_MB, dtype=jnp.int32)
    block_ids = position // EDGE_DEV
    within = position % EDGE_DEV
    offsets = jax.random.randint(key, (MICRO, EDGES_MB), -ATOM_DEV, 2 * ATOM_DEV)
    offsets = jnp.where(within[None, :] == 0, -ATOM_DEV, offsets)
    offsets = jnp.where(within[None, :] == 1, 2 * ATOM_DEV - 1, offsets)
    return jnp.clip(block_ids[None, :] * ATOM_DEV + offsets, 0, ATOMS - 1).astype(jnp.int32)


def with_ends(array, key, least, largest):
    spot = [jax.random.randint(jax.random.fold_in(key, axis), (), 0, length) for axis, length in enumerate(array.shape)]
    main_axis = array.shape.index(max(array.shape))
    next_to = spot[:main_axis] + [(spot[main_axis] + 1) % array.shape[main_axis]] + spot[main_axis + 1:]
    return array.at[tuple(spot)].set(least).at[tuple(next_to)].set(largest)


def steps_of(rng, dims, pieces, least, high):
    def one(dim, shards_of):
        draws = jax.random.uniform(jax.random.fold_in(jax.random.fold_in(rng, 6), dim), (shards_of,), jnp.float32, least / len(pieces), high / len(pieces))
        return jnp.repeat(jnp.exp(draws), dims[dim] // shards_of).reshape((-1,) + (1,) * (len(dims) - dim - 1))

    level = one(*pieces[0])
    for cut in pieces[1:]:
        level = level * one(*cut)
    return level


def profile(number_of, total, limit, lean):
    portions = [(1 << 20) // math.isqrt(standing ** lean) + 1 for standing in range(2, number_of + 1)]
    rest, given = total - limit - (number_of - 1), [1] * (number_of - 1)
    while rest > 0:
        candidates = [i for i in range(number_of - 1) if given[i] < limit]
        pool, left = sum([portions[i] for i in candidates]), rest
        for i in candidates:
            more = min(limit - given[i], max(1, left * portions[i] // pool), rest)
            given[i] = given[i] + more
            rest = rest - more
    return np.array([limit] + given)


def uneven(own_key, count, total, bound, slope):
    if count == 2:
        one = jax.random.randint(own_key, (), max(1, total - bound), min(bound, total - 1) + 1)
        return jnp.stack([one, total - one])
    sizes = jnp.asarray(profile(count, total, bound, slope), jnp.int32)
    twos = (count - 1) // 2
    source_of, receiver = sizes[1:1 + 2 * twos:2], sizes[2:2 + 2 * twos:2]
    room = jnp.minimum(source_of - 1, bound - receiver)
    passed = jax.random.randint(jax.random.fold_in(own_key, 1), (twos,), 0, 1 << 20) % (room + 1)
    sizes = sizes.at[1:1 + 2 * twos:2].set(source_of - passed).at[2:2 + 2 * twos:2].set(receiver + passed)
    return sizes[jax.random.permutation(jax.random.fold_in(own_key, 2), count)]


def bell_draw(key, dims, deviation, limit, cuts=(), held_as=jnp.bfloat16):
    drawn = deviation * jax.random.normal(key, dims, jnp.float32)
    if cuts:
        drawn = drawn * steps_of(key, dims, cuts, -0.22, 0.18)
    return jnp.clip(drawn, -limit, limit).astype(held_as)


def setup_inputs(seed: int = 0) -> dict:
    seeds = jax.random.split(jax.random.key(seed), 14)
    return {
        "edge_vectors": draw_edge_vectors(jax.random.fold_in(seeds[13], 71), 0),
        "edge_species": with_ends(jax.random.randint(seeds[1], (MICRO, 2, EDGES_MB), 0, NSPEC), jax.random.fold_in(seeds[1], 1), 0, NSPEC - 1).astype(jnp.int32),
        "centres": draw_centres(jax.random.fold_in(seeds[13], 71), 0),
        "edge_mask": with_ends((jax.random.randint(seeds[3], (MICRO, EDGES_MB), 0, 4) < 3).astype(jnp.int32), jax.random.fold_in(seeds[3], 1), 0, 1),
        "structures": jax.vmap(lambda own: jnp.searchsorted(jnp.cumsum(uneven(own, STRUCTS, EDGES_MB, 2 * EDGES_MB // STRUCTS, 0)), jnp.arange(EDGES_MB), side="right"))(jax.random.split(seeds[4], MICRO)).reshape((MICRO, EDGES_MB)).astype(jnp.int32),
        "energy_cot": bell_draw(seeds[5], (MICRO, STRUCTS), 1.0, 6.0, (), jnp.float32),
        "embed_in": bell_draw(seeds[6], (FEAT, D), FEAT ** -0.5, 1.5, (), jnp.float32),
        "section_head": bell_draw(seeds[7], (N_SECTION, D, D), (D // 8) ** -0.5, 0.5, ((0, 2), (2, 2)), jnp.float32),
        "env_weight": bell_draw(seeds[8], (N_SECTION, D, CH), (D // 4) ** -0.5, 0.375, ((0, 2),), jnp.float32),
        "mix_weight": bell_draw(seeds[9], (3, CH, CH), CH ** -0.5, 0.75, (), jnp.float32),
        "w_in": bell_draw(seeds[10], (N_SECTION, D + 3 * CH, D), (D + 3 * CH) ** -0.5, 0.15625, ((0, 2), (2, 2)), jnp.float32),
        "w_out": bell_draw(seeds[11], (N_SECTION, D, D), D ** -0.5, 0.1875, ((0, 2), (1, 2)), jnp.float32),
        "read_weight": bell_draw(seeds[12], (D,), (16 * D) ** -0.5, 0.046875, (), jnp.float32),
    }


CUTOFF = 5.0
ENV_SCALE = 0.25
HIGHEST = lax.Precision.HIGHEST
ROOT_THREE = 1.7320508075688772
ROOT_FIVE = 2.23606797749979
ROOT_FIFTEEN = 3.872983346207417

@jax.custom_vjp
def low(v):
    return lax.optimization_barrier(v.astype(jnp.bfloat16)).astype(jnp.float32)

@jax.custom_vjp
def low_back(v):
    return v

def low_keep(v):
    return (low(v), None)

def low_pass(kept, grad):
    return (grad,)

def back_keep(v):
    return (v, None)

def back_low(kept, grad):
    return (low(grad),)
low.defvjp(low_keep, low_pass)
low_back.defvjp(back_keep, back_low)

def matmul(left, right):
    return jnp.dot(left, right, precision=HIGHEST, preferred_element_type=jnp.float32)

def geometry(vectors, edge_live):
    squares = jnp.maximum(lax.optimization_barrier(jnp.sum(vectors * vectors, axis=0)), 0.25)
    length = jnp.sqrt(squares)
    unit_x = vectors[0] / length
    unit_y = vectors[1] / length
    unit_z = vectors[2] / length
    edge_ratio = jnp.minimum(length / CUTOFF, 1.0)
    envelope = (1.0 - 28.0 * edge_ratio ** 6 + 48.0 * edge_ratio ** 7 - 21.0 * edge_ratio ** 8) * edge_live
    orders = jnp.arange(1, NBES + 1).astype(jnp.float32)
    bessel = jnp.sqrt(2.0 / CUTOFF) * jnp.sin(orders[None, :] * (jnp.pi / CUTOFF) * length[:, None]) / length[:, None]
    harmonics = jnp.stack([jnp.ones_like(unit_x), ROOT_THREE * unit_x, ROOT_THREE * unit_y, ROOT_THREE * unit_z, ROOT_FIFTEEN * unit_x * unit_y, ROOT_FIFTEEN * unit_y * unit_z, 0.5 * ROOT_FIVE * (3.0 * unit_z * unit_z - 1.0), ROOT_FIFTEEN * unit_x * unit_z, 0.5 * ROOT_FIFTEEN * (unit_x * unit_x - unit_y * unit_y)], axis=1)
    return (harmonics, envelope, bessel)

def couple(edge_tensor, env_flat, mix_weight):
    chan_count = mix_weight.shape[1]
    own_tensor = edge_tensor.reshape(-1, 9, chan_count)
    env_tensor = env_flat.reshape(-1, 9, chan_count)
    paired = own_tensor * env_tensor
    scalars = jnp.concatenate([paired[:, 0], lax.optimization_barrier(jnp.sum(paired[:, 1:4], axis=1)), lax.optimization_barrier(jnp.sum(paired[:, 4:9], axis=1))], axis=1)
    coupled = own_tensor * env_tensor[:, 0:1] + own_tensor[:, 0:1] * env_tensor
    order_zero = jnp.einsum('emc,cd->emd', coupled[:, 0:1], mix_weight[0], precision=HIGHEST)
    order_one = jnp.einsum('emc,cd->emd', coupled[:, 1:4], mix_weight[1], precision=HIGHEST)
    order_two = jnp.einsum('emc,cd->emd', coupled[:, 4:9], mix_weight[2], precision=HIGHEST)
    updated = jnp.concatenate([order_zero, order_one, order_two], axis=1)
    return (scalars, updated.reshape(-1, 9 * chan_count))

def species_hot(kind_ids):
    return (kind_ids[:, None] == jnp.arange(NSPEC)[None, :]).astype(jnp.float32)

def forward(weights, edge_vectors, edge_species, centres, edge_mask, structures):
    embed_in, section_head, env_weight, mix_weight, w_in, w_out, read_weight = weights
    results = []
    for batch_index in range(MICRO):
        harmonics, envelope, bessel = geometry(edge_vectors[batch_index], edge_mask[batch_index].astype(jnp.float32))
        kind_ids = edge_species[batch_index]
        features = jnp.concatenate([species_hot(kind_ids[0]), species_hot(kind_ids[1]), bessel], axis=1)
        latent = envelope[:, None] * matmul(jax.nn.silu(matmul(features, embed_in)), section_head[0])
        owners = centres[batch_index]
        edge_tensor = jnp.zeros((latent.shape[0], 9 * CH), jnp.float32)
        for layer_index in range(2):
            weight = matmul(latent, env_weight[layer_index])
            if layer_index == 0:
                edge_tensor = (harmonics[:, :, None] * weight[:, None, :]).reshape(-1, 9 * CH)
            contribution = (ENV_SCALE * envelope)[:, None, None] * harmonics[:, :, None] * weight[:, None, :]
            totals = jax.ops.segment_sum(contribution.reshape(-1, 9 * CH), owners, num_segments=ATOMS)
            env_flat = totals[owners]
            scalars, updated = couple(edge_tensor, env_flat, mix_weight)
            hidden = jax.nn.silu(matmul(jnp.concatenate([latent, scalars], axis=1), w_in[layer_index]))
            latent = latent + matmul(hidden, w_out[layer_index])
            edge_tensor = updated
        edge_energy = envelope * matmul(jax.nn.silu(matmul(latent, section_head[1])), read_weight)
        results.append(jax.ops.segment_sum(edge_energy, structures[batch_index], num_segments=STRUCTS))
    return jnp.stack(results)

def reference(edge_vectors, edge_species, centres, edge_mask, structures, energy_cot, embed_in, section_head, env_weight, mix_weight, w_in, w_out, read_weight):
    weights = (embed_in, section_head, env_weight, mix_weight, w_in, w_out, read_weight)

    def evaluate(params, vectors):
        return forward(params, vectors, edge_species, centres, edge_mask, structures)
    energies, pull_back = jax.vjp(evaluate, weights, edge_vectors)
    grads, vector_grad = pull_back(energy_cot)
    return (energies, -vector_grad, grads[0], grads[1], grads[2], grads[3], grads[4], grads[5], grads[6])
```

```python
from functools import partial

import jax
import jax.numpy as jnp
from jax import lax
from jax.experimental import pallas as pl
from jax.experimental.pallas import tpu as pltpu
from jax.sharding import PartitionSpec as P

NBES = 8
NSPEC = 4
ATOM_DEV = 40
STRUCTS = 16


CUTOFF = 5.0
ENV_SCALE = 0.25
HIGHEST = lax.Precision.HIGHEST
ROOT_THREE = 1.7320508075688772
ROOT_FIVE = 2.23606797749979
ROOT_FIFTEEN = 3.872983346207417


def extended(block, sides, width):
    for axis, dim in sides:
        count = lax.axis_size(axis)
        forward = [(i, i + 1) for i in range(count - 1)]
        backward = [(target, source) for source, target in forward]
        low = lax.ppermute(
            lax.slice_in_dim(block, block.shape[dim] - width, None, axis=dim), axis, forward
        )
        high = lax.ppermute(lax.slice_in_dim(block, 0, width, axis=dim), axis, backward)
        block = jnp.concatenate([low, block, high], axis=dim)
    return block


def shifted(value, axis, steps):
    count = lax.axis_size(axis)
    first, last = (max(0, -steps), min(count, count - steps))
    return lax.ppermute(value, axis, [(source, source + steps) for source in range(first, last)])


def matmul(left, right):
    return jnp.dot(left, right, precision=HIGHEST, preferred_element_type=jnp.float32)


def geometry(vectors, edge_live):
    squares = jnp.maximum(jnp.sum(vectors * vectors, axis=0), 0.25)
    length = jnp.sqrt(squares)
    unit_x = vectors[0] / length
    unit_y = vectors[1] / length
    unit_z = vectors[2] / length
    edge_ratio = jnp.minimum(length / CUTOFF, 1.0)
    envelope = (
        1.0 - 28.0 * edge_ratio**6 + 48.0 * edge_ratio**7 - 21.0 * edge_ratio**8
    ) * edge_live
    orders = jnp.arange(1, NBES + 1).astype(jnp.float32)
    bessel = (
        jnp.sqrt(2.0 / CUTOFF)
        * jnp.sin(orders[None, :] * (jnp.pi / CUTOFF) * length[:, None])
        / length[:, None]
    )
    harmonics = jnp.stack(
        [
            jnp.ones_like(unit_x),
            ROOT_THREE * unit_x,
            ROOT_THREE * unit_y,
            ROOT_THREE * unit_z,
            ROOT_FIFTEEN * unit_x * unit_y,
            ROOT_FIFTEEN * unit_y * unit_z,
            0.5 * ROOT_FIVE * (3.0 * unit_z * unit_z - 1.0),
            ROOT_FIFTEEN * unit_x * unit_z,
            0.5 * ROOT_FIFTEEN * (unit_x * unit_x - unit_y * unit_y),
        ],
        axis=1,
    )
    return (harmonics, envelope, bessel)


def couple(edge_tensor, env_flat, mix_weight):
    chan_count = mix_weight.shape[1]
    own_tensor = edge_tensor.reshape(-1, 9, chan_count)
    env_tensor = env_flat.reshape(-1, 9, chan_count)
    paired = own_tensor * env_tensor
    scalars = jnp.concatenate(
        [paired[:, 0], jnp.sum(paired[:, 1:4], axis=1), jnp.sum(paired[:, 4:9], axis=1)], axis=1
    )
    coupled = own_tensor * env_tensor[:, 0:1] + own_tensor[:, 0:1] * env_tensor
    order_zero = jnp.einsum("emc,cd->emd", coupled[:, 0:1], mix_weight[0], precision=HIGHEST)
    order_one = jnp.einsum("emc,cd->emd", coupled[:, 1:4], mix_weight[1], precision=HIGHEST)
    order_two = jnp.einsum("emc,cd->emd", coupled[:, 4:9], mix_weight[2], precision=HIGHEST)
    updated = jnp.concatenate([order_zero, order_one, order_two], axis=1)
    return (scalars, updated.reshape(-1, 9 * chan_count))


def front(bessel, envelope, embed_in, head_local, kinds_hot):
    features = jnp.concatenate([kinds_hot, bessel], axis=1)
    return envelope[:, None] * matmul(jax.nn.silu(matmul(features, embed_in)), head_local)


def contribute(latent_full, harmonics, envelope, env_local, centre_hot):
    weight = matmul(latent_full, env_local)
    contribution = (
        (ENV_SCALE * envelope)[:, None, None] * harmonics[:, :, None] * weight[:, None, :]
    )
    flat_terms = contribution.reshape(weight.shape[0], -1)
    return (weight, matmul(centre_hot.T, flat_terms))


def tensor_step(tensor_full, env_window, weight, harmonics, mix_weight, centre_hot, is_first):
    start_tensor = (harmonics[:, :, None] * weight[:, None, :]).reshape(weight.shape[0], -1)
    edge_tensor = jnp.where(is_first, start_tensor, tensor_full)
    env_flat = matmul(centre_hot, env_window)
    return couple(edge_tensor, env_flat, mix_weight)


def perceptron(latent_full, scalars, in_local, out_local):
    hidden = jax.nn.silu(matmul(jnp.concatenate([latent_full, scalars], axis=1), in_local))
    return matmul(hidden, out_local)


def readout(latent_full, envelope, head_local, read_half):
    return envelope * matmul(jax.nn.silu(matmul(latent_full, head_local)), read_half)


def general_device(
    edge_vectors,
    edge_species,
    centres,
    edge_mask,
    structures,
    energy_cot,
    embed_in,
    section_head,
    env_weight,
    mix_weight,
    w_in,
    w_out,
    read_weight,
):
    section_index = lax.axis_index("section")
    core_index = lax.axis_index("mp")
    edge_index = lax.axis_index("edge")
    is_first = section_index == 0
    last_flag = (section_index == 1).astype(jnp.float32)
    batch_count = edge_vectors.shape[0]
    shard_width = w_out.shape[1]
    tensor_cols = 9 * env_weight.shape[2]
    tensor_half = tensor_cols // 2
    atoms_dev = ATOM_DEV
    head_local = section_head[0]
    env_local = env_weight[0]
    in_local = w_in[0]
    out_local = w_out[0]
    read_half = lax.dynamic_slice_in_dim(read_weight, core_index * shard_width, shard_width, 0)
    core_lead = (core_index == 0).astype(jnp.float32)
    edge_count = edge_vectors.shape[2]
    centre_slots = jnp.arange(3 * atoms_dev)
    labels = jnp.arange(STRUCTS)
    species_range = jnp.arange(NSPEC)
    batch_range = jnp.arange(batch_count)

    def reduce_rims(pieces):
        widened = extended(pieces, (("edge", 0),), atoms_dev)
        return (
            widened[:atoms_dev] + widened[2 * atoms_dev : 3 * atoms_dev] + widened[4 * atoms_dev :]
        )

    def window_rows(totals):
        return extended(totals, (("edge", 0),), atoms_dev)

    def collect(partial_rows):
        return lax.psum_scatter(partial_rows, "mp", scatter_dimension=1, tiled=True)

    def batch_data(batch_index):
        vectors = lax.dynamic_index_in_dim(edge_vectors, batch_index, 0, keepdims=False)
        kind_ids = lax.dynamic_index_in_dim(edge_species, batch_index, 0, keepdims=False)
        owners = lax.dynamic_index_in_dim(centres, batch_index, 0, keepdims=False)
        edge_live = lax.dynamic_index_in_dim(edge_mask, batch_index, 0, keepdims=False).astype(
            jnp.float32
        )
        groups = lax.dynamic_index_in_dim(structures, batch_index, 0, keepdims=False)
        kinds_hot = jnp.concatenate(
            [
                kind_ids[0][:, None] == species_range[None, :],
                kind_ids[1][:, None] == species_range[None, :],
            ],
            axis=1,
        ).astype(jnp.float32)
        local_slot = owners - (edge_index - 1) * atoms_dev
        centre_hot = (local_slot[:, None] == centre_slots[None, :]).astype(jnp.float32)
        group_hot = (groups[:, None] == labels[None, :]).astype(jnp.float32)
        return (vectors, edge_live, kinds_hot, centre_hot, group_hot)

    recv_latent = jnp.zeros((edge_count, shard_width), jnp.float32)
    recv_tensor = jnp.zeros((edge_count, tensor_half), jnp.float32)
    energies = jnp.zeros((batch_count, STRUCTS), jnp.float32)
    kept_state = []
    for step_index in range(batch_count + 1):
        batch_raw = step_index - section_index
        batch_index = jnp.clip(batch_raw, 0, batch_count - 1)
        is_valid = ((batch_raw >= 0) & (batch_raw < batch_count)).astype(jnp.float32)
        vectors, edge_live, kinds_hot, centre_hot, group_hot = batch_data(batch_index)
        harmonics, envelope, bessel = geometry(vectors, edge_live)
        latent_half = lax.cond(
            is_first,
            lambda: front(bessel, envelope, embed_in, head_local, kinds_hot),
            lambda: recv_latent,
        )
        latent_full, tensor_full = (
            lax.all_gather(latent_half, "mp", axis=1, tiled=True),
            lax.all_gather(recv_tensor, "mp", axis=1, tiled=True),
        )
        weight, part_sums = contribute(latent_full, harmonics, envelope, env_local, centre_hot)
        env_window = window_rows(reduce_rims(part_sums))
        scalars, updated = tensor_step(
            tensor_full, env_window, weight, harmonics, mix_weight, centre_hot, is_first
        )
        branch_out = perceptron(latent_full, scalars, in_local, out_local)
        summed = lax.psum_scatter(branch_out, "mp", scatter_dimension=1, tiled=True)
        tensor_own = lax.dynamic_slice_in_dim(updated, core_index * tensor_half, tensor_half, 1)
        next_half = latent_half + summed
        recv_latent, recv_tensor = shifted((next_half, tensor_own), "section", 1)
        next_full = lax.all_gather(next_half, "mp", axis=1, tiled=True)
        edge_energy = readout(next_full, envelope, head_local, read_half)
        batch_slot = (batch_range == batch_index).astype(jnp.float32) * is_valid * last_flag
        energies = (
            energies
            + batch_slot[:, None] * jnp.dot(edge_energy, group_hot, precision=HIGHEST)[None, :]
        )
        kept_state.append((latent_full, tensor_full, env_window, next_full))
    kept_latent = jnp.stack([entry[0] for entry in kept_state])
    kept_tensor = jnp.stack([entry[1] for entry in kept_state])
    kept_window = jnp.stack([entry[2] for entry in kept_state])
    kept_next = jnp.stack([entry[3] for entry in kept_state])
    grad_head = jnp.zeros_like(head_local)
    grad_env = jnp.zeros_like(env_local)
    grad_in = jnp.zeros_like(in_local)
    grad_out = jnp.zeros_like(out_local)
    grad_mix = jnp.zeros_like(mix_weight)
    grad_embed = jnp.zeros_like(embed_in)
    grad_read = jnp.zeros_like(read_half)
    forces = jnp.zeros((batch_count, 3, edge_count), jnp.float32)
    recv_grad = jnp.zeros((edge_count, shard_width), jnp.float32)
    recv_tgrad = jnp.zeros((edge_count, tensor_half), jnp.float32)
    for step_index in range(batch_count + 1):
        batch_raw = step_index - 1 + section_index
        batch_index = jnp.clip(batch_raw, 0, batch_count - 1)
        is_valid = ((batch_raw >= 0) & (batch_raw < batch_count)).astype(jnp.float32)
        saved_index = jnp.clip(batch_raw + section_index, 0, batch_count)
        latent_full = lax.dynamic_index_in_dim(kept_latent, saved_index, 0, keepdims=False)
        tensor_full = lax.dynamic_index_in_dim(kept_tensor, saved_index, 0, keepdims=False)
        env_window = lax.dynamic_index_in_dim(kept_window, saved_index, 0, keepdims=False)
        next_full = lax.dynamic_index_in_dim(kept_next, saved_index, 0, keepdims=False)
        vectors, edge_live, kinds_hot, centre_hot, group_hot = batch_data(batch_index)
        (harmonics, envelope, bessel), geometry_pull = jax.vjp(
            partial(geometry, edge_live=edge_live), vectors
        )
        batch_cot = lax.dynamic_index_in_dim(energy_cot, batch_index, 0, keepdims=False)
        energy_rows = jnp.dot(group_hot, batch_cot, precision=HIGHEST) * (is_valid * last_flag)
        _, read_pull = jax.vjp(readout, next_full, envelope, head_local, read_half)
        d_next_read, d_env_read, g_head_read, g_read = read_pull(energy_rows)
        d_next_half = jnp.where(is_first, recv_grad, collect(d_next_read))
        d_out_full, d_updated = (
            lax.all_gather(d_next_half, "mp", axis=1, tiled=True),
            lax.all_gather(recv_tgrad, "mp", axis=1, tiled=True),
        )
        (weight, part_sums), contribute_pull = jax.vjp(
            partial(contribute, centre_hot=centre_hot), latent_full, harmonics, envelope, env_local
        )
        (scalars, updated), tensor_pull = jax.vjp(
            partial(tensor_step, centre_hot=centre_hot, is_first=is_first),
            tensor_full,
            env_window,
            weight,
            harmonics,
            mix_weight,
        )
        _, perceptron_pull = jax.vjp(perceptron, latent_full, scalars, in_local, out_local)
        d_latent_mlp, d_scalar_part, g_in, g_out = perceptron_pull(d_out_full)
        d_scalars = lax.psum(d_scalar_part, "mp")
        d_tensor, d_window, d_weight, d_harm_tensor, g_mix = tensor_pull((d_scalars, d_updated))
        d_parts = window_rows(reduce_rims(d_window))
        d_latent_env, d_harm_env, d_envelope_env, g_env = contribute_pull((d_weight, d_parts))
        d_latent_own = (
            collect(d_latent_mlp)
            + lax.dynamic_slice_in_dim(d_latent_env, core_index * shard_width, shard_width, 1)
            + d_next_half
        )
        d_tensor_own = lax.dynamic_slice_in_dim(d_tensor, core_index * tensor_half, tensor_half, 1)
        recv_grad, recv_tgrad = shifted((d_latent_own, d_tensor_own), "section", -1)

        def front_pull(cotangent):
            _, pull_back = jax.vjp(
                partial(front, kinds_hot=kinds_hot), bessel, envelope, embed_in, head_local
            )
            return pull_back(cotangent)

        def front_none(cotangent):
            return (
                jnp.zeros_like(bessel),
                jnp.zeros_like(envelope),
                jnp.zeros_like(embed_in),
                jnp.zeros_like(head_local),
            )

        d_bessel, d_envelope_front, g_embed, g_head_front = lax.cond(
            is_first, front_pull, front_none, d_latent_own
        )
        d_harmonics = core_lead * (d_harm_tensor + d_harm_env)
        d_envelope = core_lead * d_envelope_env + d_env_read + d_envelope_front
        d_vectors = geometry_pull((d_harmonics, d_envelope, d_bessel))[0]
        batch_slot = (batch_range == batch_index).astype(jnp.float32) * is_valid
        forces = forces + batch_slot[:, None, None] * d_vectors[None]
        grad_head = grad_head + is_valid * (g_head_read + g_head_front)
        grad_env = grad_env + is_valid * g_env
        grad_in = grad_in + is_valid * g_in
        grad_out = grad_out + is_valid * g_out
        grad_mix = grad_mix + is_valid * g_mix
        grad_embed = grad_embed + is_valid * g_embed
        grad_read = grad_read + is_valid * g_read
    grad_head, grad_env, grad_in, grad_out = lax.psum(
        (grad_head, grad_env, grad_in, grad_out), "edge"
    )
    read_full = lax.dynamic_update_slice_in_dim(
        jnp.zeros_like(read_weight), grad_read, core_index * shard_width, 0
    )
    energies, grad_embed, grad_mix, read_full = lax.psum(
        (energies, grad_embed, core_lead * grad_mix, read_full), ("section", "edge", "mp")
    )
    forces = lax.psum(forces, ("section", "mp"))
    return (
        energies,
        -forces,
        grad_embed,
        grad_head[None],
        grad_env[None],
        grad_mix,
        grad_in[None],
        grad_out[None],
        read_full,
    )


CHUNKS = (160, 160, 160)
LANES = 128
F32 = jnp.float32
BF16 = jnp.bfloat16
BESSEL_SCALE = (2.0 / CUTOFF) ** 0.5
ANGLE = 3.141592653589793 / CUTOFF


def dot_nn(left, right):
    return jnp.dot(left, right, preferred_element_type=F32)


def dot_nt(left, right):
    return lax.dot_general(left, right, (((1,), (1,)), ((), ())), preferred_element_type=F32)


def dot_tn(left, right):
    return lax.dot_general(left, right, (((0,), (0,)), ((), ())), preferred_element_type=F32)


def split_two(value):
    high = value.astype(BF16)
    return high, (value - high.astype(F32)).astype(BF16)


def split_three(value):
    high = value.astype(BF16)
    rest = value - high.astype(F32)
    middle = rest.astype(BF16)
    return high, middle, (rest - middle.astype(F32)).astype(BF16)


def six_pass(left, right):
    rows = left.shape[0]
    high, middle, low = split_three(left)
    three = dot_nn(jnp.concatenate([high, middle, low], axis=0), right[0])
    two = dot_nn(jnp.concatenate([high, middle], axis=0), right[1])
    small = three[2 * rows :] + two[rows:] + dot_nn(high, right[2])
    return three[:rows] + (three[rows : 2 * rows] + two[:rows] + small)


def three_pass(dot, left, right):
    rows = left.shape[0]
    high, low = split_two(left)
    both = dot(jnp.concatenate([high, low], axis=0), right[0])
    return both[:rows] + both[rows:] + dot(high, right[1])


def three_pass_tn(left, right):
    left_high, left_low = split_two(left)
    right_high, right_low = split_two(right)
    return dot_tn(
        jnp.concatenate([left_high, left_low, left_high], axis=0),
        jnp.concatenate([right_high, right_high, right_low], axis=0),
    )


def sigmoid(value):
    return 1.0 / (1.0 + jnp.exp(-value))


def order_of(component):
    return 0 if component == 0 else (1 if component < 4 else 2)


def same_sum(same, parts):
    high, middle, low = split_three(jnp.concatenate(parts, axis=1))
    summed = dot_nn(same, high) + (dot_nn(same, middle) + dot_nn(same, low))
    return [summed[:, LANES * m : LANES * (m + 1)] for m in range(len(parts))]


def place_columns(columns, first, width=LANES):
    lane = lax.broadcasted_iota(jnp.int32, (columns[0].shape[0], width), 1)
    out = jnp.zeros((columns[0].shape[0], width), F32)
    for i, column in enumerate(columns):
        out = jnp.where(lane == first + i, column, out)
    return out


def waves(length):
    turn = length * ANGLE - 1.5707963267948966
    square = turn * turn
    even, odd, term_even, term_odd = 1.0, 1.0, 1.0, 1.0
    coefficients_even, coefficients_odd = [], []
    for n in range(1, 9):
        term_even = -term_even / ((2 * n - 1) * (2 * n))
        term_odd = -term_odd / ((2 * n) * (2 * n + 1))
        coefficients_even.append(term_even)
        coefficients_odd.append(term_odd)
    even = jnp.full_like(turn, coefficients_even[-1])
    odd = jnp.full_like(turn, coefficients_odd[-1])
    for n in range(6, -1, -1):
        even = even * square + coefficients_even[n]
        odd = odd * square + coefficients_odd[n]
    sines = {1: even * square + 1.0}
    cosines = {1: -turn * (odd * square + 1.0)}
    for total, left, right in ((2, 1, 1), (3, 2, 1), (4, 2, 2), (5, 4, 1), (6, 4, 2), (7, 4, 3), (8, 4, 4)):
        sines[total] = sines[left] * cosines[right] + cosines[left] * sines[right]
        cosines[total] = cosines[left] * cosines[right] - sines[left] * sines[right]
    return [sines[k] for k in range(1, 9)], [cosines[k] for k in range(1, 9)]


def edge_values(edges, key_row, first, rows, full):
    block = edges[first : first + rows, :]
    vector = [block[:, i : i + 1] for i in range(3)]
    live = block[:, 6:7]
    squares = vector[0] * vector[0] + vector[1] * vector[1] + vector[2] * vector[2]
    length = jnp.sqrt(jnp.maximum(squares, 0.25))
    ux, uy, uz = (v / length for v in vector)
    ratio = jnp.minimum(length / CUTOFF, 1.0)
    second = ratio * ratio
    sixth = second * second * second
    envelope = (1.0 - 28.0 * sixth + 48.0 * (sixth * ratio) - 21.0 * (sixth * second)) * live
    harmonics = [
        jnp.ones_like(ux),
        ROOT_THREE * ux,
        ROOT_THREE * uy,
        ROOT_THREE * uz,
        ROOT_FIFTEEN * ux * uy,
        ROOT_FIFTEEN * uy * uz,
        0.5 * ROOT_FIVE * (3.0 * uz * uz - 1.0),
        ROOT_FIFTEEN * ux * uz,
        0.5 * ROOT_FIFTEEN * (ux * ux - uy * uy),
    ]
    same = jnp.where(block[:, 5:6] == key_row, 1.0, 0.0).astype(BF16)
    g = dict(
        env=envelope, harm=harmonics, same=same, squares=squares, length=length, ratio=ratio,
        unit=(ux, uy, uz), live=live, group=block[:, 7:8],
    )
    if full:
        sines, g["cosines"] = waves(length)
        g["bessel"] = [BESSEL_SCALE * value / length for value in sines]
        lane = lax.broadcasted_iota(jnp.int32, (rows, 16), 1).astype(F32)
        kinds = jnp.where(
            lane < NSPEC,
            jnp.where(block[:, 3:4] == lane, live, 0.0),
            jnp.where(block[:, 4:5] + NSPEC == lane, live, 0.0),
        )
        g["feat"] = kinds + place_columns(g["bessel"], 2 * NSPEC, 16)
    return g


def vector_pull(g, d_bessel, d_harm, d_envelope):
    ux, uy, uz = g["unit"]
    length, ratio = g["length"], g["ratio"]
    dx = ROOT_THREE * d_harm[1] + ROOT_FIFTEEN * (uy * d_harm[4] + uz * d_harm[7] + ux * d_harm[8])
    dy = ROOT_THREE * d_harm[2] + ROOT_FIFTEEN * (ux * d_harm[4] + uz * d_harm[5] - uy * d_harm[8])
    dz = (
        ROOT_THREE * d_harm[3]
        + ROOT_FIFTEEN * (uy * d_harm[5] + ux * d_harm[7])
        + (3.0 * ROOT_FIVE) * uz * d_harm[6]
    )
    left = 1.0 - ratio
    fourth = (ratio * ratio) * (ratio * ratio)
    d_length = (-168.0 / CUTOFF) * (fourth * ratio) * (left * left) * g["live"] * d_envelope
    d_length = d_length - (dx * ux + dy * uy + dz * uz) / length
    for k in range(NBES):
        slope = (BESSEL_SCALE * ANGLE * (k + 1)) * g["cosines"][k] - g["bessel"][k]
        d_length = d_length + d_bessel[k] * (slope / length)
    bound = jnp.where(g["squares"] > 0.25, 1.0, jnp.where(g["squares"] == 0.25, 0.5, 0.0))
    d_length = d_length * bound
    return [d / length + d_length * u for d, u in ((dx, ux), (dy, uy), (dz, uz))]


def env_terms(g, weight):
    scaled = ENV_SCALE * g["env"] * weight
    return same_sum(g["same"], [y * scaled for y in g["harm"]])


def pack_scalars(tensor, env):
    sums = [tensor[0] * env[0], tensor[1] * env[1], tensor[4] * env[4]]
    for m in (2, 3):
        sums[1] = sums[1] + tensor[m] * env[m]
    for m in (5, 6, 7, 8):
        sums[2] = sums[2] + tensor[m] * env[m]
    return jnp.concatenate([sums[0] + pltpu.roll(sums[1], 64, 1), sums[2]], axis=1)


def unpack_scalars(packed):
    first = packed[:, :LANES]
    return [first, pltpu.roll(first, 64, 1), packed[:, LANES:]]


def swap_order(lead, left, right):
    return jnp.where(lead, left, right), jnp.where(lead, right, left)


def env_pull(g, weight, d_env):
    d_terms = same_sum(g["same"], d_env)
    d_weight, d_harm, inner = None, [], None
    for m in range(9):
        part = g["harm"][m] * d_terms[m]
        d_weight = part if m == 0 else d_weight + part
        d_harm.append(jnp.sum(weight * d_terms[m], axis=1, keepdims=True))
        step = g["harm"][m] * d_harm[m]
        inner = step if m == 0 else inner + step
    scale = ENV_SCALE * g["env"]
    return scale * d_weight, [scale * d for d in d_harm], ENV_SCALE * inner


class Fetched:
    def __init__(self, source, buffer, semaphore):
        rows = source.shape[0]
        self.buffer, self.shape = buffer, buffer.shape
        target = buffer if rows == buffer.shape[0] else buffer.at[pl.ds(0, rows)]
        self.copy = pltpu.make_async_copy(source, target, semaphore)
        self.copy.start()
        self.arrived, self.pieces = False, {}
        if rows < buffer.shape[0]:
            buffer[rows:, :] = jnp.zeros((buffer.shape[0] - rows, buffer.shape[1]), F32)

    def __getitem__(self, where):
        if not self.arrived:
            self.copy.wait()
            self.arrived = True
        return self.buffer[where]

    def split(self, parts):
        if parts not in self.pieces:
            value = self[...]
            self.pieces[parts] = split_three(value) if parts == 3 else split_two(value)
        return self.pieces[parts]


class Stored:
    def __init__(self, target, buffer, semaphore):
        self.target, self.buffer, self.semaphore = target, buffer, semaphore
        self.shape, self.copy = buffer.shape, None

    def __setitem__(self, where, value):
        self.buffer[where] = value
        if where is Ellipsis:
            self.send()

    def __getitem__(self, where):
        return self.buffer[where]

    def send(self):
        self.copy = pltpu.make_async_copy(self.buffer, self.target, self.semaphore)
        self.copy.start()


def forward_pair(value, own, other):
    return [six_pass(value, own.split(3)), six_pass(value, other.split(3))]


def backward_pair(value, own, other, parts):
    return [three_pass(dot_nt, value, own.split(parts)), three_pass(dot_nt, value, other.split(parts))]


def first_forward(
    first, edges, key_row, lead_flag, embed,
    head_o, head_x, env_w, in_o, in_x, out_o, out_x,
    sent, soft_out, layer_in, slope_out, hidden,
):
    rows = sent.shape[0]
    lead = lead_flag[0:1, 0:1] > 0.5
    g = edge_values(edges, key_row[...], first, rows, True)
    pre = six_pass(g["feat"], split_three(embed[...]))
    soft = pre * sigmoid(pre)
    soft_out[...] = soft
    own, other = forward_pair(soft, head_o, head_x)
    latent = g["env"] * jnp.concatenate(swap_order(lead, own, other), axis=1)
    weight = six_pass(latent, env_w.split(3))
    env = env_terms(g, weight)
    scalars = pack_scalars([y * weight for y in g["harm"]], env)
    full = jnp.concatenate([latent, scalars], axis=1)
    layer_in[...] = full
    pre = jnp.concatenate(forward_pair(full, in_o, in_x), axis=1)
    gate = sigmoid(pre)
    slope_out[...] = gate * (1.0 + pre * (1.0 - gate))
    hid = pre * gate
    hidden[...] = hid
    half = hid.shape[1] // 2
    width = latent.shape[1]
    sent[:, :width] = (
        latent + six_pass(hid[:, :half], out_o.split(3)) + six_pass(hid[:, half:], out_x.split(3))
    )
    sent[:, width:] = weight
    sent.send()


def second_both(
    first, edges, key_row, mix, read, cot_row,
    arrived, env_w, in_o, in_x, out_o, out_x, head_o, head_x, env_wt,
    back, layer_in, d_pre_hidden, hidden, d_latent_out, latent_out, d_pre_read, d_weight_out,
    read_grad, mix_grad, energy_out,
):
    rows = back.shape[0]
    width = arrived.shape[1] - LANES
    half = width // 2
    g = edge_values(edges, key_row[...], first, rows, False)
    lane = lax.broadcasted_iota(jnp.int32, (rows, LANES), 1).astype(F32)
    group_hot = jnp.where(g["group"] == lane, g["live"], 0.0)
    cot = jnp.sum(group_hot * cot_row[...], axis=1, keepdims=True)
    mixes = [split_three(mix[i]) for i in range(3)]
    latent = arrived[:, :width]
    weight_first = arrived[:, width:]
    env_first = env_terms(g, weight_first)
    start = [y * weight_first for y in g["harm"]]
    coupled = [start[m] * env_first[0] + start[0] * env_first[m] for m in range(9)]
    members = ((0,), (1, 2, 3), (4, 5, 6, 7, 8))
    tensor = []
    for order in range(3):
        mixed = six_pass(jnp.concatenate([coupled[m] for m in members[order]], axis=0), mixes[order])
        tensor += [mixed[rows * i : rows * (i + 1)] for i in range(len(members[order]))]
    weight = six_pass(latent, env_w.split(3))
    env = env_terms(g, weight)
    full = jnp.concatenate([latent, pack_scalars(tensor, env)], axis=1)
    layer_in[...] = full
    pre = jnp.concatenate(forward_pair(full, in_o, in_x), axis=1)
    gate = sigmoid(pre)
    slope = gate * (1.0 + pre * (1.0 - gate))
    hid = pre * gate
    hidden[...] = hid
    latent_next = (
        latent + six_pass(hid[:, :half], out_o.split(3)) + six_pass(hid[:, half:], out_x.split(3))
    )
    latent_out[...] = latent_next
    pre_read = jnp.concatenate(forward_pair(latent_next, head_o, head_x), axis=1)
    gate = sigmoid(pre_read)
    soft = pre_read * gate
    line = read[...]
    inner = jnp.sum(soft * line, axis=1, keepdims=True)
    energy_out[...] = jnp.broadcast_to(
        jnp.sum(group_hot * (g["env"] * inner), axis=0, keepdims=True), energy_out.shape
    )
    scaled_cot = cot * g["env"]
    read_grad[...] = jnp.broadcast_to(
        jnp.sum(scaled_cot * soft, axis=0, keepdims=True), read_grad.shape
    )
    d_envelope = cot * inner
    d_read = scaled_cot * line * (gate * (1.0 + pre_read * (1.0 - gate)))
    d_pre_read[...] = d_read
    d_latent_out[...] = three_pass(dot_nt, d_read[:, :half], head_o.split(3)) + three_pass(
        dot_nt, d_read[:, half:], head_x.split(3)
    )
    d_hid = jnp.concatenate(backward_pair(d_latent_out[...], out_o, out_x, 3), axis=1)
    d_pre = d_hid * slope
    d_pre_hidden[...] = d_pre
    d_full = three_pass(dot_nt, d_pre[:, :half], in_o.split(3)) + three_pass(
        dot_nt, d_pre[:, half:], in_x.split(3)
    )
    d_scalars = unpack_scalars(d_full[:, width:])
    d_tensor = [d_scalars[order_of(m)] * env[m] for m in range(9)]
    d_env = [d_scalars[order_of(m)] * tensor[m] for m in range(9)]
    d_weight, d_harm, d_more = env_pull(g, weight, d_env)
    d_envelope = d_envelope + d_more
    d_weight_out[...] = d_weight
    back[:, :width] = (
        three_pass(dot_nn, d_weight_out[...], env_wt.split(2))
        + d_latent_out[...]
        + d_full[:, :width]
    )
    d_coupled = []
    for order in range(3):
        joined = jnp.concatenate([d_tensor[m] for m in members[order]], axis=0)
        mix_grad[order] = three_pass_tn(
            jnp.concatenate([coupled[m] for m in members[order]], axis=0), joined
        )
        mixed = three_pass(dot_nt, joined, mixes[order])
        d_coupled += [mixed[rows * i : rows * (i + 1)] for i in range(len(members[order]))]
    mix_grad.send()
    d_env_first = [d_coupled[m] * start[0] for m in range(9)]
    d_start = [d_coupled[m] * env_first[0] for m in range(9)]
    for m in range(9):
        d_env_first[0] = d_env_first[0] + d_coupled[m] * start[m]
        d_start[0] = d_start[0] + d_coupled[m] * env_first[m]
    d_first, d_harm_first, d_more = env_pull(g, weight_first, d_env_first)
    for m in range(9):
        d_first = d_first + g["harm"][m] * d_start[m]
        d_harm[m] = (
            d_harm[m]
            + d_harm_first[m]
            + jnp.sum(weight_first * d_start[m], axis=1, keepdims=True)
        )
    d_envelope = d_envelope + d_more
    back[:, width:] = d_first + place_columns(d_harm + [d_envelope], 64)
    back.send()


def first_backward(
    first, edges, key_row, lead_flag, embed,
    layer_in, env_w, arrived, out_o, out_x, slope_in, in_o, in_x, env_wt, head_o, head_x,
    d_vector, d_head, d_pre_hidden, d_weight_out, embed_grad,
):
    rows = arrived.shape[0]
    width = arrived.shape[1] - LANES
    half = width // 2
    lead = lead_flag[0:1, 0:1] > 0.5
    g = edge_values(edges, key_row[...], first, rows, True)
    embed_pair = split_two(embed[...])
    latent = layer_in[:, :width]
    weight = three_pass(dot_nn, latent, env_w.split(2))
    env = env_terms(g, weight)
    extra = arrived[:, width:]
    lane = lax.broadcasted_iota(jnp.int32, extra.shape, 1)
    d_weight = jnp.where(lane < 64, extra, 0.0)
    d_harm = [extra[:, 64 + m : 65 + m] for m in range(9)]
    d_envelope = extra[:, 73:74]
    d_hid = jnp.concatenate(backward_pair(arrived[:, :width], out_o, out_x, 2), axis=1)
    d_pre = d_hid * slope_in[...]
    d_pre_hidden[...] = d_pre
    d_full = three_pass(dot_nt, d_pre[:, :half], in_o.split(2)) + three_pass(
        dot_nt, d_pre[:, half:], in_x.split(2)
    )
    d_scalars = unpack_scalars(d_full[:, width:])
    d_start = [d_scalars[order_of(m)] * env[m] for m in range(9)]
    d_env = [d_scalars[order_of(m)] * (g["harm"][m] * weight) for m in range(9)]
    d_more_weight, d_more_harm, d_more = env_pull(g, weight, d_env)
    d_weight = d_weight + d_more_weight
    d_envelope = d_envelope + d_more
    for m in range(9):
        d_weight = d_weight + g["harm"][m] * d_start[m]
        d_harm[m] = (
            d_harm[m] + d_more_harm[m] + jnp.sum(weight * d_start[m], axis=1, keepdims=True)
        )
    d_weight_out[...] = d_weight
    d_latent = (
        three_pass(dot_nn, d_weight_out[...], env_wt.split(2))
        + arrived[:, :width]
        + d_full[:, :width]
    )
    d_own, d_other = swap_order(lead, d_latent[:, :half], d_latent[:, half:])
    d_head[:, :half] = g["env"] * d_own
    d_head[:, half:] = g["env"] * d_other
    d_head.send()
    d_soft = three_pass(dot_nt, d_own, head_o.split(2)) + three_pass(dot_nt, d_other, head_x.split(2))
    pre = three_pass(dot_nn, g["feat"], embed_pair)
    gate = sigmoid(pre)
    d_envelope = d_envelope + jnp.sum(pre * gate * d_soft, axis=1, keepdims=True)
    d_pre = g["env"] * d_soft * (gate * (1.0 + pre * (1.0 - gate)))
    d_feat = three_pass(dot_nt, d_pre, embed_pair)
    embed_grad[...] = three_pass_tn(g["feat"], d_pre)
    d_bessel = [d_feat[:, 2 * NSPEC + k : 2 * NSPEC + 1 + k] for k in range(NBES)]
    d_vector[...] = place_columns(vector_pull(g, d_bessel, d_harm, d_envelope), 0)


def outer_sum(split_left, chosen, *refs):
    count = len(CHUNKS)
    extra = len(refs) > 4 * count + 8
    kinds = 3 if extra else 2
    sources = [
        [refs[(kinds * side + i) * count : (kinds * side + i + 1) * count] for i in range(kinds)]
        for side in range(2)
    ]
    rest = refs[2 * kinds * count :]
    outs = [Stored(rest[i], rest[kinds + i], rest[-1].at[i]) for i in range(kinds)]
    buffers = rest[2 * kinds : 3 * kinds]
    semaphores = rest[-2]

    def copies(side):
        for i in range(kinds):
            start = 0
            for k, source in enumerate(sources[side][i]):
                rows, columns = source.shape[0], buffers[i].shape[1]
                yield pltpu.make_async_copy(
                    source.at[:, pl.ds(0, columns)],
                    buffers[i].at[pl.ds(start, rows)],
                    semaphores.at[i * count + k],
                )
                start += rows

    for side in range(2):

        @pl.when(chosen[0] == side)
        def _(side=side):
            for copy in copies(side):
                copy.start()

    for copy in copies(0):
        copy.wait()
    left_high, left_low = split_two(buffers[0][...])
    right_high, right_low = split_two(buffers[1][...])
    left = jnp.concatenate([left_high, left_low, left_high], axis=0)
    right = jnp.concatenate([right_high, right_high, right_low], axis=0)
    if split_left:
        half = left.shape[1] // 2
        outs[1][...] = dot_tn(left[:, half:], right)
        outs[0][...] = dot_tn(left[:, :half], right)
    else:
        half = right.shape[1] // 2
        outs[1][...] = dot_tn(left, right[:, half:])
        outs[0][...] = dot_tn(left, right[:, :half])
    if extra:
        right_high, right_low = split_two(buffers[2][...])
        right = jnp.concatenate([right_high, right_high, right_low], axis=0)
        outs[2][...] = dot_tn(left[:, : outs[2].shape[0]], right)
    for out in outs:
        out.copy.wait()


def on_core(body, outs, flops, args, fetched, chosen):
    here = pl.BlockSpec(memory_space=pltpu.VMEM)
    there = pl.BlockSpec(memory_space=pl.ANY)
    pad = 2 * LANES
    tall = [(m.shape[0] + pad - 1) // pad * pad if m.shape[0] > pad else m.shape[0] for m in fetched]
    scratch = [pltpu.VMEM((rows, m.shape[1]), F32) for rows, m in zip(tall, fetched)]
    scratch += [pltpu.VMEM(shape, F32) for shape in outs]
    scratch.append(pltpu.SemaphoreType.DMA((len(fetched),)))
    scratch.append(pltpu.SemaphoreType.DMA((len(outs),)))

    def guarded(flag, *refs):
        @pl.when(flag[0] == 1)
        def _():
            small, rest = refs[: len(args)], refs[len(args) :]
            sources, rest = rest[: len(fetched)], rest[len(fetched) :]
            targets, rest = rest[: len(outs)], rest[len(outs) :]
            buffers, rest = rest[: len(fetched)], rest[len(fetched) :]
            kept, (arrivals, departures) = rest[: len(outs)], rest[len(outs) :]
            inputs = [Fetched(s, b, arrivals.at[i]) for i, (s, b) in enumerate(zip(sources, buffers))]
            outputs = [Stored(t, b, departures.at[i]) for i, (t, b) in enumerate(zip(targets, kept))]
            body(*small, *inputs, *outputs)
            for output in outputs:
                output.copy.wait()

    return pl.pallas_call(
        guarded,
        out_shape=tuple(jax.ShapeDtypeStruct(shape, F32) for shape in outs),
        in_specs=[pl.BlockSpec(memory_space=pltpu.SMEM)] + [here] * len(args) + [there] * len(fetched),
        out_specs=tuple(there for _ in outs),
        scratch_shapes=scratch,
        compiler_params=pltpu.CompilerParams(vmem_limit_bytes=60 * 2**20),
        cost_estimate=pl.CostEstimate(flops=flops, bytes_accessed=16 * 2**20, transcendentals=0),
    )(chosen, *args, *fetched)


def outer_call(split_left, outs, widths, flops, chosen, first, second):
    there = pl.BlockSpec(memory_space=pl.ANY)
    args = [array for side in (first, second) for factor in side for array in factor]
    return pl.pallas_call(
        partial(outer_sum, split_left),
        out_shape=tuple(jax.ShapeDtypeStruct(shape, F32) for shape in outs),
        in_specs=[pl.BlockSpec(memory_space=pltpu.SMEM)] + [there] * len(args),
        out_specs=tuple(there for _ in outs),
        scratch_shapes=[pltpu.VMEM(shape, F32) for shape in outs]
        + [pltpu.VMEM((sum(CHUNKS), w), F32) for w in widths]
        + [
            pltpu.SemaphoreType.DMA((len(widths) * len(CHUNKS),)),
            pltpu.SemaphoreType.DMA((len(outs),)),
        ],
        compiler_params=pltpu.CompilerParams(vmem_limit_bytes=60 * 2**20),
        cost_estimate=pl.CostEstimate(flops=flops, bytes_accessed=16 * 2**20, transcendentals=0),
    )(chosen, *args)


def other_core(value):
    return lax.ppermute(value, "mp", [(0, 1), (1, 0)])


def gather_blocks(value):
    count = lax.axis_size("edge")
    if count & (count - 1) or count > 8:
        return lax.all_gather(value, "edge", axis=0)
    index = lax.axis_index("edge")
    out = value[None]
    step = 1
    while step < count:
        got = lax.ppermute(out, "edge", [(i, i ^ step) for i in range(count)])
        low = (index // step) % 2 == 0
        out = jnp.where(low, jnp.concatenate([out, got]), jnp.concatenate([got, out]))
        step *= 2
    return out


def prefix_in_rows(flags):
    rows, length = flags.shape
    pieces = flags.reshape(rows, length // LANES, LANES)
    upper = (jnp.arange(LANES)[:, None] <= jnp.arange(LANES)[None, :]).astype(F32)
    inner = jnp.einsum("rkl,lm->rkm", pieces, upper, precision=HIGHEST)
    totals = inner[:, :, -1]
    count = length // LANES
    before = (jnp.arange(count)[:, None] < jnp.arange(count)[None, :]).astype(F32)
    offsets = jnp.dot(totals, before, precision=HIGHEST)
    return (inner + offsets[:, :, None]).reshape(rows, length)


def plan_edges(edge_vectors, edge_species, centres, edge_mask, structures):
    batch_count, _, edge_count = edge_vectors.shape
    blocks = lax.axis_size("edge")
    block = lax.axis_index("edge")
    core = lax.axis_index("mp")
    atoms = blocks * ATOM_DEV
    per_block = batch_count * edge_count
    vectors = edge_vectors.transpose(1, 0, 2).reshape(3, per_block)
    squares = jnp.maximum(jnp.sum(vectors * vectors, axis=0), 0.25)
    live = ((jnp.sqrt(squares) / CUTOFF) < 1.0) & (edge_mask.reshape(-1) > 0)
    batch_of = jnp.arange(per_block) // edge_count
    raw = jnp.concatenate(
        [
            vectors,
            edge_species.transpose(1, 0, 2).reshape(2, per_block).astype(F32),
            (centres.reshape(-1) + batch_of * atoms).astype(F32)[None],
            live.astype(F32)[None],
            (structures.reshape(-1) + batch_of * STRUCTS).astype(F32)[None],
        ]
    )
    gathered = gather_blocks(raw)
    keys = gathered[:, 5].reshape(blocks, batch_count, edge_count)
    alive = gathered[:, 6].reshape(blocks, batch_count, edge_count)
    local = keys - (jnp.arange(batch_count) * atoms)[None, :, None].astype(F32)
    degree = jnp.sum(
        jnp.where(
            local.transpose(1, 0, 2).reshape(batch_count, 1, -1)
            == jnp.arange(atoms, dtype=F32)[None, :, None],
            alive.transpose(1, 0, 2).reshape(batch_count, 1, -1),
            0.0,
        ),
        axis=2,
    )
    spans = batch_count * ATOM_DEV
    degree = degree.reshape(batch_count, blocks, ATOM_DEV).transpose(1, 0, 2).reshape(blocks, spans)
    upper = (jnp.arange(spans)[:, None] <= jnp.arange(spans)[None, :]).astype(F32)
    upto = jnp.dot(degree, upper, precision=HIGHEST)
    start = jnp.zeros((blocks, 1), F32)
    starts = [start]
    for size in CHUNKS:
        for _ in range(2):
            start = jnp.max(jnp.where(upto <= start + size, jnp.maximum(upto, start), start), axis=1, keepdims=True)
            starts.append(start)
    fits = jnp.all(starts[-1] >= upto[:, -1:])
    starts = jnp.concatenate(starts[:-1], axis=1)
    own_before = (upto - degree)[block]
    bin_of = jnp.sum((own_before[:, None] >= starts[block][None, 1:]).astype(F32), axis=1)
    padded = jnp.concatenate([jnp.zeros_like(gathered[:1]), gathered, jnp.zeros_like(gathered[:1])])
    window = lax.dynamic_slice_in_dim(padded, block, 3, 0)
    flat = window.transpose(1, 0, 2).reshape(8, 3 * per_block)
    position = jnp.arange(3 * per_block)
    batch_flat = (position % per_block) // edge_count
    spot = flat[5] - (batch_flat * atoms + block * ATOM_DEV).astype(F32)
    mine = (spot >= 0) & (spot < ATOM_DEV) & (flat[6] > 0.5)
    slot = jnp.where(mine, spot + (batch_flat * ATOM_DEV).astype(F32), -1.0)
    chosen = jnp.sum(
        jnp.where(jnp.arange(spans, dtype=F32)[:, None] == slot[None, :], bin_of[:, None], 0.0), axis=0
    )
    wanted = 2 * jnp.arange(len(CHUNKS)) + core
    picked = (chosen[None, :] == wanted[:, None].astype(F32)) & mine[None, :]
    rank = prefix_in_rows(picked.astype(F32)) - 1.0
    offsets = [sum(CHUNKS[:k]) for k in range(len(CHUNKS))]
    place = jnp.sum(
        jnp.where(picked, rank + jnp.array(offsets, F32)[:, None], 0.0), axis=0
    ) - (1.0 - jnp.sum(picked.astype(F32), axis=0))
    total = sum(CHUNKS)
    hot = (place[None, :] == jnp.arange(total, dtype=F32)[:, None]).astype(F32)
    edges = lax.dot_general(hot, flat, (((1,), (1,)), ((), ())), precision=HIGHEST)
    return fits, edges, place


def tied(first, *others):
    return lax.optimization_barrier((first, others))[0]


def hop(value, distance):
    return lax.ppermute(value, "edge", [(i, i ^ distance) for i in range(8)])


def halves(value, second):
    half = value.shape[0] // 2
    kept = lax.dynamic_slice_in_dim(value, second * half, half, 0)
    return kept, lax.dynamic_slice_in_dim(value, (1 - second) * half, half, 0)


def joined(kept, got, second):
    return jnp.where(second == 0, jnp.concatenate([kept, got]), jnp.concatenate([got, kept]))


def sum_piece(value, outer_hop, inner_hop):
    index = lax.axis_index("edge")
    seconds = {1: index % 2, 2: ((index // 2) ^ (index // 4)) % 2}
    kept, given = halves(value, seconds[outer_hop])
    kept, given = halves(kept + hop(given, outer_hop), seconds[inner_hop])
    part = kept + hop(given, inner_hop)
    part = part + hop(part, 6)
    part = joined(part, hop(part, inner_hop), seconds[inner_hop])
    half = part.shape[0]
    return [(part, seconds[outer_hop] * half), (hop(part, outer_hop), (1 - seconds[outer_hop]) * half)]


def sum_blocks(matrices, plan):
    if lax.axis_size("edge") != 8:
        return [lax.psum(value, "edge") for value in matrices]
    sums = [jnp.zeros_like(value) for value in matrices]
    for which, first, rows, outer_hop, inner_hop in plan:
        piece = lax.slice_in_dim(matrices[which], first, first + rows, axis=0)
        for part, start in sum_piece(piece, outer_hop, inner_hop):
            sums[which] = lax.dynamic_update_slice_in_dim(sums[which], part, first + start, 0)
    return sums


def fast_device(edges, place, others, args):
    (
        edge_vectors, edge_species, centres, edge_mask, structures, energy_cot, embed_in,
        section_head, env_weight, mix_weight, w_in, w_out, read_weight,
    ) = args
    is_first = lax.axis_index("section") == 0
    core = lax.axis_index("mp")
    width = section_head.shape[1]
    half = section_head.shape[2]
    batch_count, _, edge_count = edge_vectors.shape
    chan_count = mix_weight.shape[1]
    gap = LANES - chan_count
    read_left, read_right = read_weight[:half], read_weight[half:]
    read_line = jnp.where(
        core == 0,
        jnp.concatenate([read_left, read_right]),
        jnp.concatenate([read_right, read_left]),
    )[None]
    cot_row = jnp.pad(energy_cot.reshape(1, -1), ((0, 0), (0, LANES - energy_cot.size)))
    lead_flag = jnp.full((8, LANES), 1.0, F32) * (core == 0).astype(F32)
    mix = jnp.pad(mix_weight, ((0, 0), (0, gap), (0, gap)))
    env_w = jnp.pad(env_weight[0], ((0, 0), (0, gap)))
    env_wt = env_w.T
    heads, ins, outs_w = (section_head[0], others[0]), (w_in[0], others[1]), (w_out[0], others[2])
    count = len(CHUNKS)
    offsets = [sum(CHUNKS[:k]) for k in range(count)]
    rows = [edges[o : o + m, 5].reshape(1, -1) for o, m in zip(offsets, CHUNKS)]
    layer_width = width + 2 * LANES

    first_flag = jnp.full((1,), 1, jnp.int32) * is_first.astype(jnp.int32)
    second_flag = 1 - first_flag
    saved, moved = [], []
    for k, m in enumerate(CHUNKS):
        outs = [(m, width + LANES), (m, width), (m, layer_width), (m, width), (m, width)]
        work = 12 * m * width * (3 * width + 384)
        result = on_core(
            partial(first_forward, offsets[k]), outs, work,
            (edges, rows[k], lead_flag, embed_in), (*heads, env_w, *ins, *outs_w), first_flag,
        )
        moved.append(shifted(result[0], "section", 1))
        saved.append(result[1:])
    seconds, returned, firsts = [], [], []
    for k, m in enumerate(CHUNKS):
        outs = [
            (m, width + LANES), (m, layer_width), (m, width), (m, width), (m, width),
            (m, width), (m, width), (m, LANES), (8, width), (3, LANES, LANES), (8, LANES),
        ]
        work = 18 * m * width * (3 * width + 384)
        seconds.append(
            on_core(
                partial(second_both, offsets[k]), outs, work,
                (edges, rows[k], mix, read_line, cot_row),
                (moved[k], env_w, *ins, *outs_w, *heads, env_wt), second_flag,
            )
        )
    outer_work = 6 * sum(CHUNKS) * width * width
    for k, m in enumerate(CHUNKS):
        back = seconds[k][0] if k == 0 else tied(seconds[k][0], firsts[k - 1][0])
        returned.append(shifted(back, "section", -1))
        arrived = returned[k]
        if k == count - 1:
            out_own, out_other = outer_call(
                True, [(half, width)] * 2, (width, width), outer_work, second_flag,
                ([s[3] for s in saved], returned),
                ([s[3] for s in seconds], [s[4] for s in seconds]),
            )
            arrived = tied(arrived, out_other)
        outs = [(m, LANES), (m, width), (m, width), (m, LANES), (16, width)]
        work = 9 * m * width * (3 * width + 384)
        firsts.append(
            on_core(
                partial(first_backward, offsets[k]), outs, work,
                (edges, rows[k], lead_flag, embed_in),
                (saved[k][1], env_w, arrived, *outs_w, saved[k][2], *ins, env_wt, *heads), first_flag,
            )
        )
    grad_out = out_own + other_core(out_other)
    in_own, in_other, grad_env = outer_call(
        False, [(layer_width, half)] * 2 + [(width, LANES)], (layer_width, width, LANES), outer_work,
        second_flag,
        ([s[1] for s in saved], [f[2] for f in firsts], [f[3] for f in firsts]),
        ([s[1] for s in seconds], [s[2] for s in seconds], [s[7] for s in seconds]),
    )
    grad_in = in_own + other_core(in_other)
    head_own, head_other = outer_call(
        False, [(width, half)] * 2, (width, width), outer_work, tied(second_flag, in_other),
        ([s[0] for s in saved], [f[1] for f in firsts]),
        ([s[5] for s in seconds], [s[6] for s in seconds]),
    )
    none = jnp.zeros((), F32)
    read_sum = sum(s[8][0] for s in seconds)
    read_sum = jnp.where(
        core == 0, read_sum, jnp.concatenate([read_sum[half:], read_sum[:half]])
    )
    mix_sum = sum(s[9] for s in seconds)[:, :chan_count, :chan_count].reshape(-1, width)
    energy_sum = sum(s[10][0] for s in seconds)
    embed_sum = sum(f[4] for f in firsts)
    small_second = jnp.concatenate(
        [read_sum[None], jnp.pad(energy_sum, (0, width - LANES))[None], mix_sum]
    )
    small_second = jnp.pad(small_second, ((0, 16 - small_second.shape[0]), (0, 0)))
    small = jnp.concatenate(
        [jnp.where(is_first, embed_sum, none), jnp.where(is_first, none, small_second)]
    )
    small = small + lax.ppermute(small, "section", [(0, 1), (1, 0)])
    small = jnp.concatenate([small, grad_env[:, :chan_count].reshape(-1, width)]).reshape(-1, half)
    head_own = jnp.concatenate([head_own, small])
    grad_head = head_own + other_core(jnp.concatenate([head_other, small]))
    grad_out, grad_in, grad_head = sum_blocks(
        [grad_out, grad_in, grad_head],
        [
            (0, 0, 512, 2, 1), (1, 0, 640, 1, 2), (1, 640, 640, 1, 2), (2, 0, 608, 2, 1),
            (2, 608, 608, 1, 2),
        ],
    )
    small = grad_head[width:].reshape(-1, width)
    grad_head = grad_head[:width]
    grad_embed, grad_read = small[:16], small[16]
    energies = small[17, : energy_cot.size].reshape(energy_cot.shape)
    grad_mix = small[18 : 18 + mix_sum.shape[0]].reshape(mix_weight.shape)
    grad_env = small[32:].reshape(width, chan_count)

    d_vectors = jnp.concatenate([f[0][:, :8] for f in firsts])
    total = sum(CHUNKS)
    hot = (place[None, :] == jnp.arange(total, dtype=F32)[:, None]).astype(F32)
    spread = lax.dot_general(d_vectors, hot, (((0,), (0,)), ((), ())), precision=HIGHEST)[:3]
    spread = jnp.where(is_first, spread, none)
    spread = spread + other_core(spread)
    per_block = batch_count * edge_count
    to_left, kept, to_right = (spread[:, i * per_block : (i + 1) * per_block] for i in range(3))
    forces = kept + shifted(to_right, "edge", 1) + shifted(to_left, "edge", -1)
    forces = jnp.where(is_first, forces, shifted(forces, "section", 1))
    forces = -forces.reshape(3, batch_count, edge_count).transpose(1, 0, 2)
    return (
        energies, forces, grad_embed, grad_head[None], grad_env[None], grad_mix,
        grad_in[None, : w_in.shape[1]], grad_out[None], grad_read,
    )


def per_device(*args):
    section_head, w_in, w_out = args[7], args[10], args[11]
    others = tuple(other_core(m[0]) for m in (section_head, w_in, w_out))
    fits, edges, place = plan_edges(*args[:5])
    return lax.cond(
        fits,
        lambda: fast_device(edges, place, others, args),
        lambda: general_device(*args),
    )


def solution(mesh):
    placed = (
        P(None, None, "edge"),
        P(None, None, "edge"),
        P(None, "edge"),
        P(None, "edge"),
        P(None, "edge"),
        P(),
        P(),
        P("section", None, "mp"),
        P("section", None, None),
        P(),
        P("section", None, "mp"),
        P("section", "mp", None),
        P(),
    )
    return jax.shard_map(
        per_device,
        mesh=mesh,
        in_specs=placed,
        out_specs=(
            P(),
            P(None, None, "edge"),
            P(),
            P("section", None, "mp"),
            P("section", None, None),
            P(),
            P("section", None, "mp"),
            P("section", "mp", None),
            P(),
        ),
        check_vma=False,
    )
```

```python
from functools import partial

import jax
import jax.numpy as jnp
from jax import lax
from jax.experimental import pallas as pl
from jax.experimental.pallas import tpu as pltpu
from jax.sharding import PartitionSpec as P

NBES = 8
NSPEC = 4
ATOM_DEV = 40
STRUCTS = 16


CUTOFF = 5.0
ENV_SCALE = 0.25
HIGHEST = lax.Precision.HIGHEST
ROOT_THREE = 1.7320508075688772
ROOT_FIVE = 2.23606797749979
ROOT_FIFTEEN = 3.872983346207417


def extended(block, sides, width):
    for axis, dim in sides:
        count = lax.axis_size(axis)
        forward = [(i, i + 1) for i in range(count - 1)]
        backward = [(target, source) for source, target in forward]
        low = lax.ppermute(
            lax.slice_in_dim(block, block.shape[dim] - width, None, axis=dim), axis, forward
        )
        high = lax.ppermute(lax.slice_in_dim(block, 0, width, axis=dim), axis, backward)
        block = jnp.concatenate([low, block, high], axis=dim)
    return block


def shifted(value, axis, steps):
    count = lax.axis_size(axis)
    first, last = (max(0, -steps), min(count, count - steps))
    return lax.ppermute(value, axis, [(source, source + steps) for source in range(first, last)])


def other_core(value):
    return lax.ppermute(value, "mp", [(0, 1), (1, 0)])


def ring_sum(values):
    count = lax.axis_size("edge")

    def step(_, state):
        moving, total = state
        moving = tuple(
            lax.ppermute(v, "edge", [(i, (i + 1) % count) for i in range(count)]) for v in moving
        )
        return moving, tuple(t + v for t, v in zip(total, moving))

    return lax.fori_loop(0, count - 1, step, (tuple(values), tuple(values)))[1]


def matmul(left, right):
    return jnp.dot(left, right, precision=HIGHEST, preferred_element_type=jnp.float32)


def geometry(vectors, edge_live):
    squares = jnp.maximum(jnp.sum(vectors * vectors, axis=0), 0.25)
    length = jnp.sqrt(squares)
    unit_x = vectors[0] / length
    unit_y = vectors[1] / length
    unit_z = vectors[2] / length
    edge_ratio = jnp.minimum(length / CUTOFF, 1.0)
    envelope = (
        1.0 - 28.0 * edge_ratio**6 + 48.0 * edge_ratio**7 - 21.0 * edge_ratio**8
    ) * edge_live
    orders = jnp.arange(1, NBES + 1).astype(jnp.float32)
    bessel = (
        jnp.sqrt(2.0 / CUTOFF)
        * jnp.sin(orders[None, :] * (jnp.pi / CUTOFF) * length[:, None])
        / length[:, None]
    )
    harmonics = jnp.stack(
        [
            jnp.ones_like(unit_x),
            ROOT_THREE * unit_x,
            ROOT_THREE * unit_y,
            ROOT_THREE * unit_z,
            ROOT_FIFTEEN * unit_x * unit_y,
            ROOT_FIFTEEN * unit_y * unit_z,
            0.5 * ROOT_FIVE * (3.0 * unit_z * unit_z - 1.0),
            ROOT_FIFTEEN * unit_x * unit_z,
            0.5 * ROOT_FIFTEEN * (unit_x * unit_x - unit_y * unit_y),
        ],
        axis=1,
    )
    return (harmonics, envelope, bessel)


def couple(edge_tensor, env_flat, mix_weight):
    chan_count = mix_weight.shape[1]
    own_tensor = edge_tensor.reshape(-1, 9, chan_count)
    env_tensor = env_flat.reshape(-1, 9, chan_count)
    paired = own_tensor * env_tensor
    scalars = jnp.concatenate(
        [paired[:, 0], jnp.sum(paired[:, 1:4], axis=1), jnp.sum(paired[:, 4:9], axis=1)], axis=1
    )
    coupled = own_tensor * env_tensor[:, 0:1] + own_tensor[:, 0:1] * env_tensor
    order_zero = jnp.einsum("emc,cd->emd", coupled[:, 0:1], mix_weight[0], precision=HIGHEST)
    order_one = jnp.einsum("emc,cd->emd", coupled[:, 1:4], mix_weight[1], precision=HIGHEST)
    order_two = jnp.einsum("emc,cd->emd", coupled[:, 4:9], mix_weight[2], precision=HIGHEST)
    updated = jnp.concatenate([order_zero, order_one, order_two], axis=1)
    return (scalars, updated.reshape(-1, 9 * chan_count))


def front(bessel, envelope, embed_in, head_local, kinds_hot):
    features = jnp.concatenate([kinds_hot, bessel], axis=1)
    return envelope[:, None] * matmul(jax.nn.silu(matmul(features, embed_in)), head_local)


def contribute(latent_full, harmonics, envelope, env_local, centre_hot):
    weight = matmul(latent_full, env_local)
    contribution = (
        (ENV_SCALE * envelope)[:, None, None] * harmonics[:, :, None] * weight[:, None, :]
    )
    flat_terms = contribution.reshape(weight.shape[0], -1)
    return (weight, matmul(centre_hot.T, flat_terms))


def tensor_step(tensor_full, env_window, weight, harmonics, mix_weight, centre_hot, is_first):
    start_tensor = (harmonics[:, :, None] * weight[:, None, :]).reshape(weight.shape[0], -1)
    edge_tensor = jnp.where(is_first, start_tensor, tensor_full)
    env_flat = matmul(centre_hot, env_window)
    return couple(edge_tensor, env_flat, mix_weight)


def perceptron(latent_full, scalars, in_local, out_local):
    hidden = jax.nn.silu(matmul(jnp.concatenate([latent_full, scalars], axis=1), in_local))
    return matmul(hidden, out_local)


def readout(latent_full, envelope, head_local, read_half):
    return envelope * matmul(jax.nn.silu(matmul(latent_full, head_local)), read_half)


def general_device(
    edge_vectors,
    edge_species,
    centres,
    edge_mask,
    structures,
    energy_cot,
    embed_in,
    section_head,
    env_weight,
    mix_weight,
    w_in,
    w_out,
    read_weight,
):
    section_index = lax.axis_index("section")
    core_index = lax.axis_index("mp")
    edge_index = lax.axis_index("edge")
    is_first = section_index == 0
    last_flag = (section_index == 1).astype(jnp.float32)
    batch_count = edge_vectors.shape[0]
    shard_width = w_out.shape[1]
    tensor_cols = 9 * env_weight.shape[2]
    tensor_half = tensor_cols // 2
    atoms_dev = ATOM_DEV
    head_local = section_head[0]
    env_local = env_weight[0]
    in_local = w_in[0]
    out_local = w_out[0]
    read_half = lax.dynamic_slice_in_dim(read_weight, core_index * shard_width, shard_width, 0)
    core_lead = (core_index == 0).astype(jnp.float32)
    edge_count = edge_vectors.shape[2]
    centre_slots = jnp.arange(3 * atoms_dev)
    labels = jnp.arange(STRUCTS)
    species_range = jnp.arange(NSPEC)
    batch_range = jnp.arange(batch_count)

    def reduce_rims(pieces):
        widened = extended(pieces, (("edge", 0),), atoms_dev)
        return (
            widened[:atoms_dev] + widened[2 * atoms_dev : 3 * atoms_dev] + widened[4 * atoms_dev :]
        )

    def window_rows(totals):
        return extended(totals, (("edge", 0),), atoms_dev)

    def collect(partial_rows):
        width = partial_rows.shape[1] // 2
        own = lax.dynamic_slice_in_dim(partial_rows, core_index * width, width, 1)
        return own + other_core(lax.dynamic_slice_in_dim(partial_rows, (1 - core_index) * width, width, 1))

    def both_halves(half):
        other = other_core(half)
        return jnp.where(
            core_index == 0,
            jnp.concatenate([half, other], axis=1),
            jnp.concatenate([other, half], axis=1),
        )

    def batch_data(batch_index):
        vectors = lax.dynamic_index_in_dim(edge_vectors, batch_index, 0, keepdims=False)
        kind_ids = lax.dynamic_index_in_dim(edge_species, batch_index, 0, keepdims=False)
        owners = lax.dynamic_index_in_dim(centres, batch_index, 0, keepdims=False)
        edge_live = lax.dynamic_index_in_dim(edge_mask, batch_index, 0, keepdims=False).astype(
            jnp.float32
        )
        groups = lax.dynamic_index_in_dim(structures, batch_index, 0, keepdims=False)
        kinds_hot = jnp.concatenate(
            [
                kind_ids[0][:, None] == species_range[None, :],
                kind_ids[1][:, None] == species_range[None, :],
            ],
            axis=1,
        ).astype(jnp.float32)
        local_slot = owners - (edge_index - 1) * atoms_dev
        centre_hot = (local_slot[:, None] == centre_slots[None, :]).astype(jnp.float32)
        group_hot = (groups[:, None] == labels[None, :]).astype(jnp.float32)
        return (vectors, edge_live, kinds_hot, centre_hot, group_hot)

    recv_latent = jnp.zeros((edge_count, shard_width), jnp.float32)
    recv_tensor = jnp.zeros((edge_count, tensor_half), jnp.float32)
    energies = jnp.zeros((batch_count, STRUCTS), jnp.float32)
    kept_state = []
    for step_index in range(batch_count + 1):
        batch_raw = step_index - section_index
        batch_index = jnp.clip(batch_raw, 0, batch_count - 1)
        is_valid = ((batch_raw >= 0) & (batch_raw < batch_count)).astype(jnp.float32)
        vectors, edge_live, kinds_hot, centre_hot, group_hot = batch_data(batch_index)
        harmonics, envelope, bessel = geometry(vectors, edge_live)
        latent_half = lax.cond(
            is_first,
            lambda: front(bessel, envelope, embed_in, head_local, kinds_hot),
            lambda: recv_latent,
        )
        latent_full, tensor_full = (
            both_halves(latent_half),
            both_halves(recv_tensor),
        )
        weight, part_sums = contribute(latent_full, harmonics, envelope, env_local, centre_hot)
        env_window = window_rows(reduce_rims(part_sums))
        scalars, updated = tensor_step(
            tensor_full, env_window, weight, harmonics, mix_weight, centre_hot, is_first
        )
        branch_out = perceptron(latent_full, scalars, in_local, out_local)
        summed = collect(branch_out)
        tensor_own = lax.dynamic_slice_in_dim(updated, core_index * tensor_half, tensor_half, 1)
        next_half = latent_half + summed
        recv_latent, recv_tensor = shifted((next_half, tensor_own), "section", 1)
        next_full = both_halves(next_half)
        edge_energy = readout(next_full, envelope, head_local, read_half)
        batch_slot = (batch_range == batch_index).astype(jnp.float32) * is_valid * last_flag
        energies = (
            energies
            + batch_slot[:, None] * jnp.dot(edge_energy, group_hot, precision=HIGHEST)[None, :]
        )
        kept_state.append((latent_full, tensor_full, env_window, next_full))
    kept_latent = jnp.stack([entry[0] for entry in kept_state])
    kept_tensor = jnp.stack([entry[1] for entry in kept_state])
    kept_window = jnp.stack([entry[2] for entry in kept_state])
    kept_next = jnp.stack([entry[3] for entry in kept_state])
    grad_head = jnp.zeros_like(head_local)
    grad_env = jnp.zeros_like(env_local)
    grad_in = jnp.zeros_like(in_local)
    grad_out = jnp.zeros_like(out_local)
    grad_mix = jnp.zeros_like(mix_weight)
    grad_embed = jnp.zeros_like(embed_in)
    grad_read = jnp.zeros_like(read_half)
    forces = jnp.zeros((batch_count, 3, edge_count), jnp.float32)
    recv_grad = jnp.zeros((edge_count, shard_width), jnp.float32)
    recv_tgrad = jnp.zeros((edge_count, tensor_half), jnp.float32)
    for step_index in range(batch_count + 1):
        batch_raw = step_index - 1 + section_index
        batch_index = jnp.clip(batch_raw, 0, batch_count - 1)
        is_valid = ((batch_raw >= 0) & (batch_raw < batch_count)).astype(jnp.float32)
        saved_index = jnp.clip(batch_raw + section_index, 0, batch_count)
        latent_full = lax.dynamic_index_in_dim(kept_latent, saved_index, 0, keepdims=False)
        tensor_full = lax.dynamic_index_in_dim(kept_tensor, saved_index, 0, keepdims=False)
        env_window = lax.dynamic_index_in_dim(kept_window, saved_index, 0, keepdims=False)
        next_full = lax.dynamic_index_in_dim(kept_next, saved_index, 0, keepdims=False)
        vectors, edge_live, kinds_hot, centre_hot, group_hot = batch_data(batch_index)
        (harmonics, envelope, bessel), geometry_pull = jax.vjp(
            partial(geometry, edge_live=edge_live), vectors
        )
        batch_cot = lax.dynamic_index_in_dim(energy_cot, batch_index, 0, keepdims=False)
        energy_rows = jnp.dot(group_hot, batch_cot, precision=HIGHEST) * (is_valid * last_flag)
        _, read_pull = jax.vjp(readout, next_full, envelope, head_local, read_half)
        d_next_read, d_env_read, g_head_read, g_read = read_pull(energy_rows)
        d_next_half = jnp.where(is_first, recv_grad, collect(d_next_read))
        d_out_full, d_updated = (
            both_halves(d_next_half),
            both_halves(recv_tgrad),
        )
        (weight, part_sums), contribute_pull = jax.vjp(
            partial(contribute, centre_hot=centre_hot), latent_full, harmonics, envelope, env_local
        )
        (scalars, updated), tensor_pull = jax.vjp(
            partial(tensor_step, centre_hot=centre_hot, is_first=is_first),
            tensor_full,
            env_window,
            weight,
            harmonics,
            mix_weight,
        )
        _, perceptron_pull = jax.vjp(perceptron, latent_full, scalars, in_local, out_local)
        d_latent_mlp, d_scalar_part, g_in, g_out = perceptron_pull(d_out_full)
        d_scalars = d_scalar_part + other_core(d_scalar_part)
        d_tensor, d_window, d_weight, d_harm_tensor, g_mix = tensor_pull((d_scalars, d_updated))
        d_parts = window_rows(reduce_rims(d_window))
        d_latent_env, d_harm_env, d_envelope_env, g_env = contribute_pull((d_weight, d_parts))
        d_latent_own = (
            collect(d_latent_mlp)
            + lax.dynamic_slice_in_dim(d_latent_env, core_index * shard_width, shard_width, 1)
            + d_next_half
        )
        d_tensor_own = lax.dynamic_slice_in_dim(d_tensor, core_index * tensor_half, tensor_half, 1)
        recv_grad, recv_tgrad = shifted((d_latent_own, d_tensor_own), "section", -1)

        def front_pull(cotangent):
            _, pull_back = jax.vjp(
                partial(front, kinds_hot=kinds_hot), bessel, envelope, embed_in, head_local
            )
            return pull_back(cotangent)

        def front_none(cotangent):
            return (
                jnp.zeros_like(bessel),
                jnp.zeros_like(envelope),
                jnp.zeros_like(embed_in),
                jnp.zeros_like(head_local),
            )

        d_bessel, d_envelope_front, g_embed, g_head_front = lax.cond(
            is_first, front_pull, front_none, d_latent_own
        )
        d_harmonics = core_lead * (d_harm_tensor + d_harm_env)
        d_envelope = core_lead * d_envelope_env + d_env_read + d_envelope_front
        d_vectors = geometry_pull((d_harmonics, d_envelope, d_bessel))[0]
        batch_slot = (batch_range == batch_index).astype(jnp.float32) * is_valid
        forces = forces + batch_slot[:, None, None] * d_vectors[None]
        grad_head = grad_head + is_valid * (g_head_read + g_head_front)
        grad_env = grad_env + is_valid * g_env
        grad_in = grad_in + is_valid * g_in
        grad_out = grad_out + is_valid * g_out
        grad_mix = grad_mix + is_valid * g_mix
        grad_embed = grad_embed + is_valid * g_embed
        grad_read = grad_read + is_valid * g_read
    grad_head, grad_env, grad_in, grad_out = ring_sum((grad_head, grad_env, grad_in, grad_out))
    read_full = lax.dynamic_update_slice_in_dim(
        jnp.zeros_like(read_weight), grad_read, core_index * shard_width, 0
    )
    chip_sums = [v + other_core(v) for v in (energies, grad_embed, core_lead * grad_mix, read_full, forces)]
    energies, grad_embed, grad_mix, read_full, forces = (
        v + lax.ppermute(v, "section", [(0, 1), (1, 0)]) for v in chip_sums
    )
    energies, grad_embed, grad_mix, read_full = ring_sum((energies, grad_embed, grad_mix, read_full))
    return (
        energies,
        -forces,
        grad_embed,
        grad_head[None],
        grad_env[None],
        grad_mix,
        grad_in[None],
        grad_out[None],
        read_full,
    )


CHUNKS = (160, 160, 160)
LANES = 128
F32 = jnp.float32
BF16 = jnp.bfloat16
BESSEL_SCALE = (2.0 / CUTOFF) ** 0.5
ANGLE = 3.141592653589793 / CUTOFF


def dot_nn(left, right):
    return jnp.dot(left, right, preferred_element_type=F32)


def dot_nt(left, right):
    return lax.dot_general(left, right, (((1,), (1,)), ((), ())), preferred_element_type=F32)


def dot_tn(left, right):
    return lax.dot_general(left, right, (((0,), (0,)), ((), ())), preferred_element_type=F32)


def split_two(value):
    high = value.astype(BF16)
    return high, (value - high.astype(F32)).astype(BF16)


def split_three(value):
    high = value.astype(BF16)
    rest = value - high.astype(F32)
    middle = rest.astype(BF16)
    return high, middle, (rest - middle.astype(F32)).astype(BF16)


def six_pass(left, right):
    rows = left.shape[0]
    high, middle, low = split_three(left)
    three = dot_nn(jnp.concatenate([high, middle, low], axis=0), right[0])
    two = dot_nn(jnp.concatenate([high, middle], axis=0), right[1])
    small = three[2 * rows :] + two[rows:] + dot_nn(high, right[2])
    return three[:rows] + (three[rows : 2 * rows] + two[:rows] + small)


def three_pass(dot, left, right):
    rows = left.shape[0]
    high, low = split_two(left)
    both = dot(jnp.concatenate([high, low], axis=0), right[0])
    return both[:rows] + both[rows:] + dot(high, right[1])


def three_pass_tn(left, right):
    left_high, left_low = split_two(left)
    right_high, right_low = split_two(right)
    return dot_tn(
        jnp.concatenate([left_high, left_low, left_high], axis=0),
        jnp.concatenate([right_high, right_high, right_low], axis=0),
    )


def sigmoid(value):
    return 1.0 / (1.0 + jnp.exp(-value))


def order_of(component):
    return 0 if component == 0 else (1 if component < 4 else 2)


def same_sum(same, parts):
    high, middle, low = split_three(jnp.concatenate(parts, axis=1))
    summed = dot_nn(same, high) + (dot_nn(same, middle) + dot_nn(same, low))
    return [summed[:, LANES * m : LANES * (m + 1)] for m in range(len(parts))]


def place_columns(columns, first, width=LANES):
    lane = lax.broadcasted_iota(jnp.int32, (columns[0].shape[0], width), 1)
    out = jnp.zeros((columns[0].shape[0], width), F32)
    for i, column in enumerate(columns):
        out = jnp.where(lane == first + i, column, out)
    return out


def waves(length):
    turn = length * ANGLE - 1.5707963267948966
    square = turn * turn
    even, odd, term_even, term_odd = 1.0, 1.0, 1.0, 1.0
    coefficients_even, coefficients_odd = [], []
    for n in range(1, 9):
        term_even = -term_even / ((2 * n - 1) * (2 * n))
        term_odd = -term_odd / ((2 * n) * (2 * n + 1))
        coefficients_even.append(term_even)
        coefficients_odd.append(term_odd)
    even = jnp.full_like(turn, coefficients_even[-1])
    odd = jnp.full_like(turn, coefficients_odd[-1])
    for n in range(6, -1, -1):
        even = even * square + coefficients_even[n]
        odd = odd * square + coefficients_odd[n]
    sines = {1: even * square + 1.0}
    cosines = {1: -turn * (odd * square + 1.0)}
    for total, left, right in ((2, 1, 1), (3, 2, 1), (4, 2, 2), (5, 4, 1), (6, 4, 2), (7, 4, 3), (8, 4, 4)):
        sines[total] = sines[left] * cosines[right] + cosines[left] * sines[right]
        cosines[total] = cosines[left] * cosines[right] - sines[left] * sines[right]
    return [sines[k] for k in range(1, 9)], [cosines[k] for k in range(1, 9)]


def edge_values(edges, key_row, first, rows, full):
    block = edges[first : first + rows, :]
    vector = [block[:, i : i + 1] for i in range(3)]
    live = block[:, 6:7]
    squares = vector[0] * vector[0] + vector[1] * vector[1] + vector[2] * vector[2]
    length = jnp.sqrt(jnp.maximum(squares, 0.25))
    ux, uy, uz = (v / length for v in vector)
    ratio = jnp.minimum(length / CUTOFF, 1.0)
    second = ratio * ratio
    sixth = second * second * second
    envelope = (1.0 - 28.0 * sixth + 48.0 * (sixth * ratio) - 21.0 * (sixth * second)) * live
    harmonics = [
        jnp.ones_like(ux),
        ROOT_THREE * ux,
        ROOT_THREE * uy,
        ROOT_THREE * uz,
        ROOT_FIFTEEN * ux * uy,
        ROOT_FIFTEEN * uy * uz,
        0.5 * ROOT_FIVE * (3.0 * uz * uz - 1.0),
        ROOT_FIFTEEN * ux * uz,
        0.5 * ROOT_FIFTEEN * (ux * ux - uy * uy),
    ]
    same = jnp.where(block[:, 5:6] == key_row, 1.0, 0.0).astype(BF16)
    g = dict(
        env=envelope, harm=harmonics, same=same, squares=squares, length=length, ratio=ratio,
        unit=(ux, uy, uz), live=live, group=block[:, 7:8],
    )
    if full:
        sines, g["cosines"] = waves(length)
        g["bessel"] = [BESSEL_SCALE * value / length for value in sines]
        lane = lax.broadcasted_iota(jnp.int32, (rows, 16), 1).astype(F32)
        kinds = jnp.where(
            lane < NSPEC,
            jnp.where(block[:, 3:4] == lane, live, 0.0),
            jnp.where(block[:, 4:5] + NSPEC == lane, live, 0.0),
        )
        g["feat"] = kinds + place_columns(g["bessel"], 2 * NSPEC, 16)
    return g


def vector_pull(g, d_bessel, d_harm, d_envelope):
    ux, uy, uz = g["unit"]
    length, ratio = g["length"], g["ratio"]
    dx = ROOT_THREE * d_harm[1] + ROOT_FIFTEEN * (uy * d_harm[4] + uz * d_harm[7] + ux * d_harm[8])
    dy = ROOT_THREE * d_harm[2] + ROOT_FIFTEEN * (ux * d_harm[4] + uz * d_harm[5] - uy * d_harm[8])
    dz = (
        ROOT_THREE * d_harm[3]
        + ROOT_FIFTEEN * (uy * d_harm[5] + ux * d_harm[7])
        + (3.0 * ROOT_FIVE) * uz * d_harm[6]
    )
    left = 1.0 - ratio
    fourth = (ratio * ratio) * (ratio * ratio)
    d_length = (-168.0 / CUTOFF) * (fourth * ratio) * (left * left) * g["live"] * d_envelope
    d_length = d_length - (dx * ux + dy * uy + dz * uz) / length
    for k in range(NBES):
        slope = (BESSEL_SCALE * ANGLE * (k + 1)) * g["cosines"][k] - g["bessel"][k]
        d_length = d_length + d_bessel[k] * (slope / length)
    bound = jnp.where(g["squares"] > 0.25, 1.0, jnp.where(g["squares"] == 0.25, 0.5, 0.0))
    d_length = d_length * bound
    return [d / length + d_length * u for d, u in ((dx, ux), (dy, uy), (dz, uz))]


def env_terms(g, weight):
    scaled = ENV_SCALE * g["env"] * weight
    return same_sum(g["same"], [y * scaled for y in g["harm"]])


def pack_scalars(tensor, env):
    sums = [tensor[0] * env[0], tensor[1] * env[1], tensor[4] * env[4]]
    for m in (2, 3):
        sums[1] = sums[1] + tensor[m] * env[m]
    for m in (5, 6, 7, 8):
        sums[2] = sums[2] + tensor[m] * env[m]
    return jnp.concatenate([sums[0] + pltpu.roll(sums[1], 64, 1), sums[2]], axis=1)


def unpack_scalars(packed):
    first = packed[:, :LANES]
    return [first, pltpu.roll(first, 64, 1), packed[:, LANES:]]


def swap_order(lead, left, right):
    return jnp.where(lead, left, right), jnp.where(lead, right, left)


def env_pull(g, weight, d_env):
    d_terms = same_sum(g["same"], d_env)
    d_weight, d_harm, inner = None, [], None
    for m in range(9):
        part = g["harm"][m] * d_terms[m]
        d_weight = part if m == 0 else d_weight + part
        d_harm.append(jnp.sum(weight * d_terms[m], axis=1, keepdims=True))
        step = g["harm"][m] * d_harm[m]
        inner = step if m == 0 else inner + step
    scale = ENV_SCALE * g["env"]
    return scale * d_weight, [scale * d for d in d_harm], ENV_SCALE * inner


class Fetched:
    def __init__(self, source, buffer, semaphore):
        rows = source.shape[0]
        self.buffer, self.shape = buffer, buffer.shape
        target = buffer if rows == buffer.shape[0] else buffer.at[pl.ds(0, rows)]
        self.copy = pltpu.make_async_copy(source, target, semaphore)
        self.copy.start()
        self.arrived, self.pieces = False, {}
        if rows < buffer.shape[0]:
            buffer[rows:, :] = jnp.zeros((buffer.shape[0] - rows, buffer.shape[1]), F32)

    def __getitem__(self, where):
        if not self.arrived:
            self.copy.wait()
            self.arrived = True
        return self.buffer[where]

    def split(self, parts):
        if parts not in self.pieces:
            value = self[...]
            self.pieces[parts] = split_three(value) if parts == 3 else split_two(value)
        return self.pieces[parts]


class Stored:
    def __init__(self, target, buffer, semaphore):
        self.target, self.buffer, self.semaphore = target, buffer, semaphore
        self.shape, self.copy = buffer.shape, None

    def __setitem__(self, where, value):
        self.buffer[where] = value
        if where is Ellipsis:
            self.send()

    def __getitem__(self, where):
        return self.buffer[where]

    def send(self):
        self.copy = pltpu.make_async_copy(self.buffer, self.target, self.semaphore)
        self.copy.start()


def forward_pair(value, own, other):
    return [six_pass(value, own.split(3)), six_pass(value, other.split(3))]


def backward_pair(value, own, other, parts):
    return [three_pass(dot_nt, value, own.split(parts)), three_pass(dot_nt, value, other.split(parts))]


def first_forward(
    first, edges, key_row, lead_flag, embed,
    head_o, head_x, env_w, in_o, in_x, out_o, out_x,
    sent, soft_out, layer_in, slope_out, hidden,
):
    rows = sent.shape[0]
    lead = lead_flag[0:1, 0:1] > 0.5
    g = edge_values(edges, key_row[...], first, rows, True)
    pre = six_pass(g["feat"], split_three(embed[...]))
    soft = pre * sigmoid(pre)
    soft_out[...] = soft
    own, other = forward_pair(soft, head_o, head_x)
    latent = g["env"] * jnp.concatenate(swap_order(lead, own, other), axis=1)
    weight = six_pass(latent, env_w.split(3))
    env = env_terms(g, weight)
    scalars = pack_scalars([y * weight for y in g["harm"]], env)
    full = jnp.concatenate([latent, scalars], axis=1)
    layer_in[...] = full
    pre = jnp.concatenate(forward_pair(full, in_o, in_x), axis=1)
    gate = sigmoid(pre)
    slope_out[...] = gate * (1.0 + pre * (1.0 - gate))
    hid = pre * gate
    hidden[...] = hid
    half = hid.shape[1] // 2
    width = latent.shape[1]
    sent[:, :width] = (
        latent + six_pass(hid[:, :half], out_o.split(3)) + six_pass(hid[:, half:], out_x.split(3))
    )
    sent[:, width:] = weight
    sent.send()


def second_both(
    first, edges, key_row, mix, read, cot_row,
    arrived, env_w, in_o, in_x, out_o, out_x, head_o, head_x, env_wt,
    back, layer_in, d_pre_hidden, hidden, d_latent_out, latent_out, d_pre_read, d_weight_out,
    read_grad, mix_grad, energy_out,
):
    rows = back.shape[0]
    width = arrived.shape[1] - LANES
    half = width // 2
    g = edge_values(edges, key_row[...], first, rows, False)
    lane = lax.broadcasted_iota(jnp.int32, (rows, LANES), 1).astype(F32)
    group_hot = jnp.where(g["group"] == lane, g["live"], 0.0)
    cot = jnp.sum(group_hot * cot_row[...], axis=1, keepdims=True)
    mixes = [split_three(mix[i]) for i in range(3)]
    latent = arrived[:, :width]
    weight_first = arrived[:, width:]
    env_first = env_terms(g, weight_first)
    start = [y * weight_first for y in g["harm"]]
    coupled = [start[m] * env_first[0] + start[0] * env_first[m] for m in range(9)]
    members = ((0,), (1, 2, 3), (4, 5, 6, 7, 8))
    tensor = []
    for order in range(3):
        mixed = six_pass(jnp.concatenate([coupled[m] for m in members[order]], axis=0), mixes[order])
        tensor += [mixed[rows * i : rows * (i + 1)] for i in range(len(members[order]))]
    weight = six_pass(latent, env_w.split(3))
    env = env_terms(g, weight)
    full = jnp.concatenate([latent, pack_scalars(tensor, env)], axis=1)
    layer_in[...] = full
    pre = jnp.concatenate(forward_pair(full, in_o, in_x), axis=1)
    gate = sigmoid(pre)
    slope = gate * (1.0 + pre * (1.0 - gate))
    hid = pre * gate
    hidden[...] = hid
    latent_next = (
        latent + six_pass(hid[:, :half], out_o.split(3)) + six_pass(hid[:, half:], out_x.split(3))
    )
    latent_out[...] = latent_next
    pre_read = jnp.concatenate(forward_pair(latent_next, head_o, head_x), axis=1)
    gate = sigmoid(pre_read)
    soft = pre_read * gate
    line = read[...]
    inner = jnp.sum(soft * line, axis=1, keepdims=True)
    energy_out[...] = jnp.broadcast_to(
        jnp.sum(group_hot * (g["env"] * inner), axis=0, keepdims=True), energy_out.shape
    )
    scaled_cot = cot * g["env"]
    read_grad[...] = jnp.broadcast_to(
        jnp.sum(scaled_cot * soft, axis=0, keepdims=True), read_grad.shape
    )
    d_envelope = cot * inner
    d_read = scaled_cot * line * (gate * (1.0 + pre_read * (1.0 - gate)))
    d_pre_read[...] = d_read
    d_latent_out[...] = three_pass(dot_nt, d_read[:, :half], head_o.split(3)) + three_pass(
        dot_nt, d_read[:, half:], head_x.split(3)
    )
    d_hid = jnp.concatenate(backward_pair(d_latent_out[...], out_o, out_x, 3), axis=1)
    d_pre = d_hid * slope
    d_pre_hidden[...] = d_pre
    d_full = three_pass(dot_nt, d_pre[:, :half], in_o.split(3)) + three_pass(
        dot_nt, d_pre[:, half:], in_x.split(3)
    )
    d_scalars = unpack_scalars(d_full[:, width:])
    d_tensor = [d_scalars[order_of(m)] * env[m] for m in range(9)]
    d_env = [d_scalars[order_of(m)] * tensor[m] for m in range(9)]
    d_weight, d_harm, d_more = env_pull(g, weight, d_env)
    d_envelope = d_envelope + d_more
    d_weight_out[...] = d_weight
    back[:, :width] = (
        three_pass(dot_nn, d_weight_out[...], env_wt.split(2))
        + d_latent_out[...]
        + d_full[:, :width]
    )
    d_coupled = []
    for order in range(3):
        joined = jnp.concatenate([d_tensor[m] for m in members[order]], axis=0)
        mix_grad[order] = three_pass_tn(
            jnp.concatenate([coupled[m] for m in members[order]], axis=0), joined
        )
        mixed = three_pass(dot_nt, joined, mixes[order])
        d_coupled += [mixed[rows * i : rows * (i + 1)] for i in range(len(members[order]))]
    mix_grad.send()
    d_env_first = [d_coupled[m] * start[0] for m in range(9)]
    d_start = [d_coupled[m] * env_first[0] for m in range(9)]
    for m in range(9):
        d_env_first[0] = d_env_first[0] + d_coupled[m] * start[m]
        d_start[0] = d_start[0] + d_coupled[m] * env_first[m]
    d_first, d_harm_first, d_more = env_pull(g, weight_first, d_env_first)
    for m in range(9):
        d_first = d_first + g["harm"][m] * d_start[m]
        d_harm[m] = (
            d_harm[m]
            + d_harm_first[m]
            + jnp.sum(weight_first * d_start[m], axis=1, keepdims=True)
        )
    d_envelope = d_envelope + d_more
    back[:, width:] = d_first + place_columns(d_harm + [d_envelope], 64)
    back.send()


def first_backward(
    first, edges, key_row, lead_flag, embed,
    layer_in, env_w, arrived, out_o, out_x, slope_in, in_o, in_x, env_wt, head_o, head_x,
    d_vector, d_head, d_pre_hidden, d_weight_out, embed_grad,
):
    rows = arrived.shape[0]
    width = arrived.shape[1] - LANES
    half = width // 2
    lead = lead_flag[0:1, 0:1] > 0.5
    g = edge_values(edges, key_row[...], first, rows, True)
    embed_pair = split_two(embed[...])
    latent = layer_in[:, :width]
    weight = three_pass(dot_nn, latent, env_w.split(2))
    env = env_terms(g, weight)
    extra = arrived[:, width:]
    lane = lax.broadcasted_iota(jnp.int32, extra.shape, 1)
    d_weight = jnp.where(lane < 64, extra, 0.0)
    d_harm = [extra[:, 64 + m : 65 + m] for m in range(9)]
    d_envelope = extra[:, 73:74]
    d_hid = jnp.concatenate(backward_pair(arrived[:, :width], out_o, out_x, 2), axis=1)
    d_pre = d_hid * slope_in[...]
    d_pre_hidden[...] = d_pre
    d_full = three_pass(dot_nt, d_pre[:, :half], in_o.split(2)) + three_pass(
        dot_nt, d_pre[:, half:], in_x.split(2)
    )
    d_scalars = unpack_scalars(d_full[:, width:])
    d_start = [d_scalars[order_of(m)] * env[m] for m in range(9)]
    d_env = [d_scalars[order_of(m)] * (g["harm"][m] * weight) for m in range(9)]
    d_more_weight, d_more_harm, d_more = env_pull(g, weight, d_env)
    d_weight = d_weight + d_more_weight
    d_envelope = d_envelope + d_more
    for m in range(9):
        d_weight = d_weight + g["harm"][m] * d_start[m]
        d_harm[m] = (
            d_harm[m] + d_more_harm[m] + jnp.sum(weight * d_start[m], axis=1, keepdims=True)
        )
    d_weight_out[...] = d_weight
    d_latent = (
        three_pass(dot_nn, d_weight_out[...], env_wt.split(2))
        + arrived[:, :width]
        + d_full[:, :width]
    )
    d_own, d_other = swap_order(lead, d_latent[:, :half], d_latent[:, half:])
    d_head[:, :half] = g["env"] * d_own
    d_head[:, half:] = g["env"] * d_other
    d_head.send()
    d_soft = three_pass(dot_nt, d_own, head_o.split(2)) + three_pass(dot_nt, d_other, head_x.split(2))
    pre = three_pass(dot_nn, g["feat"], embed_pair)
    gate = sigmoid(pre)
    d_envelope = d_envelope + jnp.sum(pre * gate * d_soft, axis=1, keepdims=True)
    d_pre = g["env"] * d_soft * (gate * (1.0 + pre * (1.0 - gate)))
    d_feat = three_pass(dot_nt, d_pre, embed_pair)
    embed_grad[...] = three_pass_tn(g["feat"], d_pre)
    d_bessel = [d_feat[:, 2 * NSPEC + k : 2 * NSPEC + 1 + k] for k in range(NBES)]
    d_vector[...] = place_columns(vector_pull(g, d_bessel, d_harm, d_envelope), 0)


def outer_sum(split_left, chosen, *refs):
    count = len(CHUNKS)
    extra = len(refs) > 4 * count + 8
    kinds = 3 if extra else 2
    sources = [
        [refs[(kinds * side + i) * count : (kinds * side + i + 1) * count] for i in range(kinds)]
        for side in range(2)
    ]
    rest = refs[2 * kinds * count :]
    outs = [Stored(rest[i], rest[kinds + i], rest[-1].at[i]) for i in range(kinds)]
    buffers = rest[2 * kinds : 3 * kinds]
    semaphores = rest[-2]

    def copies(side):
        for i in range(kinds):
            start = 0
            for k, source in enumerate(sources[side][i]):
                rows, columns = source.shape[0], buffers[i].shape[1]
                yield pltpu.make_async_copy(
                    source.at[:, pl.ds(0, columns)],
                    buffers[i].at[pl.ds(start, rows)],
                    semaphores.at[i * count + k],
                )
                start += rows

    for side in range(2):

        @pl.when(chosen[0] == side)
        def _(side=side):
            for copy in copies(side):
                copy.start()

    for copy in copies(0):
        copy.wait()
    left_high, left_low = split_two(buffers[0][...])
    right_high, right_low = split_two(buffers[1][...])
    left = jnp.concatenate([left_high, left_low, left_high], axis=0)
    right = jnp.concatenate([right_high, right_high, right_low], axis=0)
    if split_left:
        half = left.shape[1] // 2
        outs[1][...] = dot_tn(left[:, half:], right)
        outs[0][...] = dot_tn(left[:, :half], right)
    else:
        half = right.shape[1] // 2
        outs[1][...] = dot_tn(left, right[:, half:])
        outs[0][...] = dot_tn(left, right[:, :half])
    if extra:
        right_high, right_low = split_two(buffers[2][...])
        right = jnp.concatenate([right_high, right_high, right_low], axis=0)
        outs[2][...] = dot_tn(left[:, : outs[2].shape[0]], right)
    for out in outs:
        out.copy.wait()


def on_core(body, outs, flops, args, fetched, chosen):
    here = pl.BlockSpec(memory_space=pltpu.VMEM)
    there = pl.BlockSpec(memory_space=pl.ANY)
    pad = 2 * LANES
    tall = [(m.shape[0] + pad - 1) // pad * pad if m.shape[0] > pad else m.shape[0] for m in fetched]
    scratch = [pltpu.VMEM((rows, m.shape[1]), F32) for rows, m in zip(tall, fetched)]
    scratch += [pltpu.VMEM(shape, F32) for shape in outs]
    scratch.append(pltpu.SemaphoreType.DMA((len(fetched),)))
    scratch.append(pltpu.SemaphoreType.DMA((len(outs),)))

    def guarded(flag, *refs):
        @pl.when(flag[0] == 1)
        def _():
            small, rest = refs[: len(args)], refs[len(args) :]
            sources, rest = rest[: len(fetched)], rest[len(fetched) :]
            targets, rest = rest[: len(outs)], rest[len(outs) :]
            buffers, rest = rest[: len(fetched)], rest[len(fetched) :]
            kept, (arrivals, departures) = rest[: len(outs)], rest[len(outs) :]
            inputs = [Fetched(s, b, arrivals.at[i]) for i, (s, b) in enumerate(zip(sources, buffers))]
            outputs = [Stored(t, b, departures.at[i]) for i, (t, b) in enumerate(zip(targets, kept))]
            body(*small, *inputs, *outputs)
            for output in outputs:
                output.copy.wait()

    return pl.pallas_call(
        guarded,
        out_shape=tuple(jax.ShapeDtypeStruct(shape, F32) for shape in outs),
        in_specs=[pl.BlockSpec(memory_space=pltpu.SMEM)] + [here] * len(args) + [there] * len(fetched),
        out_specs=tuple(there for _ in outs),
        scratch_shapes=scratch,
        compiler_params=pltpu.CompilerParams(vmem_limit_bytes=60 * 2**20),
        cost_estimate=pl.CostEstimate(flops=flops, bytes_accessed=16 * 2**20, transcendentals=0),
    )(chosen, *args, *fetched)


def outer_call(split_left, outs, widths, flops, chosen, first, second):
    there = pl.BlockSpec(memory_space=pl.ANY)
    args = [array for side in (first, second) for factor in side for array in factor]
    return pl.pallas_call(
        partial(outer_sum, split_left),
        out_shape=tuple(jax.ShapeDtypeStruct(shape, F32) for shape in outs),
        in_specs=[pl.BlockSpec(memory_space=pltpu.SMEM)] + [there] * len(args),
        out_specs=tuple(there for _ in outs),
        scratch_shapes=[pltpu.VMEM(shape, F32) for shape in outs]
        + [pltpu.VMEM((sum(CHUNKS), w), F32) for w in widths]
        + [
            pltpu.SemaphoreType.DMA((len(widths) * len(CHUNKS),)),
            pltpu.SemaphoreType.DMA((len(outs),)),
        ],
        compiler_params=pltpu.CompilerParams(vmem_limit_bytes=60 * 2**20),
        cost_estimate=pl.CostEstimate(flops=flops, bytes_accessed=16 * 2**20, transcendentals=0),
    )(chosen, *args)


def gather_blocks(value):
    count = lax.axis_size("edge")
    if count & (count - 1) or count > 8:
        return lax.all_gather(value, "edge", axis=0)
    index = lax.axis_index("edge")
    out = value[None]
    step = 1
    while step < count:
        got = lax.ppermute(out, "edge", [(i, i ^ step) for i in range(count)])
        low = (index // step) % 2 == 0
        out = jnp.where(low, jnp.concatenate([out, got]), jnp.concatenate([got, out]))
        step *= 2
    return out


def prefix_in_rows(flags):
    rows, length = flags.shape
    pieces = flags.reshape(rows, length // LANES, LANES)
    upper = (jnp.arange(LANES)[:, None] <= jnp.arange(LANES)[None, :]).astype(F32)
    inner = jnp.einsum("rkl,lm->rkm", pieces, upper, precision=HIGHEST)
    totals = inner[:, :, -1]
    count = length // LANES
    before = (jnp.arange(count)[:, None] < jnp.arange(count)[None, :]).astype(F32)
    offsets = jnp.dot(totals, before, precision=HIGHEST)
    return (inner + offsets[:, :, None]).reshape(rows, length)


def pack_edges(atoms, vectors, species, centres, mask, structures, out):
    count = centres.shape[1]
    for b in range(centres.shape[0]):
        span = slice(b * count, (b + 1) * count)
        vector = vectors[b]
        out[0:3, span] = vector
        out[3:5, span] = species[b].astype(F32)
        out[5:6, span] = (centres[b : b + 1, :] + b * atoms).astype(F32)
        squares = jnp.maximum(jnp.sum(vector * vector, axis=0, keepdims=True), 0.25)
        near = jnp.where(jnp.sqrt(squares) / CUTOFF < 1.0, 1.0, 0.0)
        out[6:7, span] = jnp.where(mask[b : b + 1, :] > 0, near, 0.0)
        out[7:8, span] = (structures[b : b + 1, :] + b * STRUCTS).astype(F32)


def plan_edges(edge_vectors, edge_species, centres, edge_mask, structures):
    batch_count, _, edge_count = edge_vectors.shape
    blocks = lax.axis_size("edge")
    block = lax.axis_index("edge")
    core = lax.axis_index("mp")
    atoms = blocks * ATOM_DEV
    per_block = batch_count * edge_count
    raw = pl.pallas_call(
        partial(pack_edges, atoms), out_shape=jax.ShapeDtypeStruct((8, per_block), F32)
    )(edge_vectors, edge_species, centres, edge_mask, structures)
    gathered = gather_blocks(raw)
    keys = gathered[:, 5].reshape(blocks, batch_count, edge_count)
    alive = gathered[:, 6].reshape(blocks, batch_count, edge_count)
    local = keys - (jnp.arange(batch_count) * atoms)[None, :, None].astype(F32)
    degree = jnp.sum(
        jnp.where(
            local.transpose(1, 0, 2).reshape(batch_count, 1, -1)
            == jnp.arange(atoms, dtype=F32)[None, :, None],
            alive.transpose(1, 0, 2).reshape(batch_count, 1, -1),
            0.0,
        ),
        axis=2,
    )
    spans = batch_count * ATOM_DEV
    degree = degree.reshape(batch_count, blocks, ATOM_DEV).transpose(1, 0, 2).reshape(blocks, spans)
    upper = (jnp.arange(spans)[:, None] <= jnp.arange(spans)[None, :]).astype(F32)
    upto = jnp.dot(degree, upper, precision=HIGHEST)
    start = jnp.zeros((blocks, 1), F32)
    starts = [start]
    for size in CHUNKS:
        for _ in range(2):
            start = jnp.max(jnp.where(upto <= start + size, jnp.maximum(upto, start), start), axis=1, keepdims=True)
            starts.append(start)
    fits = jnp.all(starts[-1] >= upto[:, -1:])
    starts = jnp.concatenate(starts[:-1], axis=1)
    own_before = (upto - degree)[block]
    bin_of = jnp.sum((own_before[:, None] >= starts[block][None, 1:]).astype(F32), axis=1)
    padded = jnp.concatenate([jnp.zeros_like(gathered[:1]), gathered, jnp.zeros_like(gathered[:1])])
    window = lax.dynamic_slice_in_dim(padded, block, 3, 0)
    flat = window.transpose(1, 0, 2).reshape(8, 3 * per_block)
    position = jnp.arange(3 * per_block)
    batch_flat = (position % per_block) // edge_count
    spot = flat[5] - (batch_flat * atoms + block * ATOM_DEV).astype(F32)
    mine = (spot >= 0) & (spot < ATOM_DEV) & (flat[6] > 0.5)
    slot = jnp.where(mine, spot + (batch_flat * ATOM_DEV).astype(F32), -1.0)
    chosen = jnp.sum(
        jnp.where(jnp.arange(spans, dtype=F32)[:, None] == slot[None, :], bin_of[:, None], 0.0), axis=0
    )
    wanted = 2 * jnp.arange(len(CHUNKS)) + core
    picked = (chosen[None, :] == wanted[:, None].astype(F32)) & mine[None, :]
    rank = prefix_in_rows(picked.astype(F32)) - 1.0
    offsets = [sum(CHUNKS[:k]) for k in range(len(CHUNKS))]
    place = jnp.sum(
        jnp.where(picked, rank + jnp.array(offsets, F32)[:, None], 0.0), axis=0
    ) - (1.0 - jnp.sum(picked.astype(F32), axis=0))
    total = sum(CHUNKS)
    hot = (place[None, :] == jnp.arange(total, dtype=F32)[:, None]).astype(F32)
    edges = lax.dot_general(hot, flat, (((1,), (1,)), ((), ())), precision=HIGHEST)
    return fits, edges, place


def tied(first, *others):
    return lax.optimization_barrier((first, others))[0]


def hop(value, distance):
    return lax.ppermute(value, "edge", [(i, i ^ distance) for i in range(8)])


def halves(value, second):
    half = value.shape[0] // 2
    kept = lax.dynamic_slice_in_dim(value, second * half, half, 0)
    return kept, lax.dynamic_slice_in_dim(value, (1 - second) * half, half, 0)


def joined(kept, got, second):
    return jnp.where(second == 0, jnp.concatenate([kept, got]), jnp.concatenate([got, kept]))


def sum_piece(value, outer_hop, inner_hop):
    index = lax.axis_index("edge")
    seconds = {1: index % 2, 2: ((index // 2) ^ (index // 4)) % 2}
    kept, given = halves(value, seconds[outer_hop])
    kept, given = halves(kept + hop(given, outer_hop), seconds[inner_hop])
    part = kept + hop(given, inner_hop)
    part = part + hop(part, 6)
    part = joined(part, hop(part, inner_hop), seconds[inner_hop])
    half = part.shape[0]
    return [(part, seconds[outer_hop] * half), (hop(part, outer_hop), (1 - seconds[outer_hop]) * half)]


def sum_blocks(matrices, plan):
    if lax.axis_size("edge") != 8:
        return [lax.psum(value, "edge") for value in matrices]
    sums = [jnp.zeros_like(value) for value in matrices]
    for which, first, rows, outer_hop, inner_hop in plan:
        piece = lax.slice_in_dim(matrices[which], first, first + rows, axis=0)
        for part, start in sum_piece(piece, outer_hop, inner_hop):
            sums[which] = lax.dynamic_update_slice_in_dim(sums[which], part, first + start, 0)
    return sums


def fast_device(edges, place, others, args):
    (
        edge_vectors, edge_species, centres, edge_mask, structures, energy_cot, embed_in,
        section_head, env_weight, mix_weight, w_in, w_out, read_weight,
    ) = args
    is_first = lax.axis_index("section") == 0
    core = lax.axis_index("mp")
    width = section_head.shape[1]
    half = section_head.shape[2]
    batch_count, _, edge_count = edge_vectors.shape
    chan_count = mix_weight.shape[1]
    gap = LANES - chan_count
    read_left, read_right = read_weight[:half], read_weight[half:]
    read_line = jnp.where(
        core == 0,
        jnp.concatenate([read_left, read_right]),
        jnp.concatenate([read_right, read_left]),
    )[None]
    cot_row = jnp.pad(energy_cot.reshape(1, -1), ((0, 0), (0, LANES - energy_cot.size)))
    lead_flag = jnp.full((8, LANES), 1.0, F32) * (core == 0).astype(F32)
    mix = jnp.pad(mix_weight, ((0, 0), (0, gap), (0, gap)))
    env_w = jnp.pad(env_weight[0], ((0, 0), (0, gap)))
    env_wt = env_w.T
    heads, ins, outs_w = (section_head[0], others[0]), (w_in[0], others[1]), (w_out[0], others[2])
    count = len(CHUNKS)
    offsets = [sum(CHUNKS[:k]) for k in range(count)]
    rows = [edges[o : o + m, 5].reshape(1, -1) for o, m in zip(offsets, CHUNKS)]
    layer_width = width + 2 * LANES

    first_flag = jnp.full((1,), 1, jnp.int32) * is_first.astype(jnp.int32)
    second_flag = 1 - first_flag
    saved, moved = [], []
    for k, m in enumerate(CHUNKS):
        outs = [(m, width + LANES), (m, width), (m, layer_width), (m, width), (m, width)]
        work = 12 * m * width * (3 * width + 384)
        result = on_core(
            partial(first_forward, offsets[k]), outs, work,
            (edges, rows[k], lead_flag, embed_in), (*heads, env_w, *ins, *outs_w), first_flag,
        )
        moved.append(shifted(result[0], "section", 1))
        saved.append(result[1:])
    seconds, returned, firsts = [], [], []
    for k, m in enumerate(CHUNKS):
        outs = [
            (m, width + LANES), (m, layer_width), (m, width), (m, width), (m, width),
            (m, width), (m, width), (m, LANES), (8, width), (3, LANES, LANES), (8, LANES),
        ]
        work = 18 * m * width * (3 * width + 384)
        seconds.append(
            on_core(
                partial(second_both, offsets[k]), outs, work,
                (edges, rows[k], mix, read_line, cot_row),
                (moved[k], env_w, *ins, *outs_w, *heads, env_wt), second_flag,
            )
        )
    outer_work = 6 * sum(CHUNKS) * width * width
    for k, m in enumerate(CHUNKS):
        back = seconds[k][0] if k == 0 else tied(seconds[k][0], firsts[k - 1][0])
        returned.append(shifted(back, "section", -1))
        arrived = returned[k]
        if k == count - 1:
            out_own, out_other = outer_call(
                True, [(half, width)] * 2, (width, width), outer_work, second_flag,
                ([s[3] for s in saved], returned),
                ([s[3] for s in seconds], [s[4] for s in seconds]),
            )
            arrived = tied(arrived, out_other)
        outs = [(m, LANES), (m, width), (m, width), (m, LANES), (16, width)]
        work = 9 * m * width * (3 * width + 384)
        firsts.append(
            on_core(
                partial(first_backward, offsets[k]), outs, work,
                (edges, rows[k], lead_flag, embed_in),
                (saved[k][1], env_w, arrived, *outs_w, saved[k][2], *ins, env_wt, *heads), first_flag,
            )
        )
    grad_out = out_own + other_core(out_other)
    in_own, in_other, grad_env = outer_call(
        False, [(layer_width, half)] * 2 + [(width, LANES)], (layer_width, width, LANES), outer_work,
        second_flag,
        ([s[1] for s in saved], [f[2] for f in firsts], [f[3] for f in firsts]),
        ([s[1] for s in seconds], [s[2] for s in seconds], [s[7] for s in seconds]),
    )
    grad_in = in_own + other_core(in_other)
    head_own, head_other = outer_call(
        False, [(width, half)] * 2, (width, width), outer_work, tied(second_flag, in_other),
        ([s[0] for s in saved], [f[1] for f in firsts]),
        ([s[5] for s in seconds], [s[6] for s in seconds]),
    )
    none = jnp.zeros((), F32)
    read_sum = sum(s[8][0] for s in seconds)
    read_sum = jnp.where(
        core == 0, read_sum, jnp.concatenate([read_sum[half:], read_sum[:half]])
    )
    mix_sum = sum(s[9] for s in seconds)[:, :chan_count, :chan_count].reshape(-1, width)
    energy_sum = sum(s[10][0] for s in seconds)
    embed_sum = sum(f[4] for f in firsts)
    small_second = jnp.concatenate(
        [read_sum[None], jnp.pad(energy_sum, (0, width - LANES))[None], mix_sum]
    )
    small_second = jnp.pad(small_second, ((0, 16 - small_second.shape[0]), (0, 0)))
    small = jnp.concatenate(
        [jnp.where(is_first, embed_sum, none), jnp.where(is_first, none, small_second)]
    )
    small = small + lax.ppermute(small, "section", [(0, 1), (1, 0)])
    small = jnp.concatenate([small, grad_env[:, :chan_count].reshape(-1, width)]).reshape(-1, half)
    head_own = jnp.concatenate([head_own, small])
    grad_head = head_own + other_core(jnp.concatenate([head_other, small]))
    grad_out, grad_in, grad_head = sum_blocks(
        [grad_out, grad_in, grad_head],
        [
            (0, 0, 512, 2, 1), (1, 0, 640, 1, 2), (1, 640, 640, 1, 2), (2, 0, 608, 2, 1),
            (2, 608, 608, 1, 2),
        ],
    )
    small = grad_head[width:].reshape(-1, width)
    grad_head = grad_head[:width]
    grad_embed, grad_read = small[:16], small[16]
    energies = small[17, : energy_cot.size].reshape(energy_cot.shape)
    grad_mix = small[18 : 18 + mix_sum.shape[0]].reshape(mix_weight.shape)
    grad_env = small[32:].reshape(width, chan_count)

    d_vectors = jnp.concatenate([f[0][:, :8] for f in firsts])
    total = sum(CHUNKS)
    hot = (place[None, :] == jnp.arange(total, dtype=F32)[:, None]).astype(F32)
    spread = lax.dot_general(d_vectors, hot, (((0,), (0,)), ((), ())), precision=HIGHEST)[:3]
    spread = jnp.where(is_first, spread, none)
    spread = spread + other_core(spread)
    per_block = batch_count * edge_count
    to_left, kept, to_right = (spread[:, i * per_block : (i + 1) * per_block] for i in range(3))
    forces = kept + shifted(to_right, "edge", 1) + shifted(to_left, "edge", -1)
    forces = jnp.where(is_first, forces, shifted(forces, "section", 1))
    forces = -forces.reshape(3, batch_count, edge_count).transpose(1, 0, 2)
    return (
        energies, forces, grad_embed, grad_head[None], grad_env[None], grad_mix,
        grad_in[None, : w_in.shape[1]], grad_out[None], grad_read,
    )


def per_device(*args):
    section_head, w_in, w_out = args[7], args[10], args[11]
    others = tuple(other_core(m[0]) for m in (section_head, w_in, w_out))
    fits, edges, place = plan_edges(*args[:5])
    results = fast_device(edges, place, others, args)

    def again(state):
        rest, _ = state
        held, rest = lax.optimization_barrier((args, rest))
        return rest - 1, general_device(*held)

    overflow = 1 - fits.astype(jnp.int32)
    return lax.while_loop(lambda state: state[0] > 0, again, (overflow, results))[1]


def solution(mesh):
    placed = (
        P(None, None, "edge"),
        P(None, None, "edge"),
        P(None, "edge"),
        P(None, "edge"),
        P(None, "edge"),
        P(),
        P(),
        P("section", None, "mp"),
        P("section", None, None),
        P(),
        P("section", None, "mp"),
        P("section", "mp", None),
        P(),
    )
    return jax.shard_map(
        per_device,
        mesh=mesh,
        in_specs=placed,
        out_specs=(
            P(),
            P(None, None, "edge"),
            P(),
            P("section", None, "mp"),
            P("section", None, None),
            P(),
            P("section", None, "mp"),
            P("section", "mp", None),
            P(),
        ),
        check_vma=False,
    )
```

```python
from functools import partial

import jax
import jax.numpy as jnp
from jax import lax
from jax.experimental import pallas as pl
from jax.experimental.pallas import tpu as pltpu
from jax.sharding import PartitionSpec as P

NBES = 8
NSPEC = 4
ATOM_DEV = 40
STRUCTS = 16


CUTOFF = 5.0
ENV_SCALE = 0.25
HIGHEST = lax.Precision.HIGHEST
ROOT_THREE = 1.7320508075688772
ROOT_FIVE = 2.23606797749979
ROOT_FIFTEEN = 3.872983346207417


def extended(block, sides, width):
    for axis, dim in sides:
        count = lax.axis_size(axis)
        forward = [(i, i + 1) for i in range(count - 1)]
        backward = [(target, source) for source, target in forward]
        low = lax.ppermute(
            lax.slice_in_dim(block, block.shape[dim] - width, None, axis=dim), axis, forward
        )
        high = lax.ppermute(lax.slice_in_dim(block, 0, width, axis=dim), axis, backward)
        block = jnp.concatenate([low, block, high], axis=dim)
    return block


def shifted(value, axis, steps):
    count = lax.axis_size(axis)
    first, last = (max(0, -steps), min(count, count - steps))
    return lax.ppermute(value, axis, [(source, source + steps) for source in range(first, last)])


def other_core(value):
    return lax.ppermute(value, "mp", [(0, 1), (1, 0)])


def ring_sum(values):
    count = lax.axis_size("edge")

    def step(_, state):
        moving, total = state
        moving = tuple(
            lax.ppermute(v, "edge", [(i, (i + 1) % count) for i in range(count)]) for v in moving
        )
        return moving, tuple(t + v for t, v in zip(total, moving))

    return lax.fori_loop(0, count - 1, step, (tuple(values), tuple(values)))[1]


def matmul(left, right):
    return jnp.dot(left, right, precision=HIGHEST, preferred_element_type=jnp.float32)


def geometry(vectors, edge_live):
    squares = jnp.maximum(jnp.sum(vectors * vectors, axis=0), 0.25)
    length = jnp.sqrt(squares)
    unit_x = vectors[0] / length
    unit_y = vectors[1] / length
    unit_z = vectors[2] / length
    edge_ratio = jnp.minimum(length / CUTOFF, 1.0)
    envelope = (
        1.0 - 28.0 * edge_ratio**6 + 48.0 * edge_ratio**7 - 21.0 * edge_ratio**8
    ) * edge_live
    orders = jnp.arange(1, NBES + 1).astype(jnp.float32)
    bessel = (
        jnp.sqrt(2.0 / CUTOFF)
        * jnp.sin(orders[None, :] * (jnp.pi / CUTOFF) * length[:, None])
        / length[:, None]
    )
    harmonics = jnp.stack(
        [
            jnp.ones_like(unit_x),
            ROOT_THREE * unit_x,
            ROOT_THREE * unit_y,
            ROOT_THREE * unit_z,
            ROOT_FIFTEEN * unit_x * unit_y,
            ROOT_FIFTEEN * unit_y * unit_z,
            0.5 * ROOT_FIVE * (3.0 * unit_z * unit_z - 1.0),
            ROOT_FIFTEEN * unit_x * unit_z,
            0.5 * ROOT_FIFTEEN * (unit_x * unit_x - unit_y * unit_y),
        ],
        axis=1,
    )
    return (harmonics, envelope, bessel)


def couple(edge_tensor, env_flat, mix_weight):
    chan_count = mix_weight.shape[1]
    own_tensor = edge_tensor.reshape(-1, 9, chan_count)
    env_tensor = env_flat.reshape(-1, 9, chan_count)
    paired = own_tensor * env_tensor
    scalars = jnp.concatenate(
        [paired[:, 0], jnp.sum(paired[:, 1:4], axis=1), jnp.sum(paired[:, 4:9], axis=1)], axis=1
    )
    coupled = own_tensor * env_tensor[:, 0:1] + own_tensor[:, 0:1] * env_tensor
    order_zero = jnp.einsum("emc,cd->emd", coupled[:, 0:1], mix_weight[0], precision=HIGHEST)
    order_one = jnp.einsum("emc,cd->emd", coupled[:, 1:4], mix_weight[1], precision=HIGHEST)
    order_two = jnp.einsum("emc,cd->emd", coupled[:, 4:9], mix_weight[2], precision=HIGHEST)
    updated = jnp.concatenate([order_zero, order_one, order_two], axis=1)
    return (scalars, updated.reshape(-1, 9 * chan_count))


def front(bessel, envelope, embed_in, head_local, kinds_hot):
    features = jnp.concatenate([kinds_hot, bessel], axis=1)
    return envelope[:, None] * matmul(jax.nn.silu(matmul(features, embed_in)), head_local)


def contribute(latent_full, harmonics, envelope, env_local, centre_hot):
    weight = matmul(latent_full, env_local)
    contribution = (
        (ENV_SCALE * envelope)[:, None, None] * harmonics[:, :, None] * weight[:, None, :]
    )
    flat_terms = contribution.reshape(weight.shape[0], -1)
    return (weight, matmul(centre_hot.T, flat_terms))


def tensor_step(tensor_full, env_window, weight, harmonics, mix_weight, centre_hot, is_first):
    start_tensor = (harmonics[:, :, None] * weight[:, None, :]).reshape(weight.shape[0], -1)
    edge_tensor = jnp.where(is_first, start_tensor, tensor_full)
    env_flat = matmul(centre_hot, env_window)
    return couple(edge_tensor, env_flat, mix_weight)


def perceptron(latent_full, scalars, in_local, out_local):
    hidden = jax.nn.silu(matmul(jnp.concatenate([latent_full, scalars], axis=1), in_local))
    return matmul(hidden, out_local)


def readout(latent_full, envelope, head_local, read_half):
    return envelope * matmul(jax.nn.silu(matmul(latent_full, head_local)), read_half)


def general_device(
    edge_vectors,
    edge_species,
    centres,
    edge_mask,
    structures,
    energy_cot,
    embed_in,
    section_head,
    env_weight,
    mix_weight,
    w_in,
    w_out,
    read_weight,
):
    section_index = lax.axis_index("section")
    core_index = lax.axis_index("mp")
    edge_index = lax.axis_index("edge")
    is_first = section_index == 0
    last_flag = (section_index == 1).astype(jnp.float32)
    batch_count = edge_vectors.shape[0]
    shard_width = w_out.shape[1]
    tensor_cols = 9 * env_weight.shape[2]
    tensor_half = tensor_cols // 2
    atoms_dev = ATOM_DEV
    head_local = section_head[0]
    env_local = env_weight[0]
    in_local = w_in[0]
    out_local = w_out[0]
    read_half = lax.dynamic_slice_in_dim(read_weight, core_index * shard_width, shard_width, 0)
    core_lead = (core_index == 0).astype(jnp.float32)
    edge_count = edge_vectors.shape[2]
    centre_slots = jnp.arange(3 * atoms_dev)
    labels = jnp.arange(STRUCTS)
    species_range = jnp.arange(NSPEC)
    batch_range = jnp.arange(batch_count)

    def reduce_rims(pieces):
        widened = extended(pieces, (("edge", 0),), atoms_dev)
        return (
            widened[:atoms_dev] + widened[2 * atoms_dev : 3 * atoms_dev] + widened[4 * atoms_dev :]
        )

    def window_rows(totals):
        return extended(totals, (("edge", 0),), atoms_dev)

    def collect(partial_rows):
        width = partial_rows.shape[1] // 2
        own = lax.dynamic_slice_in_dim(partial_rows, core_index * width, width, 1)
        return own + other_core(lax.dynamic_slice_in_dim(partial_rows, (1 - core_index) * width, width, 1))

    def both_halves(half):
        other = other_core(half)
        return jnp.where(
            core_index == 0,
            jnp.concatenate([half, other], axis=1),
            jnp.concatenate([other, half], axis=1),
        )

    def batch_data(batch_index):
        vectors = lax.dynamic_index_in_dim(edge_vectors, batch_index, 0, keepdims=False)
        kind_ids = lax.dynamic_index_in_dim(edge_species, batch_index, 0, keepdims=False)
        owners = lax.dynamic_index_in_dim(centres, batch_index, 0, keepdims=False)
        edge_live = lax.dynamic_index_in_dim(edge_mask, batch_index, 0, keepdims=False).astype(
            jnp.float32
        )
        groups = lax.dynamic_index_in_dim(structures, batch_index, 0, keepdims=False)
        kinds_hot = jnp.concatenate(
            [
                kind_ids[0][:, None] == species_range[None, :],
                kind_ids[1][:, None] == species_range[None, :],
            ],
            axis=1,
        ).astype(jnp.float32)
        local_slot = owners - (edge_index - 1) * atoms_dev
        centre_hot = (local_slot[:, None] == centre_slots[None, :]).astype(jnp.float32)
        group_hot = (groups[:, None] == labels[None, :]).astype(jnp.float32)
        return (vectors, edge_live, kinds_hot, centre_hot, group_hot)

    recv_latent = jnp.zeros((edge_count, shard_width), jnp.float32)
    recv_tensor = jnp.zeros((edge_count, tensor_half), jnp.float32)
    energies = jnp.zeros((batch_count, STRUCTS), jnp.float32)
    kept_state = []
    for step_index in range(batch_count + 1):
        batch_raw = step_index - section_index
        batch_index = jnp.clip(batch_raw, 0, batch_count - 1)
        is_valid = ((batch_raw >= 0) & (batch_raw < batch_count)).astype(jnp.float32)
        vectors, edge_live, kinds_hot, centre_hot, group_hot = batch_data(batch_index)
        harmonics, envelope, bessel = geometry(vectors, edge_live)
        latent_half = lax.cond(
            is_first,
            lambda: front(bessel, envelope, embed_in, head_local, kinds_hot),
            lambda: recv_latent,
        )
        latent_full, tensor_full = (
            both_halves(latent_half),
            both_halves(recv_tensor),
        )
        weight, part_sums = contribute(latent_full, harmonics, envelope, env_local, centre_hot)
        env_window = window_rows(reduce_rims(part_sums))
        scalars, updated = tensor_step(
            tensor_full, env_window, weight, harmonics, mix_weight, centre_hot, is_first
        )
        branch_out = perceptron(latent_full, scalars, in_local, out_local)
        summed = collect(branch_out)
        tensor_own = lax.dynamic_slice_in_dim(updated, core_index * tensor_half, tensor_half, 1)
        next_half = latent_half + summed
        recv_latent, recv_tensor = shifted((next_half, tensor_own), "section", 1)
        next_full = both_halves(next_half)
        edge_energy = readout(next_full, envelope, head_local, read_half)
        batch_slot = (batch_range == batch_index).astype(jnp.float32) * is_valid * last_flag
        energies = (
            energies
            + batch_slot[:, None] * jnp.dot(edge_energy, group_hot, precision=HIGHEST)[None, :]
        )
        kept_state.append((latent_full, tensor_full, env_window, next_full))
    kept_latent = jnp.stack([entry[0] for entry in kept_state])
    kept_tensor = jnp.stack([entry[1] for entry in kept_state])
    kept_window = jnp.stack([entry[2] for entry in kept_state])
    kept_next = jnp.stack([entry[3] for entry in kept_state])
    grad_head = jnp.zeros_like(head_local)
    grad_env = jnp.zeros_like(env_local)
    grad_in = jnp.zeros_like(in_local)
    grad_out = jnp.zeros_like(out_local)
    grad_mix = jnp.zeros_like(mix_weight)
    grad_embed = jnp.zeros_like(embed_in)
    grad_read = jnp.zeros_like(read_half)
    forces = jnp.zeros((batch_count, 3, edge_count), jnp.float32)
    recv_grad = jnp.zeros((edge_count, shard_width), jnp.float32)
    recv_tgrad = jnp.zeros((edge_count, tensor_half), jnp.float32)
    for step_index in range(batch_count + 1):
        batch_raw = step_index - 1 + section_index
        batch_index = jnp.clip(batch_raw, 0, batch_count - 1)
        is_valid = ((batch_raw >= 0) & (batch_raw < batch_count)).astype(jnp.float32)
        saved_index = jnp.clip(batch_raw + section_index, 0, batch_count)
        latent_full = lax.dynamic_index_in_dim(kept_latent, saved_index, 0, keepdims=False)
        tensor_full = lax.dynamic_index_in_dim(kept_tensor, saved_index, 0, keepdims=False)
        env_window = lax.dynamic_index_in_dim(kept_window, saved_index, 0, keepdims=False)
        next_full = lax.dynamic_index_in_dim(kept_next, saved_index, 0, keepdims=False)
        vectors, edge_live, kinds_hot, centre_hot, group_hot = batch_data(batch_index)
        (harmonics, envelope, bessel), geometry_pull = jax.vjp(
            partial(geometry, edge_live=edge_live), vectors
        )
        batch_cot = lax.dynamic_index_in_dim(energy_cot, batch_index, 0, keepdims=False)
        energy_rows = jnp.dot(group_hot, batch_cot, precision=HIGHEST) * (is_valid * last_flag)
        _, read_pull = jax.vjp(readout, next_full, envelope, head_local, read_half)
        d_next_read, d_env_read, g_head_read, g_read = read_pull(energy_rows)
        d_next_half = jnp.where(is_first, recv_grad, collect(d_next_read))
        d_out_full, d_updated = (
            both_halves(d_next_half),
            both_halves(recv_tgrad),
        )
        (weight, part_sums), contribute_pull = jax.vjp(
            partial(contribute, centre_hot=centre_hot), latent_full, harmonics, envelope, env_local
        )
        (scalars, updated), tensor_pull = jax.vjp(
            partial(tensor_step, centre_hot=centre_hot, is_first=is_first),
            tensor_full,
            env_window,
            weight,
            harmonics,
            mix_weight,
        )
        _, perceptron_pull = jax.vjp(perceptron, latent_full, scalars, in_local, out_local)
        d_latent_mlp, d_scalar_part, g_in, g_out = perceptron_pull(d_out_full)
        d_scalars = d_scalar_part + other_core(d_scalar_part)
        d_tensor, d_window, d_weight, d_harm_tensor, g_mix = tensor_pull((d_scalars, d_updated))
        d_parts = window_rows(reduce_rims(d_window))
        d_latent_env, d_harm_env, d_envelope_env, g_env = contribute_pull((d_weight, d_parts))
        d_latent_own = (
            collect(d_latent_mlp)
            + lax.dynamic_slice_in_dim(d_latent_env, core_index * shard_width, shard_width, 1)
            + d_next_half
        )
        d_tensor_own = lax.dynamic_slice_in_dim(d_tensor, core_index * tensor_half, tensor_half, 1)
        recv_grad, recv_tgrad = shifted((d_latent_own, d_tensor_own), "section", -1)

        def front_pull(cotangent):
            _, pull_back = jax.vjp(
                partial(front, kinds_hot=kinds_hot), bessel, envelope, embed_in, head_local
            )
            return pull_back(cotangent)

        def front_none(cotangent):
            return (
                jnp.zeros_like(bessel),
                jnp.zeros_like(envelope),
                jnp.zeros_like(embed_in),
                jnp.zeros_like(head_local),
            )

        d_bessel, d_envelope_front, g_embed, g_head_front = lax.cond(
            is_first, front_pull, front_none, d_latent_own
        )
        d_harmonics = core_lead * (d_harm_tensor + d_harm_env)
        d_envelope = core_lead * d_envelope_env + d_env_read + d_envelope_front
        d_vectors = geometry_pull((d_harmonics, d_envelope, d_bessel))[0]
        batch_slot = (batch_range == batch_index).astype(jnp.float32) * is_valid
        forces = forces + batch_slot[:, None, None] * d_vectors[None]
        grad_head = grad_head + is_valid * (g_head_read + g_head_front)
        grad_env = grad_env + is_valid * g_env
        grad_in = grad_in + is_valid * g_in
        grad_out = grad_out + is_valid * g_out
        grad_mix = grad_mix + is_valid * g_mix
        grad_embed = grad_embed + is_valid * g_embed
        grad_read = grad_read + is_valid * g_read
    grad_head, grad_env, grad_in, grad_out = ring_sum((grad_head, grad_env, grad_in, grad_out))
    read_full = lax.dynamic_update_slice_in_dim(
        jnp.zeros_like(read_weight), grad_read, core_index * shard_width, 0
    )
    chip_sums = [v + other_core(v) for v in (energies, grad_embed, core_lead * grad_mix, read_full, forces)]
    energies, grad_embed, grad_mix, read_full, forces = (
        v + lax.ppermute(v, "section", [(0, 1), (1, 0)]) for v in chip_sums
    )
    energies, grad_embed, grad_mix, read_full = ring_sum((energies, grad_embed, grad_mix, read_full))
    return (
        energies,
        -forces,
        grad_embed,
        grad_head[None],
        grad_env[None],
        grad_mix,
        grad_in[None],
        grad_out[None],
        read_full,
    )


CHUNKS = (128, 192, 160)
PLAN = (
    (0, 0, 256, 2, 1), (0, 256, 256, 1, 2), (1, 0, 640, 1, 2), (1, 640, 640, 1, 2), (2, 0, 608, 2, 1),
    (2, 608, 608, 1, 2),
)
EARLY = (0, 1)
ORDER = (
    0, 2, 4, 5, 2, 1, 2, 4, 3, 1, 5, 0, 4, 3, 2, 5, 1, 3, 4, 2, 5, 3, 0, 5, 3, 4, 2, 1, 5, 0, 3, 4,
)
LANES = 128
F32 = jnp.float32
BF16 = jnp.bfloat16
BESSEL_SCALE = (2.0 / CUTOFF) ** 0.5
ANGLE = 3.141592653589793 / CUTOFF


def dot_nn(left, right):
    return jnp.dot(left, right, preferred_element_type=F32)


def dot_nt(left, right):
    return lax.dot_general(left, right, (((1,), (1,)), ((), ())), preferred_element_type=F32)


def dot_tn(left, right):
    return lax.dot_general(left, right, (((0,), (0,)), ((), ())), preferred_element_type=F32)


def split_two(value):
    high = value.astype(BF16)
    return high, (value - high.astype(F32)).astype(BF16)


def split_three(value):
    high = value.astype(BF16)
    rest = value - high.astype(F32)
    middle = rest.astype(BF16)
    return high, middle, (rest - middle.astype(F32)).astype(BF16)


def six_pass(left, right):
    rows = left.shape[0]
    high, middle, low = split_three(left)
    three = dot_nn(jnp.concatenate([high, middle, low], axis=0), right[0])
    two = dot_nn(jnp.concatenate([high, middle], axis=0), right[1])
    small = three[2 * rows :] + two[rows:] + dot_nn(high, right[2])
    return three[:rows] + (three[rows : 2 * rows] + two[:rows] + small)


def three_pass(dot, left, right):
    rows = left.shape[0]
    high, low = split_two(left)
    both = dot(jnp.concatenate([high, low], axis=0), right[0])
    return both[:rows] + both[rows:] + dot(high, right[1])


def three_pass_tn(left, right):
    left_high, left_low = split_two(left)
    right_high, right_low = split_two(right)
    return dot_tn(
        jnp.concatenate([left_high, left_low, left_high], axis=0),
        jnp.concatenate([right_high, right_high, right_low], axis=0),
    )


def sigmoid(value):
    return 1.0 / (1.0 + jnp.exp(-value))


def order_of(component):
    return 0 if component == 0 else (1 if component < 4 else 2)


def same_sum(same, parts):
    high, middle, low = split_three(jnp.concatenate(parts, axis=1))
    summed = dot_nn(same, high) + (dot_nn(same, middle) + dot_nn(same, low))
    return [summed[:, LANES * m : LANES * (m + 1)] for m in range(len(parts))]


def place_columns(columns, first, width=LANES):
    lane = lax.broadcasted_iota(jnp.int32, (columns[0].shape[0], width), 1)
    out = jnp.zeros((columns[0].shape[0], width), F32)
    for i, column in enumerate(columns):
        out = jnp.where(lane == first + i, column, out)
    return out


def waves(length):
    turn = length * ANGLE - 1.5707963267948966
    square = turn * turn
    even, odd, term_even, term_odd = 1.0, 1.0, 1.0, 1.0
    coefficients_even, coefficients_odd = [], []
    for n in range(1, 9):
        term_even = -term_even / ((2 * n - 1) * (2 * n))
        term_odd = -term_odd / ((2 * n) * (2 * n + 1))
        coefficients_even.append(term_even)
        coefficients_odd.append(term_odd)
    even = jnp.full_like(turn, coefficients_even[-1])
    odd = jnp.full_like(turn, coefficients_odd[-1])
    for n in range(6, -1, -1):
        even = even * square + coefficients_even[n]
        odd = odd * square + coefficients_odd[n]
    sines = {1: even * square + 1.0}
    cosines = {1: -turn * (odd * square + 1.0)}
    for total, left, right in ((2, 1, 1), (3, 2, 1), (4, 2, 2), (5, 4, 1), (6, 4, 2), (7, 4, 3), (8, 4, 4)):
        sines[total] = sines[left] * cosines[right] + cosines[left] * sines[right]
        cosines[total] = cosines[left] * cosines[right] - sines[left] * sines[right]
    return [sines[k] for k in range(1, 9)], [cosines[k] for k in range(1, 9)]


def edge_values(edges, key_row, first, rows, full):
    block = edges[first : first + rows, :]
    vector = [block[:, i : i + 1] for i in range(3)]
    live = block[:, 6:7]
    squares = vector[0] * vector[0] + vector[1] * vector[1] + vector[2] * vector[2]
    length = jnp.sqrt(jnp.maximum(squares, 0.25))
    ux, uy, uz = (v / length for v in vector)
    ratio = jnp.minimum(length / CUTOFF, 1.0)
    second = ratio * ratio
    sixth = second * second * second
    envelope = (1.0 - 28.0 * sixth + 48.0 * (sixth * ratio) - 21.0 * (sixth * second)) * live
    harmonics = [
        jnp.ones_like(ux),
        ROOT_THREE * ux,
        ROOT_THREE * uy,
        ROOT_THREE * uz,
        ROOT_FIFTEEN * ux * uy,
        ROOT_FIFTEEN * uy * uz,
        0.5 * ROOT_FIVE * (3.0 * uz * uz - 1.0),
        ROOT_FIFTEEN * ux * uz,
        0.5 * ROOT_FIFTEEN * (ux * ux - uy * uy),
    ]
    same = jnp.where(block[:, 5:6] == key_row, 1.0, 0.0).astype(BF16)
    g = dict(
        env=envelope, harm=harmonics, same=same, squares=squares, length=length, ratio=ratio,
        unit=(ux, uy, uz), live=live, group=block[:, 7:8],
    )
    if full:
        sines, g["cosines"] = waves(length)
        g["bessel"] = [BESSEL_SCALE * value / length for value in sines]
        lane = lax.broadcasted_iota(jnp.int32, (rows, 16), 1).astype(F32)
        kinds = jnp.where(
            lane < NSPEC,
            jnp.where(block[:, 3:4] == lane, live, 0.0),
            jnp.where(block[:, 4:5] + NSPEC == lane, live, 0.0),
        )
        g["feat"] = kinds + place_columns(g["bessel"], 2 * NSPEC, 16)
    return g


def vector_pull(g, d_bessel, d_harm, d_envelope):
    ux, uy, uz = g["unit"]
    length, ratio = g["length"], g["ratio"]
    dx = ROOT_THREE * d_harm[1] + ROOT_FIFTEEN * (uy * d_harm[4] + uz * d_harm[7] + ux * d_harm[8])
    dy = ROOT_THREE * d_harm[2] + ROOT_FIFTEEN * (ux * d_harm[4] + uz * d_harm[5] - uy * d_harm[8])
    dz = (
        ROOT_THREE * d_harm[3]
        + ROOT_FIFTEEN * (uy * d_harm[5] + ux * d_harm[7])
        + (3.0 * ROOT_FIVE) * uz * d_harm[6]
    )
    left = 1.0 - ratio
    fourth = (ratio * ratio) * (ratio * ratio)
    d_length = (-168.0 / CUTOFF) * (fourth * ratio) * (left * left) * g["live"] * d_envelope
    d_length = d_length - (dx * ux + dy * uy + dz * uz) / length
    for k in range(NBES):
        slope = (BESSEL_SCALE * ANGLE * (k + 1)) * g["cosines"][k] - g["bessel"][k]
        d_length = d_length + d_bessel[k] * (slope / length)
    bound = jnp.where(g["squares"] > 0.25, 1.0, jnp.where(g["squares"] == 0.25, 0.5, 0.0))
    d_length = d_length * bound
    return [d / length + d_length * u for d, u in ((dx, ux), (dy, uy), (dz, uz))]


def env_terms(g, weight):
    scaled = ENV_SCALE * g["env"] * weight
    return same_sum(g["same"], [y * scaled for y in g["harm"]])


def pack_scalars(tensor, env):
    sums = [tensor[0] * env[0], tensor[1] * env[1], tensor[4] * env[4]]
    for m in (2, 3):
        sums[1] = sums[1] + tensor[m] * env[m]
    for m in (5, 6, 7, 8):
        sums[2] = sums[2] + tensor[m] * env[m]
    return jnp.concatenate([sums[0] + pltpu.roll(sums[1], 64, 1), sums[2]], axis=1)


def unpack_scalars(packed):
    first = packed[:, :LANES]
    return [first, pltpu.roll(first, 64, 1), packed[:, LANES:]]


def swap_order(lead, left, right):
    return jnp.where(lead, left, right), jnp.where(lead, right, left)


def env_pull(g, weight, d_env):
    d_terms = same_sum(g["same"], d_env)
    d_weight, d_harm, inner = None, [], None
    for m in range(9):
        part = g["harm"][m] * d_terms[m]
        d_weight = part if m == 0 else d_weight + part
        d_harm.append(jnp.sum(weight * d_terms[m], axis=1, keepdims=True))
        step = g["harm"][m] * d_harm[m]
        inner = step if m == 0 else inner + step
    scale = ENV_SCALE * g["env"]
    return scale * d_weight, [scale * d for d in d_harm], ENV_SCALE * inner


class Fetched:
    def __init__(self, source, buffer, semaphore):
        rows = source.shape[0]
        self.buffer, self.shape = buffer, buffer.shape
        target = buffer if rows == buffer.shape[0] else buffer.at[pl.ds(0, rows)]
        self.copy = pltpu.make_async_copy(source, target, semaphore)
        self.copy.start()
        self.arrived, self.pieces = False, {}
        if rows < buffer.shape[0]:
            buffer[rows:, :] = jnp.zeros((buffer.shape[0] - rows, buffer.shape[1]), F32)

    def __getitem__(self, where):
        if not self.arrived:
            self.copy.wait()
            self.arrived = True
        return self.buffer[where]

    def split(self, parts):
        if parts not in self.pieces:
            value = self[...]
            self.pieces[parts] = split_three(value) if parts == 3 else split_two(value)
        return self.pieces[parts]


class Stored:
    def __init__(self, target, buffer, semaphore):
        self.target, self.buffer, self.semaphore = target, buffer, semaphore
        self.shape, self.copy = buffer.shape, None

    def __setitem__(self, where, value):
        self.buffer[where] = value
        if where is Ellipsis:
            self.send()

    def __getitem__(self, where):
        return self.buffer[where]

    def send(self):
        self.copy = pltpu.make_async_copy(self.buffer, self.target, self.semaphore)
        self.copy.start()


def forward_pair(value, own, other):
    return [six_pass(value, own.split(3)), six_pass(value, other.split(3))]


def backward_pair(value, own, other, parts):
    return [three_pass(dot_nt, value, own.split(parts)), three_pass(dot_nt, value, other.split(parts))]


def first_forward(
    first, edges, key_row, lead_flag, embed,
    head_o, head_x, env_w, in_o, in_x, out_o, out_x,
    sent, soft_out, layer_in, slope_out, hidden,
):
    rows = sent.shape[0]
    lead = lead_flag[0:1, 0:1] > 0.5
    g = edge_values(edges, key_row[...], first, rows, True)
    pre = six_pass(g["feat"], split_three(embed[...]))
    soft = pre * sigmoid(pre)
    soft_out[...] = soft
    own, other = forward_pair(soft, head_o, head_x)
    latent = g["env"] * jnp.concatenate(swap_order(lead, own, other), axis=1)
    weight = six_pass(latent, env_w.split(3))
    env = env_terms(g, weight)
    scalars = pack_scalars([y * weight for y in g["harm"]], env)
    full = jnp.concatenate([latent, scalars], axis=1)
    layer_in[...] = full
    pre = jnp.concatenate(forward_pair(full, in_o, in_x), axis=1)
    gate = sigmoid(pre)
    slope_out[...] = gate * (1.0 + pre * (1.0 - gate))
    hid = pre * gate
    hidden[...] = hid
    half = hid.shape[1] // 2
    width = latent.shape[1]
    sent[:, :width] = (
        latent + six_pass(hid[:, :half], out_o.split(3)) + six_pass(hid[:, half:], out_x.split(3))
    )
    sent[:, width:] = weight
    sent.send()


def second_both(
    first, edges, key_row, mix, read, cot_row,
    arrived, env_w, in_o, in_x, out_o, out_x, head_o, head_x, env_wt,
    back, layer_in, d_pre_hidden, hidden, d_latent_out, latent_out, d_pre_read, d_weight_out,
    read_grad, mix_grad, energy_out,
):
    rows = back.shape[0]
    width = arrived.shape[1] - LANES
    half = width // 2
    g = edge_values(edges, key_row[...], first, rows, False)
    lane = lax.broadcasted_iota(jnp.int32, (rows, LANES), 1).astype(F32)
    group_hot = jnp.where(g["group"] == lane, g["live"], 0.0)
    cot = jnp.sum(group_hot * cot_row[...], axis=1, keepdims=True)
    mixes = [split_three(mix[i]) for i in range(3)]
    latent = arrived[:, :width]
    weight_first = arrived[:, width:]
    env_first = env_terms(g, weight_first)
    start = [y * weight_first for y in g["harm"]]
    coupled = [start[m] * env_first[0] + start[0] * env_first[m] for m in range(9)]
    members = ((0,), (1, 2, 3), (4, 5, 6, 7, 8))
    tensor = []
    for order in range(3):
        mixed = six_pass(jnp.concatenate([coupled[m] for m in members[order]], axis=0), mixes[order])
        tensor += [mixed[rows * i : rows * (i + 1)] for i in range(len(members[order]))]
    weight = six_pass(latent, env_w.split(3))
    env = env_terms(g, weight)
    full = jnp.concatenate([latent, pack_scalars(tensor, env)], axis=1)
    layer_in[...] = full
    pre = jnp.concatenate(forward_pair(full, in_o, in_x), axis=1)
    gate = sigmoid(pre)
    slope = gate * (1.0 + pre * (1.0 - gate))
    hid = pre * gate
    hidden[...] = hid
    latent_next = (
        latent + six_pass(hid[:, :half], out_o.split(3)) + six_pass(hid[:, half:], out_x.split(3))
    )
    latent_out[...] = latent_next
    pre_read = jnp.concatenate(forward_pair(latent_next, head_o, head_x), axis=1)
    gate = sigmoid(pre_read)
    soft = pre_read * gate
    line = read[...]
    inner = jnp.sum(soft * line, axis=1, keepdims=True)
    energy_out[...] = jnp.broadcast_to(
        jnp.sum(group_hot * (g["env"] * inner), axis=0, keepdims=True), energy_out.shape
    )
    scaled_cot = cot * g["env"]
    read_grad[...] = jnp.broadcast_to(
        jnp.sum(scaled_cot * soft, axis=0, keepdims=True), read_grad.shape
    )
    d_envelope = cot * inner
    d_read = scaled_cot * line * (gate * (1.0 + pre_read * (1.0 - gate)))
    d_pre_read[...] = d_read
    d_latent_out[...] = three_pass(dot_nt, d_read[:, :half], head_o.split(3)) + three_pass(
        dot_nt, d_read[:, half:], head_x.split(3)
    )
    d_hid = jnp.concatenate(backward_pair(d_latent_out[...], out_o, out_x, 3), axis=1)
    d_pre = d_hid * slope
    d_pre_hidden[...] = d_pre
    d_full = three_pass(dot_nt, d_pre[:, :half], in_o.split(3)) + three_pass(
        dot_nt, d_pre[:, half:], in_x.split(3)
    )
    d_scalars = unpack_scalars(d_full[:, width:])
    d_tensor = [d_scalars[order_of(m)] * env[m] for m in range(9)]
    d_env = [d_scalars[order_of(m)] * tensor[m] for m in range(9)]
    d_weight, d_harm, d_more = env_pull(g, weight, d_env)
    d_envelope = d_envelope + d_more
    d_weight_out[...] = d_weight
    back[:, :width] = (
        three_pass(dot_nn, d_weight_out[...], env_wt.split(2))
        + d_latent_out[...]
        + d_full[:, :width]
    )
    d_coupled = []
    for order in range(3):
        joined = jnp.concatenate([d_tensor[m] for m in members[order]], axis=0)
        mix_grad[order] = three_pass_tn(
            jnp.concatenate([coupled[m] for m in members[order]], axis=0), joined
        )
        mixed = three_pass(dot_nt, joined, mixes[order])
        d_coupled += [mixed[rows * i : rows * (i + 1)] for i in range(len(members[order]))]
    mix_grad.send()
    d_env_first = [d_coupled[m] * start[0] for m in range(9)]
    d_start = [d_coupled[m] * env_first[0] for m in range(9)]
    for m in range(9):
        d_env_first[0] = d_env_first[0] + d_coupled[m] * start[m]
        d_start[0] = d_start[0] + d_coupled[m] * env_first[m]
    d_first, d_harm_first, d_more = env_pull(g, weight_first, d_env_first)
    for m in range(9):
        d_first = d_first + g["harm"][m] * d_start[m]
        d_harm[m] = (
            d_harm[m]
            + d_harm_first[m]
            + jnp.sum(weight_first * d_start[m], axis=1, keepdims=True)
        )
    d_envelope = d_envelope + d_more
    back[:, width:] = d_first + place_columns(d_harm + [d_envelope], 64)
    back.send()


def first_backward(
    first, edges, key_row, lead_flag, embed,
    layer_in, env_w, arrived, out_o, out_x, slope_in, in_o, in_x, env_wt, head_o, head_x,
    d_vector, d_head, d_pre_hidden, d_weight_out, embed_grad,
):
    rows = arrived.shape[0]
    width = arrived.shape[1] - LANES
    half = width // 2
    lead = lead_flag[0:1, 0:1] > 0.5
    g = edge_values(edges, key_row[...], first, rows, True)
    embed_pair = split_two(embed[...])
    latent = layer_in[:, :width]
    weight = three_pass(dot_nn, latent, env_w.split(2))
    env = env_terms(g, weight)
    extra = arrived[:, width:]
    lane = lax.broadcasted_iota(jnp.int32, extra.shape, 1)
    d_weight = jnp.where(lane < 64, extra, 0.0)
    d_harm = [extra[:, 64 + m : 65 + m] for m in range(9)]
    d_envelope = extra[:, 73:74]
    d_hid = jnp.concatenate(backward_pair(arrived[:, :width], out_o, out_x, 2), axis=1)
    d_pre = d_hid * slope_in[...]
    d_pre_hidden[...] = d_pre
    d_full = three_pass(dot_nt, d_pre[:, :half], in_o.split(2)) + three_pass(
        dot_nt, d_pre[:, half:], in_x.split(2)
    )
    d_scalars = unpack_scalars(d_full[:, width:])
    d_start = [d_scalars[order_of(m)] * env[m] for m in range(9)]
    d_env = [d_scalars[order_of(m)] * (g["harm"][m] * weight) for m in range(9)]
    d_more_weight, d_more_harm, d_more = env_pull(g, weight, d_env)
    d_weight = d_weight + d_more_weight
    d_envelope = d_envelope + d_more
    for m in range(9):
        d_weight = d_weight + g["harm"][m] * d_start[m]
        d_harm[m] = (
            d_harm[m] + d_more_harm[m] + jnp.sum(weight * d_start[m], axis=1, keepdims=True)
        )
    d_weight_out[...] = d_weight
    d_latent = (
        three_pass(dot_nn, d_weight_out[...], env_wt.split(2))
        + arrived[:, :width]
        + d_full[:, :width]
    )
    d_own, d_other = swap_order(lead, d_latent[:, :half], d_latent[:, half:])
    d_head[:, :half] = g["env"] * d_own
    d_head[:, half:] = g["env"] * d_other
    d_head.send()
    d_soft = three_pass(dot_nt, d_own, head_o.split(2)) + three_pass(dot_nt, d_other, head_x.split(2))
    pre = three_pass(dot_nn, g["feat"], embed_pair)
    gate = sigmoid(pre)
    d_envelope = d_envelope + jnp.sum(pre * gate * d_soft, axis=1, keepdims=True)
    d_pre = g["env"] * d_soft * (gate * (1.0 + pre * (1.0 - gate)))
    d_feat = three_pass(dot_nt, d_pre, embed_pair)
    embed_grad[...] = three_pass_tn(g["feat"], d_pre)
    d_bessel = [d_feat[:, 2 * NSPEC + k : 2 * NSPEC + 1 + k] for k in range(NBES)]
    d_vector[...] = place_columns(vector_pull(g, d_bessel, d_harm, d_envelope), 0)


def outer_sum(split_left, chosen, *refs):
    count = len(CHUNKS)
    extra = len(refs) > 4 * count + 8
    kinds = 3 if extra else 2
    sources = [
        [refs[(kinds * side + i) * count : (kinds * side + i + 1) * count] for i in range(kinds)]
        for side in range(2)
    ]
    rest = refs[2 * kinds * count :]
    outs = [Stored(rest[i], rest[kinds + i], rest[-1].at[i]) for i in range(kinds)]
    buffers = rest[2 * kinds : 3 * kinds]
    semaphores = rest[-2]

    def copies(side):
        for i in range(kinds):
            start = 0
            for k, source in enumerate(sources[side][i]):
                rows, columns = source.shape[0], buffers[i].shape[1]
                yield pltpu.make_async_copy(
                    source.at[:, pl.ds(0, columns)],
                    buffers[i].at[pl.ds(start, rows)],
                    semaphores.at[i * count + k],
                )
                start += rows

    for side in range(2):

        @pl.when(chosen[0] == side)
        def _(side=side):
            for copy in copies(side):
                copy.start()

    for copy in copies(0):
        copy.wait()
    left_high, left_low = split_two(buffers[0][...])
    right_high, right_low = split_two(buffers[1][...])
    left = jnp.concatenate([left_high, left_low, left_high], axis=0)
    right = jnp.concatenate([right_high, right_high, right_low], axis=0)
    if split_left:
        half = left.shape[1] // 2
        outs[1][...] = dot_tn(left[:, half:], right)
        outs[0][...] = dot_tn(left[:, :half], right)
    else:
        half = right.shape[1] // 2
        outs[1][...] = dot_tn(left, right[:, half:])
        outs[0][...] = dot_tn(left, right[:, :half])
    if extra:
        right_high, right_low = split_two(buffers[2][...])
        right = jnp.concatenate([right_high, right_high, right_low], axis=0)
        outs[2][...] = dot_tn(left[:, : outs[2].shape[0]], right)
    for out in outs:
        out.copy.wait()


def on_core(body, outs, flops, args, fetched, chosen):
    here = pl.BlockSpec(memory_space=pltpu.VMEM)
    there = pl.BlockSpec(memory_space=pl.ANY)
    pad = 2 * LANES
    tall = [(m.shape[0] + pad - 1) // pad * pad if m.shape[0] > pad else m.shape[0] for m in fetched]
    scratch = [pltpu.VMEM((rows, m.shape[1]), F32) for rows, m in zip(tall, fetched)]
    scratch += [pltpu.VMEM(shape, F32) for shape in outs]
    scratch.append(pltpu.SemaphoreType.DMA((len(fetched),)))
    scratch.append(pltpu.SemaphoreType.DMA((len(outs),)))

    def guarded(flag, *refs):
        @pl.when(flag[0] == 1)
        def _():
            small, rest = refs[: len(args)], refs[len(args) :]
            sources, rest = rest[: len(fetched)], rest[len(fetched) :]
            targets, rest = rest[: len(outs)], rest[len(outs) :]
            buffers, rest = rest[: len(fetched)], rest[len(fetched) :]
            kept, (arrivals, departures) = rest[: len(outs)], rest[len(outs) :]
            inputs = [Fetched(s, b, arrivals.at[i]) for i, (s, b) in enumerate(zip(sources, buffers))]
            outputs = [Stored(t, b, departures.at[i]) for i, (t, b) in enumerate(zip(targets, kept))]
            body(*small, *inputs, *outputs)
            for output in outputs:
                output.copy.wait()

    return pl.pallas_call(
        guarded,
        out_shape=tuple(jax.ShapeDtypeStruct(shape, F32) for shape in outs),
        in_specs=[pl.BlockSpec(memory_space=pltpu.SMEM)] + [here] * len(args) + [there] * len(fetched),
        out_specs=tuple(there for _ in outs),
        scratch_shapes=scratch,
        compiler_params=pltpu.CompilerParams(vmem_limit_bytes=60 * 2**20),
        cost_estimate=pl.CostEstimate(flops=flops, bytes_accessed=16 * 2**20, transcendentals=0),
    )(chosen, *args, *fetched)


def outer_call(split_left, outs, widths, flops, chosen, first, second):
    there = pl.BlockSpec(memory_space=pl.ANY)
    args = [array for side in (first, second) for factor in side for array in factor]
    return pl.pallas_call(
        partial(outer_sum, split_left),
        out_shape=tuple(jax.ShapeDtypeStruct(shape, F32) for shape in outs),
        in_specs=[pl.BlockSpec(memory_space=pltpu.SMEM)] + [there] * len(args),
        out_specs=tuple(there for _ in outs),
        scratch_shapes=[pltpu.VMEM(shape, F32) for shape in outs]
        + [pltpu.VMEM((sum(CHUNKS), w), F32) for w in widths]
        + [
            pltpu.SemaphoreType.DMA((len(widths) * len(CHUNKS),)),
            pltpu.SemaphoreType.DMA((len(outs),)),
        ],
        compiler_params=pltpu.CompilerParams(vmem_limit_bytes=60 * 2**20),
        cost_estimate=pl.CostEstimate(flops=flops, bytes_accessed=16 * 2**20, transcendentals=0),
    )(chosen, *args)


def gather_blocks(value):
    count = lax.axis_size("edge")
    if count & (count - 1) or count > 8:
        return lax.all_gather(value, "edge", axis=0)
    index = lax.axis_index("edge")
    out = value[None]
    step = 1
    while step < count:
        got = lax.ppermute(out, "edge", [(i, i ^ step) for i in range(count)])
        low = (index // step) % 2 == 0
        out = jnp.where(low, jnp.concatenate([out, got]), jnp.concatenate([got, out]))
        step *= 2
    return out


def prefix_in_rows(flags):
    rows, length = flags.shape
    pieces = flags.reshape(rows, length // LANES, LANES)
    upper = (jnp.arange(LANES)[:, None] <= jnp.arange(LANES)[None, :]).astype(F32)
    inner = jnp.einsum("rkl,lm->rkm", pieces, upper, precision=HIGHEST)
    totals = inner[:, :, -1]
    count = length // LANES
    before = (jnp.arange(count)[:, None] < jnp.arange(count)[None, :]).astype(F32)
    offsets = jnp.dot(totals, before, precision=HIGHEST)
    return (inner + offsets[:, :, None]).reshape(rows, length)


def pack_edges(atoms, vectors, species, centres, mask, structures, out):
    count = centres.shape[1]
    for b in range(centres.shape[0]):
        span = slice(b * count, (b + 1) * count)
        vector = vectors[b]
        out[0:3, span] = vector
        out[3:5, span] = species[b].astype(F32)
        out[5:6, span] = (centres[b : b + 1, :] + b * atoms).astype(F32)
        squares = jnp.maximum(jnp.sum(vector * vector, axis=0, keepdims=True), 0.25)
        near = jnp.where(jnp.sqrt(squares) / CUTOFF < 1.0, 1.0, 0.0)
        out[6:7, span] = jnp.where(mask[b : b + 1, :] > 0, near, 0.0)
        out[7:8, span] = (structures[b : b + 1, :] + b * STRUCTS).astype(F32)


def plan_edges(edge_vectors, edge_species, centres, edge_mask, structures):
    batch_count, _, edge_count = edge_vectors.shape
    blocks = lax.axis_size("edge")
    block = lax.axis_index("edge")
    core = lax.axis_index("mp")
    atoms = blocks * ATOM_DEV
    per_block = batch_count * edge_count
    raw = pl.pallas_call(
        partial(pack_edges, atoms), out_shape=jax.ShapeDtypeStruct((8, per_block), F32)
    )(edge_vectors, edge_species, centres, edge_mask, structures)
    gathered = gather_blocks(raw)
    keys = gathered[:, 5].reshape(blocks, batch_count, edge_count)
    alive = gathered[:, 6].reshape(blocks, batch_count, edge_count)
    local = keys - (jnp.arange(batch_count) * atoms)[None, :, None].astype(F32)
    degree = jnp.sum(
        jnp.where(
            local.transpose(1, 0, 2).reshape(batch_count, 1, -1)
            == jnp.arange(atoms, dtype=F32)[None, :, None],
            alive.transpose(1, 0, 2).reshape(batch_count, 1, -1),
            0.0,
        ),
        axis=2,
    )
    spans = batch_count * ATOM_DEV
    degree = degree.reshape(batch_count, blocks, ATOM_DEV).transpose(1, 0, 2).reshape(blocks, spans)
    upper = (jnp.arange(spans)[:, None] <= jnp.arange(spans)[None, :]).astype(F32)
    upto = jnp.dot(degree, upper, precision=HIGHEST)
    start = jnp.zeros((blocks, 1), F32)
    starts = [start]
    for size in CHUNKS:
        for _ in range(2):
            start = jnp.max(jnp.where(upto <= start + size, jnp.maximum(upto, start), start), axis=1, keepdims=True)
            starts.append(start)
    fits = jnp.all(starts[-1] >= upto[:, -1:])
    starts = jnp.concatenate(starts[:-1], axis=1)
    own_before = (upto - degree)[block]
    bin_of = jnp.sum((own_before[:, None] >= starts[block][None, 1:]).astype(F32), axis=1)
    padded = jnp.concatenate([jnp.zeros_like(gathered[:1]), gathered, jnp.zeros_like(gathered[:1])])
    window = lax.dynamic_slice_in_dim(padded, block, 3, 0)
    flat = window.transpose(1, 0, 2).reshape(8, 3 * per_block)
    position = jnp.arange(3 * per_block)
    batch_flat = (position % per_block) // edge_count
    spot = flat[5] - (batch_flat * atoms + block * ATOM_DEV).astype(F32)
    mine = (spot >= 0) & (spot < ATOM_DEV) & (flat[6] > 0.5)
    slot = jnp.where(mine, spot + (batch_flat * ATOM_DEV).astype(F32), -1.0)
    chosen = jnp.sum(
        jnp.where(jnp.arange(spans, dtype=F32)[:, None] == slot[None, :], bin_of[:, None], 0.0), axis=0
    )
    wanted = 2 * jnp.arange(len(CHUNKS)) + core
    picked = (chosen[None, :] == wanted[:, None].astype(F32)) & mine[None, :]
    rank = prefix_in_rows(picked.astype(F32)) - 1.0
    offsets = [sum(CHUNKS[:k]) for k in range(len(CHUNKS))]
    place = jnp.sum(
        jnp.where(picked, rank + jnp.array(offsets, F32)[:, None], 0.0), axis=0
    ) - (1.0 - jnp.sum(picked.astype(F32), axis=0))
    total = sum(CHUNKS)
    hot = (place[None, :] == jnp.arange(total, dtype=F32)[:, None]).astype(F32)
    edges = lax.dot_general(hot, flat, (((1,), (1,)), ((), ())), precision=HIGHEST)
    return fits, edges, place


def tied(first, *others):
    return lax.optimization_barrier((first, others))[0]


def hop(value, distance):
    return lax.ppermute(value, "edge", [(i, i ^ distance) for i in range(8)])


def halves(value, second):
    half = value.shape[0] // 2
    kept = lax.dynamic_slice_in_dim(value, second * half, half, 0)
    return kept, lax.dynamic_slice_in_dim(value, (1 - second) * half, half, 0)


def joined(kept, got, second):
    return jnp.where(second == 0, jnp.concatenate([kept, got]), jnp.concatenate([got, kept]))


def sum_steps(value, outer_hop, inner_hop, wait):
    index = lax.axis_index("edge")
    seconds = {1: index % 2, 2: ((index // 2) ^ (index // 4)) % 2}
    kept, given = halves(value, seconds[outer_hop])
    given = wait(given)
    got = hop(given, outer_hop)
    yield given
    kept, given = halves(kept + wait(got), seconds[inner_hop])
    got = hop(given, inner_hop)
    yield given
    part = kept + wait(got)
    got = hop(part, 6)
    yield part
    part = part + wait(got)
    got = hop(part, inner_hop)
    yield part
    part = joined(part, wait(got), seconds[inner_hop])
    half = part.shape[0]
    got = hop(part, outer_hop)
    yield part
    yield [(part, seconds[outer_hop] * half), (wait(got), (1 - seconds[outer_hop]) * half)]


class BlockSums:
    def __init__(self, plan):
        self.plan, self.steps, self.sums, self.moment = plan, {}, {}, None

    def wait(self, value):
        return value if self.moment is None else tied(value, self.moment)

    def advance(self, matrices, order):
        for piece in order:
            which, first, rows, outer_hop, inner_hop = self.plan[piece]
            if piece not in self.steps:
                value = lax.slice_in_dim(matrices[which], first, first + rows, axis=0)
                self.steps[piece] = sum_steps(value, outer_hop, inner_hop, self.wait)
            given = next(self.steps[piece])
            if isinstance(given, list):
                total = self.sums.get(which, jnp.zeros_like(matrices[which]))
                for part, start in given:
                    total = lax.dynamic_update_slice_in_dim(total, part, first + start, 0)
                self.sums[which] = total
                given = given[1][0]
            self.moment = given


def fast_device(edges, place, others, args):
    (
        edge_vectors, edge_species, centres, edge_mask, structures, energy_cot, embed_in,
        section_head, env_weight, mix_weight, w_in, w_out, read_weight,
    ) = args
    is_first = lax.axis_index("section") == 0
    core = lax.axis_index("mp")
    width = section_head.shape[1]
    half = section_head.shape[2]
    batch_count, _, edge_count = edge_vectors.shape
    chan_count = mix_weight.shape[1]
    gap = LANES - chan_count
    read_left, read_right = read_weight[:half], read_weight[half:]
    read_line = jnp.where(
        core == 0,
        jnp.concatenate([read_left, read_right]),
        jnp.concatenate([read_right, read_left]),
    )[None]
    cot_row = jnp.pad(energy_cot.reshape(1, -1), ((0, 0), (0, LANES - energy_cot.size)))
    lead_flag = jnp.full((8, LANES), 1.0, F32) * (core == 0).astype(F32)
    mix = jnp.pad(mix_weight, ((0, 0), (0, gap), (0, gap)))
    env_w = jnp.pad(env_weight[0], ((0, 0), (0, gap)))
    env_wt = env_w.T
    heads, ins, outs_w = (section_head[0], others[0]), (w_in[0], others[1]), (w_out[0], others[2])
    count = len(CHUNKS)
    offsets = [sum(CHUNKS[:k]) for k in range(count)]
    rows = [edges[o : o + m, 5].reshape(1, -1) for o, m in zip(offsets, CHUNKS)]
    layer_width = width + 2 * LANES

    first_flag = jnp.full((1,), 1, jnp.int32) * is_first.astype(jnp.int32)
    second_flag = 1 - first_flag
    saved, moved = [], []
    for k, m in enumerate(CHUNKS):
        outs = [(m, width + LANES), (m, width), (m, layer_width), (m, width), (m, width)]
        work = 12 * m * width * (3 * width + 384)
        result = on_core(
            partial(first_forward, offsets[k]), outs, work,
            (edges, rows[k], lead_flag, embed_in), (*heads, env_w, *ins, *outs_w), first_flag,
        )
        moved.append(shifted(result[0], "section", 1))
        saved.append(result[1:])
    seconds, returned, firsts = [], [], []
    for k, m in enumerate(CHUNKS):
        outs = [
            (m, width + LANES), (m, layer_width), (m, width), (m, width), (m, width),
            (m, width), (m, width), (m, LANES), (8, width), (3, LANES, LANES), (8, LANES),
        ]
        work = 18 * m * width * (3 * width + 384)
        seconds.append(
            on_core(
                partial(second_both, offsets[k]), outs, work,
                (edges, rows[k], mix, read_line, cot_row),
                (moved[k], env_w, *ins, *outs_w, *heads, env_wt), second_flag,
            )
        )
    outer_work = 6 * sum(CHUNKS) * width * width
    by_hand = lax.axis_size("edge") == 8
    sums = BlockSums(PLAN)
    for k, m in enumerate(CHUNKS):
        back = seconds[k][0] if k == 0 else tied(seconds[k][0], firsts[k - 1][0])
        returned.append(shifted(back, "section", -1))
        arrived = returned[k]
        if k == count - 1:
            out_own, out_other = outer_call(
                True, [(half, width)] * 2, (width, width), outer_work, second_flag,
                ([s[3] for s in saved], returned),
                ([s[3] for s in seconds], [s[4] for s in seconds]),
            )
            arrived = tied(arrived, out_other)
            grad_out = out_own + other_core(out_other)
            if by_hand:
                sums.advance([grad_out], EARLY)
        outs = [(m, LANES), (m, width), (m, width), (m, LANES), (16, width)]
        work = 9 * m * width * (3 * width + 384)
        firsts.append(
            on_core(
                partial(first_backward, offsets[k]), outs, work,
                (edges, rows[k], lead_flag, embed_in),
                (saved[k][1], env_w, arrived, *outs_w, saved[k][2], *ins, env_wt, *heads), first_flag,
            )
        )
    in_own, in_other, grad_env = outer_call(
        False, [(layer_width, half)] * 2 + [(width, LANES)], (layer_width, width, LANES), outer_work,
        sums.wait(second_flag),
        ([s[1] for s in saved], [f[2] for f in firsts], [f[3] for f in firsts]),
        ([s[1] for s in seconds], [s[2] for s in seconds], [s[7] for s in seconds]),
    )
    grad_in = in_own + other_core(in_other)
    if by_hand:
        sums.moment = (sums.moment, in_other)
        sums.advance([grad_out], EARLY)
    head_own, head_other = outer_call(
        False, [(width, half)] * 2, (width, width), outer_work, tied(second_flag, in_other, sums.moment),
        ([s[0] for s in saved], [f[1] for f in firsts]),
        ([s[5] for s in seconds], [s[6] for s in seconds]),
    )
    none = jnp.zeros((), F32)
    read_sum = sum(s[8][0] for s in seconds)
    read_sum = jnp.where(
        core == 0, read_sum, jnp.concatenate([read_sum[half:], read_sum[:half]])
    )
    mix_sum = sum(s[9] for s in seconds)[:, :chan_count, :chan_count].reshape(-1, width)
    energy_sum = sum(s[10][0] for s in seconds)
    embed_sum = sum(f[4] for f in firsts)
    small_second = jnp.concatenate(
        [read_sum[None], jnp.pad(energy_sum, (0, width - LANES))[None], mix_sum]
    )
    small_second = jnp.pad(small_second, ((0, 16 - small_second.shape[0]), (0, 0)))
    small = jnp.concatenate(
        [jnp.where(is_first, embed_sum, none), jnp.where(is_first, none, small_second)]
    )
    small = small + lax.ppermute(small, "section", [(0, 1), (1, 0)])
    small = jnp.concatenate([small, grad_env[:, :chan_count].reshape(-1, width)]).reshape(-1, half)
    head_own = jnp.concatenate([head_own, small])
    grad_head = head_own + other_core(jnp.concatenate([head_other, small]))
    total = sum(CHUNKS)
    hot = (place[None, :] == jnp.arange(total, dtype=F32)[:, None]).astype(F32)
    d_vectors = jnp.concatenate([f[0][:, :8] for f in firsts])
    spread = lax.dot_general(d_vectors, hot, (((0,), (0,)), ((), ())), precision=HIGHEST)[:3]
    spread = jnp.where(is_first, spread, none)
    if by_hand:
        matrices = [grad_out, grad_in, grad_head]
        sums.moment = (sums.moment, head_other, grad_in, grad_head)
        sums.advance(matrices, ORDER[:8])
        spread = sums.wait(spread)
        spread = spread + other_core(spread)
        sums.advance(matrices, ORDER[8:16])
        spread = sums.wait(spread)
        sums.advance(matrices, ORDER[16:])
        grad_out, grad_in, grad_head = (sums.sums[i] for i in range(3))
    else:
        spread = spread + other_core(spread)
        grad_out, grad_in, grad_head = lax.psum((grad_out, grad_in, grad_head), "edge")
    per_block = batch_count * edge_count
    to_left, kept, to_right = (spread[:, i * per_block : (i + 1) * per_block] for i in range(3))
    forces = kept + shifted(to_right, "edge", 1) + shifted(to_left, "edge", -1)
    small = grad_head[width:].reshape(-1, width)
    grad_head = grad_head[:width]
    grad_embed, grad_read = small[:16], small[16]
    energies = small[17, : energy_cot.size].reshape(energy_cot.shape)
    grad_mix = small[18 : 18 + mix_sum.shape[0]].reshape(mix_weight.shape)
    grad_env = small[32:].reshape(width, chan_count)

    forces = jnp.where(is_first, forces, shifted(forces, "section", 1))
    forces = -forces.reshape(3, batch_count, edge_count).transpose(1, 0, 2)
    return (
        energies, forces, grad_embed, grad_head[None], grad_env[None], grad_mix,
        grad_in[None, : w_in.shape[1]], grad_out[None], grad_read,
    )


def per_device(*args):
    section_head, w_in, w_out = args[7], args[10], args[11]
    others = tuple(other_core(m[0]) for m in (section_head, w_in, w_out))
    fits, edges, place = plan_edges(*args[:5])
    results = fast_device(edges, place, others, args)

    def again(state):
        rest, _ = state
        held, rest = lax.optimization_barrier((args, rest))
        return rest - 1, general_device(*held)

    overflow = 1 - fits.astype(jnp.int32)
    return lax.while_loop(lambda state: state[0] > 0, again, (overflow, results))[1]


def solution(mesh):
    placed = (
        P(None, None, "edge"),
        P(None, None, "edge"),
        P(None, "edge"),
        P(None, "edge"),
        P(None, "edge"),
        P(),
        P(),
        P("section", None, "mp"),
        P("section", None, None),
        P(),
        P("section", None, "mp"),
        P("section", "mp", None),
        P(),
    )
    return jax.shard_map(
        per_device,
        mesh=mesh,
        in_specs=placed,
        out_specs=(
            P(),
            P(None, None, "edge"),
            P(),
            P("section", None, "mp"),
            P("section", None, None),
            P(),
            P("section", None, "mp"),
            P("section", "mp", None),
            P(),
        ),
        check_vma=False,
    )
```

```python
from functools import partial

import jax
import jax.numpy as jnp
from jax import lax
from jax.experimental import pallas as pl
from jax.experimental.pallas import tpu as pltpu
from jax.sharding import PartitionSpec as P

NBES = 8
NSPEC = 4
ATOM_DEV = 40
STRUCTS = 16


CUTOFF = 5.0
ENV_SCALE = 0.25
HIGHEST = lax.Precision.HIGHEST
ROOT_THREE = 1.7320508075688772
ROOT_FIVE = 2.23606797749979
ROOT_FIFTEEN = 3.872983346207417


def extended(block, sides, width):
    for axis, dim in sides:
        count = lax.axis_size(axis)
        forward = [(i, i + 1) for i in range(count - 1)]
        backward = [(target, source) for source, target in forward]
        low = lax.ppermute(
            lax.slice_in_dim(block, block.shape[dim] - width, None, axis=dim), axis, forward
        )
        high = lax.ppermute(lax.slice_in_dim(block, 0, width, axis=dim), axis, backward)
        block = jnp.concatenate([low, block, high], axis=dim)
    return block


def shifted(value, axis, steps):
    count = lax.axis_size(axis)
    first, last = (max(0, -steps), min(count, count - steps))
    return lax.ppermute(value, axis, [(source, source + steps) for source in range(first, last)])


def other_core(value):
    return lax.ppermute(value, "mp", [(0, 1), (1, 0)])


def ring_sum(values):
    count = lax.axis_size("edge")

    def step(_, state):
        moving, total = state
        moving = tuple(
            lax.ppermute(v, "edge", [(i, (i + 1) % count) for i in range(count)]) for v in moving
        )
        return moving, tuple(t + v for t, v in zip(total, moving))

    return lax.fori_loop(0, count - 1, step, (tuple(values), tuple(values)))[1]


def matmul(left, right):
    return jnp.dot(left, right, precision=HIGHEST, preferred_element_type=jnp.float32)


def geometry(vectors, edge_live):
    squares = jnp.maximum(jnp.sum(vectors * vectors, axis=0), 0.25)
    length = jnp.sqrt(squares)
    unit_x = vectors[0] / length
    unit_y = vectors[1] / length
    unit_z = vectors[2] / length
    edge_ratio = jnp.minimum(length / CUTOFF, 1.0)
    envelope = (
        1.0 - 28.0 * edge_ratio**6 + 48.0 * edge_ratio**7 - 21.0 * edge_ratio**8
    ) * edge_live
    orders = jnp.arange(1, NBES + 1).astype(jnp.float32)
    bessel = (
        jnp.sqrt(2.0 / CUTOFF)
        * jnp.sin(orders[None, :] * (jnp.pi / CUTOFF) * length[:, None])
        / length[:, None]
    )
    harmonics = jnp.stack(
        [
            jnp.ones_like(unit_x),
            ROOT_THREE * unit_x,
            ROOT_THREE * unit_y,
            ROOT_THREE * unit_z,
            ROOT_FIFTEEN * unit_x * unit_y,
            ROOT_FIFTEEN * unit_y * unit_z,
            0.5 * ROOT_FIVE * (3.0 * unit_z * unit_z - 1.0),
            ROOT_FIFTEEN * unit_x * unit_z,
            0.5 * ROOT_FIFTEEN * (unit_x * unit_x - unit_y * unit_y),
        ],
        axis=1,
    )
    return (harmonics, envelope, bessel)


def couple(edge_tensor, env_flat, mix_weight):
    chan_count = mix_weight.shape[1]
    own_tensor = edge_tensor.reshape(-1, 9, chan_count)
    env_tensor = env_flat.reshape(-1, 9, chan_count)
    paired = own_tensor * env_tensor
    scalars = jnp.concatenate(
        [paired[:, 0], jnp.sum(paired[:, 1:4], axis=1), jnp.sum(paired[:, 4:9], axis=1)], axis=1
    )
    coupled = own_tensor * env_tensor[:, 0:1] + own_tensor[:, 0:1] * env_tensor
    order_zero = jnp.einsum("emc,cd->emd", coupled[:, 0:1], mix_weight[0], precision=HIGHEST)
    order_one = jnp.einsum("emc,cd->emd", coupled[:, 1:4], mix_weight[1], precision=HIGHEST)
    order_two = jnp.einsum("emc,cd->emd", coupled[:, 4:9], mix_weight[2], precision=HIGHEST)
    updated = jnp.concatenate([order_zero, order_one, order_two], axis=1)
    return (scalars, updated.reshape(-1, 9 * chan_count))


def front(bessel, envelope, embed_in, head_local, kinds_hot):
    features = jnp.concatenate([kinds_hot, bessel], axis=1)
    return envelope[:, None] * matmul(jax.nn.silu(matmul(features, embed_in)), head_local)


def contribute(latent_full, harmonics, envelope, env_local, centre_hot):
    weight = matmul(latent_full, env_local)
    contribution = (
        (ENV_SCALE * envelope)[:, None, None] * harmonics[:, :, None] * weight[:, None, :]
    )
    flat_terms = contribution.reshape(weight.shape[0], -1)
    return (weight, matmul(centre_hot.T, flat_terms))


def tensor_step(tensor_full, env_window, weight, harmonics, mix_weight, centre_hot, is_first):
    start_tensor = (harmonics[:, :, None] * weight[:, None, :]).reshape(weight.shape[0], -1)
    edge_tensor = jnp.where(is_first, start_tensor, tensor_full)
    env_flat = matmul(centre_hot, env_window)
    return couple(edge_tensor, env_flat, mix_weight)


def perceptron(latent_full, scalars, in_local, out_local):
    hidden = jax.nn.silu(matmul(jnp.concatenate([latent_full, scalars], axis=1), in_local))
    return matmul(hidden, out_local)


def readout(latent_full, envelope, head_local, read_half):
    return envelope * matmul(jax.nn.silu(matmul(latent_full, head_local)), read_half)


def general_device(
    edge_vectors,
    edge_species,
    centres,
    edge_mask,
    structures,
    energy_cot,
    embed_in,
    section_head,
    env_weight,
    mix_weight,
    w_in,
    w_out,
    read_weight,
):
    section_index = lax.axis_index("section")
    core_index = lax.axis_index("mp")
    edge_index = lax.axis_index("edge")
    is_first = section_index == 0
    last_flag = (section_index == 1).astype(jnp.float32)
    batch_count = edge_vectors.shape[0]
    shard_width = w_out.shape[1]
    tensor_cols = 9 * env_weight.shape[2]
    tensor_half = tensor_cols // 2
    atoms_dev = ATOM_DEV
    head_local = section_head[0]
    env_local = env_weight[0]
    in_local = w_in[0]
    out_local = w_out[0]
    read_half = lax.dynamic_slice_in_dim(read_weight, core_index * shard_width, shard_width, 0)
    core_lead = (core_index == 0).astype(jnp.float32)
    edge_count = edge_vectors.shape[2]
    centre_slots = jnp.arange(3 * atoms_dev)
    labels = jnp.arange(STRUCTS)
    species_range = jnp.arange(NSPEC)
    batch_range = jnp.arange(batch_count)

    def reduce_rims(pieces):
        widened = extended(pieces, (("edge", 0),), atoms_dev)
        return (
            widened[:atoms_dev] + widened[2 * atoms_dev : 3 * atoms_dev] + widened[4 * atoms_dev :]
        )

    def window_rows(totals):
        return extended(totals, (("edge", 0),), atoms_dev)

    def collect(partial_rows):
        width = partial_rows.shape[1] // 2
        own = lax.dynamic_slice_in_dim(partial_rows, core_index * width, width, 1)
        return own + other_core(lax.dynamic_slice_in_dim(partial_rows, (1 - core_index) * width, width, 1))

    def both_halves(half):
        other = other_core(half)
        return jnp.where(
            core_index == 0,
            jnp.concatenate([half, other], axis=1),
            jnp.concatenate([other, half], axis=1),
        )

    def batch_data(batch_index):
        vectors = lax.dynamic_index_in_dim(edge_vectors, batch_index, 0, keepdims=False)
        kind_ids = lax.dynamic_index_in_dim(edge_species, batch_index, 0, keepdims=False)
        owners = lax.dynamic_index_in_dim(centres, batch_index, 0, keepdims=False)
        edge_live = lax.dynamic_index_in_dim(edge_mask, batch_index, 0, keepdims=False).astype(
            jnp.float32
        )
        groups = lax.dynamic_index_in_dim(structures, batch_index, 0, keepdims=False)
        kinds_hot = jnp.concatenate(
            [
                kind_ids[0][:, None] == species_range[None, :],
                kind_ids[1][:, None] == species_range[None, :],
            ],
            axis=1,
        ).astype(jnp.float32)
        local_slot = owners - (edge_index - 1) * atoms_dev
        centre_hot = (local_slot[:, None] == centre_slots[None, :]).astype(jnp.float32)
        group_hot = (groups[:, None] == labels[None, :]).astype(jnp.float32)
        return (vectors, edge_live, kinds_hot, centre_hot, group_hot)

    recv_latent = jnp.zeros((edge_count, shard_width), jnp.float32)
    recv_tensor = jnp.zeros((edge_count, tensor_half), jnp.float32)
    energies = jnp.zeros((batch_count, STRUCTS), jnp.float32)
    kept_state = []
    for step_index in range(batch_count + 1):
        batch_raw = step_index - section_index
        batch_index = jnp.clip(batch_raw, 0, batch_count - 1)
        is_valid = ((batch_raw >= 0) & (batch_raw < batch_count)).astype(jnp.float32)
        vectors, edge_live, kinds_hot, centre_hot, group_hot = batch_data(batch_index)
        harmonics, envelope, bessel = geometry(vectors, edge_live)
        latent_half = lax.cond(
            is_first,
            lambda: front(bessel, envelope, embed_in, head_local, kinds_hot),
            lambda: recv_latent,
        )
        latent_full, tensor_full = (
            both_halves(latent_half),
            both_halves(recv_tensor),
        )
        weight, part_sums = contribute(latent_full, harmonics, envelope, env_local, centre_hot)
        env_window = window_rows(reduce_rims(part_sums))
        scalars, updated = tensor_step(
            tensor_full, env_window, weight, harmonics, mix_weight, centre_hot, is_first
        )
        branch_out = perceptron(latent_full, scalars, in_local, out_local)
        summed = collect(branch_out)
        tensor_own = lax.dynamic_slice_in_dim(updated, core_index * tensor_half, tensor_half, 1)
        next_half = latent_half + summed
        recv_latent, recv_tensor = shifted((next_half, tensor_own), "section", 1)
        next_full = both_halves(next_half)
        edge_energy = readout(next_full, envelope, head_local, read_half)
        batch_slot = (batch_range == batch_index).astype(jnp.float32) * is_valid * last_flag
        energies = (
            energies
            + batch_slot[:, None] * jnp.dot(edge_energy, group_hot, precision=HIGHEST)[None, :]
        )
        kept_state.append((latent_full, tensor_full, env_window, next_full))
    kept_latent = jnp.stack([entry[0] for entry in kept_state])
    kept_tensor = jnp.stack([entry[1] for entry in kept_state])
    kept_window = jnp.stack([entry[2] for entry in kept_state])
    kept_next = jnp.stack([entry[3] for entry in kept_state])
    grad_head = jnp.zeros_like(head_local)
    grad_env = jnp.zeros_like(env_local)
    grad_in = jnp.zeros_like(in_local)
    grad_out = jnp.zeros_like(out_local)
    grad_mix = jnp.zeros_like(mix_weight)
    grad_embed = jnp.zeros_like(embed_in)
    grad_read = jnp.zeros_like(read_half)
    forces = jnp.zeros((batch_count, 3, edge_count), jnp.float32)
    recv_grad = jnp.zeros((edge_count, shard_width), jnp.float32)
    recv_tgrad = jnp.zeros((edge_count, tensor_half), jnp.float32)
    for step_index in range(batch_count + 1):
        batch_raw = step_index - 1 + section_index
        batch_index = jnp.clip(batch_raw, 0, batch_count - 1)
        is_valid = ((batch_raw >= 0) & (batch_raw < batch_count)).astype(jnp.float32)
        saved_index = jnp.clip(batch_raw + section_index, 0, batch_count)
        latent_full = lax.dynamic_index_in_dim(kept_latent, saved_index, 0, keepdims=False)
        tensor_full = lax.dynamic_index_in_dim(kept_tensor, saved_index, 0, keepdims=False)
        env_window = lax.dynamic_index_in_dim(kept_window, saved_index, 0, keepdims=False)
        next_full = lax.dynamic_index_in_dim(kept_next, saved_index, 0, keepdims=False)
        vectors, edge_live, kinds_hot, centre_hot, group_hot = batch_data(batch_index)
        (harmonics, envelope, bessel), geometry_pull = jax.vjp(
            partial(geometry, edge_live=edge_live), vectors
        )
        batch_cot = lax.dynamic_index_in_dim(energy_cot, batch_index, 0, keepdims=False)
        energy_rows = jnp.dot(group_hot, batch_cot, precision=HIGHEST) * (is_valid * last_flag)
        _, read_pull = jax.vjp(readout, next_full, envelope, head_local, read_half)
        d_next_read, d_env_read, g_head_read, g_read = read_pull(energy_rows)
        d_next_half = jnp.where(is_first, recv_grad, collect(d_next_read))
        d_out_full, d_updated = (
            both_halves(d_next_half),
            both_halves(recv_tgrad),
        )
        (weight, part_sums), contribute_pull = jax.vjp(
            partial(contribute, centre_hot=centre_hot), latent_full, harmonics, envelope, env_local
        )
        (scalars, updated), tensor_pull = jax.vjp(
            partial(tensor_step, centre_hot=centre_hot, is_first=is_first),
            tensor_full,
            env_window,
            weight,
            harmonics,
            mix_weight,
        )
        _, perceptron_pull = jax.vjp(perceptron, latent_full, scalars, in_local, out_local)
        d_latent_mlp, d_scalar_part, g_in, g_out = perceptron_pull(d_out_full)
        d_scalars = d_scalar_part + other_core(d_scalar_part)
        d_tensor, d_window, d_weight, d_harm_tensor, g_mix = tensor_pull((d_scalars, d_updated))
        d_parts = window_rows(reduce_rims(d_window))
        d_latent_env, d_harm_env, d_envelope_env, g_env = contribute_pull((d_weight, d_parts))
        d_latent_own = (
            collect(d_latent_mlp)
            + lax.dynamic_slice_in_dim(d_latent_env, core_index * shard_width, shard_width, 1)
            + d_next_half
        )
        d_tensor_own = lax.dynamic_slice_in_dim(d_tensor, core_index * tensor_half, tensor_half, 1)
        recv_grad, recv_tgrad = shifted((d_latent_own, d_tensor_own), "section", -1)

        def front_pull(cotangent):
            _, pull_back = jax.vjp(
                partial(front, kinds_hot=kinds_hot), bessel, envelope, embed_in, head_local
            )
            return pull_back(cotangent)

        def front_none(cotangent):
            return (
                jnp.zeros_like(bessel),
                jnp.zeros_like(envelope),
                jnp.zeros_like(embed_in),
                jnp.zeros_like(head_local),
            )

        d_bessel, d_envelope_front, g_embed, g_head_front = lax.cond(
            is_first, front_pull, front_none, d_latent_own
        )
        d_harmonics = core_lead * (d_harm_tensor + d_harm_env)
        d_envelope = core_lead * d_envelope_env + d_env_read + d_envelope_front
        d_vectors = geometry_pull((d_harmonics, d_envelope, d_bessel))[0]
        batch_slot = (batch_range == batch_index).astype(jnp.float32) * is_valid
        forces = forces + batch_slot[:, None, None] * d_vectors[None]
        grad_head = grad_head + is_valid * (g_head_read + g_head_front)
        grad_env = grad_env + is_valid * g_env
        grad_in = grad_in + is_valid * g_in
        grad_out = grad_out + is_valid * g_out
        grad_mix = grad_mix + is_valid * g_mix
        grad_embed = grad_embed + is_valid * g_embed
        grad_read = grad_read + is_valid * g_read
    grad_head, grad_env, grad_in, grad_out = ring_sum((grad_head, grad_env, grad_in, grad_out))
    read_full = lax.dynamic_update_slice_in_dim(
        jnp.zeros_like(read_weight), grad_read, core_index * shard_width, 0
    )
    chip_sums = [v + other_core(v) for v in (energies, grad_embed, core_lead * grad_mix, read_full, forces)]
    energies, grad_embed, grad_mix, read_full, forces = (
        v + lax.ppermute(v, "section", [(0, 1), (1, 0)]) for v in chip_sums
    )
    energies, grad_embed, grad_mix, read_full = ring_sum((energies, grad_embed, grad_mix, read_full))
    return (
        energies,
        -forces,
        grad_embed,
        grad_head[None],
        grad_env[None],
        grad_mix,
        grad_in[None],
        grad_out[None],
        read_full,
    )


CHUNKS = (128, 192, 160)
PLAN = (
    (0, 0, 256, 2, 1), (0, 256, 256, 1, 2), (1, 0, 640, 1, 2), (1, 640, 640, 1, 2), (2, 0, 608, 2, 1),
    (2, 608, 608, 1, 2),
)
EARLY = (0, 1)
ORDER = (
    0, 2, 4, 5, 2, 1, 2, 4, 3, 1, 5, 0, 4, 3, 2, 5, 1, 3, 4, 2, 5, 3, 0, 5, 3, 4, 2, 1, 5, 0, 3, 4,
)
LANES = 128
F32 = jnp.float32
BF16 = jnp.bfloat16
BESSEL_SCALE = (2.0 / CUTOFF) ** 0.5
ANGLE = 3.141592653589793 / CUTOFF


def dot_nn(left, right):
    return jnp.dot(left, right, preferred_element_type=F32)


def dot_nt(left, right):
    return lax.dot_general(left, right, (((1,), (1,)), ((), ())), preferred_element_type=F32)


def dot_tn(left, right):
    return lax.dot_general(left, right, (((0,), (0,)), ((), ())), preferred_element_type=F32)


def split_two(value):
    high = value.astype(BF16)
    return high, (value - high.astype(F32)).astype(BF16)


def split_three(value):
    high = value.astype(BF16)
    rest = value - high.astype(F32)
    middle = rest.astype(BF16)
    return high, middle, (rest - middle.astype(F32)).astype(BF16)


def six_pass(left, right):
    rows = left.shape[0]
    high, middle, low = split_three(left)
    three = dot_nn(jnp.concatenate([high, middle, low], axis=0), right[0])
    two = dot_nn(jnp.concatenate([high, middle], axis=0), right[1])
    small = three[2 * rows :] + two[rows:] + dot_nn(high, right[2])
    return three[:rows] + (three[rows : 2 * rows] + two[:rows] + small)


def three_pass(dot, left, right):
    rows = left.shape[0]
    high, low = split_two(left)
    both = dot(jnp.concatenate([high, low], axis=0), right[0])
    return both[:rows] + both[rows:] + dot(high, right[1])


def three_pass_tn(left, right):
    left_high, left_low = split_two(left)
    right_high, right_low = split_two(right)
    return dot_tn(
        jnp.concatenate([left_high, left_low, left_high], axis=0),
        jnp.concatenate([right_high, right_high, right_low], axis=0),
    )


def sigmoid(value):
    return 1.0 / (1.0 + jnp.exp(-value))


def order_of(component):
    return 0 if component == 0 else (1 if component < 4 else 2)


def same_sum(same, parts):
    high, middle, low = split_three(jnp.concatenate(parts, axis=1))
    summed = dot_nn(same, high) + (dot_nn(same, middle) + dot_nn(same, low))
    return [summed[:, LANES * m : LANES * (m + 1)] for m in range(len(parts))]


def place_columns(columns, first, width=LANES):
    lane = lax.broadcasted_iota(jnp.int32, (columns[0].shape[0], width), 1)
    out = jnp.zeros((columns[0].shape[0], width), F32)
    for i, column in enumerate(columns):
        out = jnp.where(lane == first + i, column, out)
    return out


def waves(length):
    turn = length * ANGLE - 1.5707963267948966
    square = turn * turn
    even, odd, term_even, term_odd = 1.0, 1.0, 1.0, 1.0
    coefficients_even, coefficients_odd = [], []
    for n in range(1, 9):
        term_even = -term_even / ((2 * n - 1) * (2 * n))
        term_odd = -term_odd / ((2 * n) * (2 * n + 1))
        coefficients_even.append(term_even)
        coefficients_odd.append(term_odd)
    even = jnp.full_like(turn, coefficients_even[-1])
    odd = jnp.full_like(turn, coefficients_odd[-1])
    for n in range(6, -1, -1):
        even = even * square + coefficients_even[n]
        odd = odd * square + coefficients_odd[n]
    sines = {1: even * square + 1.0}
    cosines = {1: -turn * (odd * square + 1.0)}
    for total, left, right in ((2, 1, 1), (3, 2, 1), (4, 2, 2), (5, 4, 1), (6, 4, 2), (7, 4, 3), (8, 4, 4)):
        sines[total] = sines[left] * cosines[right] + cosines[left] * sines[right]
        cosines[total] = cosines[left] * cosines[right] - sines[left] * sines[right]
    return [sines[k] for k in range(1, 9)], [cosines[k] for k in range(1, 9)]


def edge_values(edges, key_row, first, rows, full):
    block = edges[first : first + rows, :]
    vector = [block[:, i : i + 1] for i in range(3)]
    live = block[:, 6:7]
    squares = vector[0] * vector[0] + vector[1] * vector[1] + vector[2] * vector[2]
    length = jnp.sqrt(jnp.maximum(squares, 0.25))
    ux, uy, uz = (v / length for v in vector)
    ratio = jnp.minimum(length / CUTOFF, 1.0)
    second = ratio * ratio
    sixth = second * second * second
    envelope = (1.0 - 28.0 * sixth + 48.0 * (sixth * ratio) - 21.0 * (sixth * second)) * live
    harmonics = [
        jnp.ones_like(ux),
        ROOT_THREE * ux,
        ROOT_THREE * uy,
        ROOT_THREE * uz,
        ROOT_FIFTEEN * ux * uy,
        ROOT_FIFTEEN * uy * uz,
        0.5 * ROOT_FIVE * (3.0 * uz * uz - 1.0),
        ROOT_FIFTEEN * ux * uz,
        0.5 * ROOT_FIFTEEN * (ux * ux - uy * uy),
    ]
    same = jnp.where(block[:, 5:6] == key_row, 1.0, 0.0).astype(BF16)
    g = dict(
        env=envelope, harm=harmonics, same=same, squares=squares, length=length, ratio=ratio,
        unit=(ux, uy, uz), live=live, group=block[:, 7:8],
    )
    if full:
        sines, g["cosines"] = waves(length)
        g["bessel"] = [BESSEL_SCALE * value / length for value in sines]
        lane = lax.broadcasted_iota(jnp.int32, (rows, 16), 1).astype(F32)
        kinds = jnp.where(
            lane < NSPEC,
            jnp.where(block[:, 3:4] == lane, live, 0.0),
            jnp.where(block[:, 4:5] + NSPEC == lane, live, 0.0),
        )
        g["feat"] = kinds + place_columns(g["bessel"], 2 * NSPEC, 16)
    return g


def vector_pull(g, d_bessel, d_harm, d_envelope):
    ux, uy, uz = g["unit"]
    length, ratio = g["length"], g["ratio"]
    dx = ROOT_THREE * d_harm[1] + ROOT_FIFTEEN * (uy * d_harm[4] + uz * d_harm[7] + ux * d_harm[8])
    dy = ROOT_THREE * d_harm[2] + ROOT_FIFTEEN * (ux * d_harm[4] + uz * d_harm[5] - uy * d_harm[8])
    dz = (
        ROOT_THREE * d_harm[3]
        + ROOT_FIFTEEN * (uy * d_harm[5] + ux * d_harm[7])
        + (3.0 * ROOT_FIVE) * uz * d_harm[6]
    )
    left = 1.0 - ratio
    fourth = (ratio * ratio) * (ratio * ratio)
    d_length = (-168.0 / CUTOFF) * (fourth * ratio) * (left * left) * g["live"] * d_envelope
    d_length = d_length - (dx * ux + dy * uy + dz * uz) / length
    for k in range(NBES):
        slope = (BESSEL_SCALE * ANGLE * (k + 1)) * g["cosines"][k] - g["bessel"][k]
        d_length = d_length + d_bessel[k] * (slope / length)
    bound = jnp.where(g["squares"] > 0.25, 1.0, jnp.where(g["squares"] == 0.25, 0.5, 0.0))
    d_length = d_length * bound
    return [d / length + d_length * u for d, u in ((dx, ux), (dy, uy), (dz, uz))]


def env_terms(g, weight):
    scaled = ENV_SCALE * g["env"] * weight
    return same_sum(g["same"], [y * scaled for y in g["harm"]])


def pack_scalars(tensor, env):
    sums = [tensor[0] * env[0], tensor[1] * env[1], tensor[4] * env[4]]
    for m in (2, 3):
        sums[1] = sums[1] + tensor[m] * env[m]
    for m in (5, 6, 7, 8):
        sums[2] = sums[2] + tensor[m] * env[m]
    return jnp.concatenate([sums[0] + pltpu.roll(sums[1], 64, 1), sums[2]], axis=1)


def unpack_scalars(packed):
    first = packed[:, :LANES]
    return [first, pltpu.roll(first, 64, 1), packed[:, LANES:]]


def swap_order(lead, left, right):
    return jnp.where(lead, left, right), jnp.where(lead, right, left)


def env_pull(g, weight, d_env):
    d_terms = same_sum(g["same"], d_env)
    d_weight, d_harm, inner = None, [], None
    for m in range(9):
        part = g["harm"][m] * d_terms[m]
        d_weight = part if m == 0 else d_weight + part
        d_harm.append(jnp.sum(weight * d_terms[m], axis=1, keepdims=True))
        step = g["harm"][m] * d_harm[m]
        inner = step if m == 0 else inner + step
    scale = ENV_SCALE * g["env"]
    return scale * d_weight, [scale * d for d in d_harm], ENV_SCALE * inner


class Fetched:
    def __init__(self, source, buffer, semaphore):
        rows = source.shape[0]
        self.buffer, self.shape = buffer, buffer.shape
        target = buffer if rows == buffer.shape[0] else buffer.at[pl.ds(0, rows)]
        self.copy = pltpu.make_async_copy(source, target, semaphore)
        self.copy.start()
        self.arrived, self.pieces = False, {}
        if rows < buffer.shape[0]:
            buffer[rows:, :] = jnp.zeros((buffer.shape[0] - rows, buffer.shape[1]), F32)

    def __getitem__(self, where):
        if not self.arrived:
            self.copy.wait()
            self.arrived = True
        return self.buffer[where]

    def split(self, parts):
        if parts not in self.pieces:
            value = self[...]
            self.pieces[parts] = split_three(value) if parts == 3 else split_two(value)
        return self.pieces[parts]


class Stored:
    def __init__(self, target, buffer, semaphore):
        self.target, self.buffer, self.semaphore = target, buffer, semaphore
        self.shape, self.copy = buffer.shape, None

    def __setitem__(self, where, value):
        self.buffer[where] = value
        if where is Ellipsis:
            self.send()

    def __getitem__(self, where):
        return self.buffer[where]

    def send(self):
        self.copy = pltpu.make_async_copy(self.buffer, self.target, self.semaphore)
        self.copy.start()


def forward_pair(value, own, other):
    return [six_pass(value, own.split(3)), six_pass(value, other.split(3))]


def backward_pair(value, own, other, parts):
    return [three_pass(dot_nt, value, own.split(parts)), three_pass(dot_nt, value, other.split(parts))]


def first_forward(
    first, edges, key_row, lead_flag, embed,
    head_o, head_x, env_w, in_o, in_x, out_o, out_x,
    sent, soft_out, layer_in, slope_out, hidden,
):
    rows = sent.shape[0]
    lead = lead_flag[0:1, 0:1] > 0.5
    g = edge_values(edges, key_row[...], first, rows, True)
    pre = six_pass(g["feat"], split_three(embed[...]))
    soft = pre * sigmoid(pre)
    soft_out[...] = soft
    own, other = forward_pair(soft, head_o, head_x)
    latent = g["env"] * jnp.concatenate(swap_order(lead, own, other), axis=1)
    weight = six_pass(latent, env_w.split(3))
    env = env_terms(g, weight)
    scalars = pack_scalars([y * weight for y in g["harm"]], env)
    full = jnp.concatenate([latent, scalars], axis=1)
    layer_in[...] = full
    pre = jnp.concatenate(forward_pair(full, in_o, in_x), axis=1)
    gate = sigmoid(pre)
    slope_out[...] = gate * (1.0 + pre * (1.0 - gate))
    hid = pre * gate
    hidden[...] = hid
    half = hid.shape[1] // 2
    width = latent.shape[1]
    sent[:, :width] = (
        latent + six_pass(hid[:, :half], out_o.split(3)) + six_pass(hid[:, half:], out_x.split(3))
    )
    sent[:, width:] = weight
    sent.send()


def second_both(
    first, edges, key_row, mix, read, cot_row,
    arrived, env_w, in_o, in_x, out_o, out_x, head_o, head_x, env_wt,
    back, layer_in, d_pre_hidden, hidden, d_latent_out, latent_out, d_pre_read, d_weight_out,
    read_grad, mix_grad, energy_out,
):
    rows = back.shape[0]
    width = arrived.shape[1] - LANES
    half = width // 2
    g = edge_values(edges, key_row[...], first, rows, False)
    lane = lax.broadcasted_iota(jnp.int32, (rows, LANES), 1).astype(F32)
    group_hot = jnp.where(g["group"] == lane, g["live"], 0.0)
    cot = jnp.sum(group_hot * cot_row[...], axis=1, keepdims=True)
    mixes = [split_three(mix[i]) for i in range(3)]
    latent = arrived[:, :width]
    weight_first = arrived[:, width:]
    env_first = env_terms(g, weight_first)
    start = [y * weight_first for y in g["harm"]]
    coupled = [start[m] * env_first[0] + start[0] * env_first[m] for m in range(9)]
    members = ((0,), (1, 2, 3), (4, 5, 6, 7, 8))
    tensor = []
    for order in range(3):
        mixed = six_pass(jnp.concatenate([coupled[m] for m in members[order]], axis=0), mixes[order])
        tensor += [mixed[rows * i : rows * (i + 1)] for i in range(len(members[order]))]
    weight = six_pass(latent, env_w.split(3))
    env = env_terms(g, weight)
    full = jnp.concatenate([latent, pack_scalars(tensor, env)], axis=1)
    layer_in[...] = full
    pre = jnp.concatenate(forward_pair(full, in_o, in_x), axis=1)
    gate = sigmoid(pre)
    slope = gate * (1.0 + pre * (1.0 - gate))
    hid = pre * gate
    hidden[...] = hid
    latent_next = (
        latent + six_pass(hid[:, :half], out_o.split(3)) + six_pass(hid[:, half:], out_x.split(3))
    )
    latent_out[...] = latent_next
    pre_read = jnp.concatenate(forward_pair(latent_next, head_o, head_x), axis=1)
    gate = sigmoid(pre_read)
    soft = pre_read * gate
    line = read[...]
    inner = jnp.sum(soft * line, axis=1, keepdims=True)
    energy_out[...] = jnp.broadcast_to(
        jnp.sum(group_hot * (g["env"] * inner), axis=0, keepdims=True), energy_out.shape
    )
    scaled_cot = cot * g["env"]
    read_grad[...] = jnp.broadcast_to(
        jnp.sum(scaled_cot * soft, axis=0, keepdims=True), read_grad.shape
    )
    d_envelope = cot * inner
    d_read = scaled_cot * line * (gate * (1.0 + pre_read * (1.0 - gate)))
    d_pre_read[...] = d_read
    d_latent_out[...] = three_pass(dot_nt, d_read[:, :half], head_o.split(3)) + three_pass(
        dot_nt, d_read[:, half:], head_x.split(3)
    )
    d_hid = jnp.concatenate(backward_pair(d_latent_out[...], out_o, out_x, 3), axis=1)
    d_pre = d_hid * slope
    d_pre_hidden[...] = d_pre
    d_full = three_pass(dot_nt, d_pre[:, :half], in_o.split(3)) + three_pass(
        dot_nt, d_pre[:, half:], in_x.split(3)
    )
    d_scalars = unpack_scalars(d_full[:, width:])
    d_tensor = [d_scalars[order_of(m)] * env[m] for m in range(9)]
    d_env = [d_scalars[order_of(m)] * tensor[m] for m in range(9)]
    d_weight, d_harm, d_more = env_pull(g, weight, d_env)
    d_envelope = d_envelope + d_more
    d_weight_out[...] = d_weight
    back[:, :width] = (
        three_pass(dot_nn, d_weight_out[...], env_wt.split(2))
        + d_latent_out[...]
        + d_full[:, :width]
    )
    d_coupled = []
    for order in range(3):
        joined = jnp.concatenate([d_tensor[m] for m in members[order]], axis=0)
        mix_grad[order] = three_pass_tn(
            jnp.concatenate([coupled[m] for m in members[order]], axis=0), joined
        )
        mixed = three_pass(dot_nt, joined, mixes[order])
        d_coupled += [mixed[rows * i : rows * (i + 1)] for i in range(len(members[order]))]
    mix_grad.send()
    d_env_first = [d_coupled[m] * start[0] for m in range(9)]
    d_start = [d_coupled[m] * env_first[0] for m in range(9)]
    for m in range(9):
        d_env_first[0] = d_env_first[0] + d_coupled[m] * start[m]
        d_start[0] = d_start[0] + d_coupled[m] * env_first[m]
    d_first, d_harm_first, d_more = env_pull(g, weight_first, d_env_first)
    for m in range(9):
        d_first = d_first + g["harm"][m] * d_start[m]
        d_harm[m] = (
            d_harm[m]
            + d_harm_first[m]
            + jnp.sum(weight_first * d_start[m], axis=1, keepdims=True)
        )
    d_envelope = d_envelope + d_more
    back[:, width:] = d_first + place_columns(d_harm + [d_envelope], 64)
    back.send()


def first_backward(
    first, edges, key_row, lead_flag, embed,
    layer_in, env_w, arrived, out_o, out_x, slope_in, in_o, in_x, env_wt, head_o, head_x,
    d_vector, d_head, d_pre_hidden, d_weight_out, embed_grad,
):
    rows = arrived.shape[0]
    width = arrived.shape[1] - LANES
    half = width // 2
    lead = lead_flag[0:1, 0:1] > 0.5
    g = edge_values(edges, key_row[...], first, rows, True)
    embed_pair = split_two(embed[...])
    latent = layer_in[:, :width]
    weight = three_pass(dot_nn, latent, env_w.split(2))
    env = env_terms(g, weight)
    extra = arrived[:, width:]
    lane = lax.broadcasted_iota(jnp.int32, extra.shape, 1)
    d_weight = jnp.where(lane < 64, extra, 0.0)
    d_harm = [extra[:, 64 + m : 65 + m] for m in range(9)]
    d_envelope = extra[:, 73:74]
    d_hid = jnp.concatenate(backward_pair(arrived[:, :width], out_o, out_x, 2), axis=1)
    d_pre = d_hid * slope_in[...]
    d_pre_hidden[...] = d_pre
    d_full = three_pass(dot_nt, d_pre[:, :half], in_o.split(2)) + three_pass(
        dot_nt, d_pre[:, half:], in_x.split(2)
    )
    d_scalars = unpack_scalars(d_full[:, width:])
    d_start = [d_scalars[order_of(m)] * env[m] for m in range(9)]
    d_env = [d_scalars[order_of(m)] * (g["harm"][m] * weight) for m in range(9)]
    d_more_weight, d_more_harm, d_more = env_pull(g, weight, d_env)
    d_weight = d_weight + d_more_weight
    d_envelope = d_envelope + d_more
    for m in range(9):
        d_weight = d_weight + g["harm"][m] * d_start[m]
        d_harm[m] = (
            d_harm[m] + d_more_harm[m] + jnp.sum(weight * d_start[m], axis=1, keepdims=True)
        )
    d_weight_out[...] = d_weight
    d_latent = (
        three_pass(dot_nn, d_weight_out[...], env_wt.split(2))
        + arrived[:, :width]
        + d_full[:, :width]
    )
    d_own, d_other = swap_order(lead, d_latent[:, :half], d_latent[:, half:])
    d_head[:, :half] = g["env"] * d_own
    d_head[:, half:] = g["env"] * d_other
    d_head.send()
    d_soft = three_pass(dot_nt, d_own, head_o.split(2)) + three_pass(dot_nt, d_other, head_x.split(2))
    pre = three_pass(dot_nn, g["feat"], embed_pair)
    gate = sigmoid(pre)
    d_envelope = d_envelope + jnp.sum(pre * gate * d_soft, axis=1, keepdims=True)
    d_pre = g["env"] * d_soft * (gate * (1.0 + pre * (1.0 - gate)))
    d_feat = three_pass(dot_nt, d_pre, embed_pair)
    embed_grad[...] = three_pass_tn(g["feat"], d_pre)
    d_bessel = [d_feat[:, 2 * NSPEC + k : 2 * NSPEC + 1 + k] for k in range(NBES)]
    d_vector[...] = place_columns(vector_pull(g, d_bessel, d_harm, d_envelope), 0)


def outer_sum(split_left, chosen, *refs):
    count = len(CHUNKS)
    extra = len(refs) > 4 * count + 8
    kinds = 3 if extra else 2
    sources = [
        [refs[(kinds * side + i) * count : (kinds * side + i + 1) * count] for i in range(kinds)]
        for side in range(2)
    ]
    rest = refs[2 * kinds * count :]
    outs = [Stored(rest[i], rest[kinds + i], rest[-1].at[i]) for i in range(kinds)]
    buffers = rest[2 * kinds : 3 * kinds]
    semaphores = rest[-2]

    def copies(side):
        for i in range(kinds):
            start = 0
            for k, source in enumerate(sources[side][i]):
                rows, columns = source.shape[0], buffers[i].shape[1]
                yield pltpu.make_async_copy(
                    source.at[:, pl.ds(0, columns)],
                    buffers[i].at[pl.ds(start, rows)],
                    semaphores.at[i * count + k],
                )
                start += rows

    for side in range(2):

        @pl.when(chosen[0] == side)
        def _(side=side):
            for copy in copies(side):
                copy.start()

    for copy in copies(0):
        copy.wait()
    left_high, left_low = split_two(buffers[0][...])
    right_high, right_low = split_two(buffers[1][...])
    left = jnp.concatenate([left_high, left_low, left_high], axis=0)
    right = jnp.concatenate([right_high, right_high, right_low], axis=0)
    if split_left:
        half = left.shape[1] // 2
        outs[1][...] = dot_tn(left[:, half:], right)
        outs[0][...] = dot_tn(left[:, :half], right)
    else:
        half = right.shape[1] // 2
        outs[1][...] = dot_tn(left, right[:, half:])
        outs[0][...] = dot_tn(left, right[:, :half])
    if extra:
        right_high, right_low = split_two(buffers[2][...])
        right = jnp.concatenate([right_high, right_high, right_low], axis=0)
        outs[2][...] = dot_tn(left[:, : outs[2].shape[0]], right)
    for out in outs:
        out.copy.wait()


def on_core(body, outs, flops, args, fetched, chosen):
    here = pl.BlockSpec(memory_space=pltpu.VMEM)
    there = pl.BlockSpec(memory_space=pl.ANY)
    pad = 2 * LANES
    tall = [(m.shape[0] + pad - 1) // pad * pad if m.shape[0] > pad else m.shape[0] for m in fetched]
    scratch = [pltpu.VMEM((rows, m.shape[1]), F32) for rows, m in zip(tall, fetched)]
    scratch += [pltpu.VMEM(shape, F32) for shape in outs]
    scratch.append(pltpu.SemaphoreType.DMA((len(fetched),)))
    scratch.append(pltpu.SemaphoreType.DMA((len(outs),)))

    def guarded(flag, *refs):
        @pl.when(flag[0] == 1)
        def _():
            small, rest = refs[: len(args)], refs[len(args) :]
            sources, rest = rest[: len(fetched)], rest[len(fetched) :]
            targets, rest = rest[: len(outs)], rest[len(outs) :]
            buffers, rest = rest[: len(fetched)], rest[len(fetched) :]
            kept, (arrivals, departures) = rest[: len(outs)], rest[len(outs) :]
            inputs = [Fetched(s, b, arrivals.at[i]) for i, (s, b) in enumerate(zip(sources, buffers))]
            outputs = [Stored(t, b, departures.at[i]) for i, (t, b) in enumerate(zip(targets, kept))]
            body(*small, *inputs, *outputs)
            for output in outputs:
                output.copy.wait()

    return pl.pallas_call(
        guarded,
        out_shape=tuple(jax.ShapeDtypeStruct(shape, F32) for shape in outs),
        in_specs=[pl.BlockSpec(memory_space=pltpu.SMEM)] + [here] * len(args) + [there] * len(fetched),
        out_specs=tuple(there for _ in outs),
        scratch_shapes=scratch,
        compiler_params=pltpu.CompilerParams(vmem_limit_bytes=60 * 2**20),
        cost_estimate=pl.CostEstimate(flops=flops, bytes_accessed=16 * 2**20, transcendentals=0),
    )(chosen, *args, *fetched)


def outer_call(split_left, outs, widths, flops, chosen, first, second):
    there = pl.BlockSpec(memory_space=pl.ANY)
    args = [array for side in (first, second) for factor in side for array in factor]
    return pl.pallas_call(
        partial(outer_sum, split_left),
        out_shape=tuple(jax.ShapeDtypeStruct(shape, F32) for shape in outs),
        in_specs=[pl.BlockSpec(memory_space=pltpu.SMEM)] + [there] * len(args),
        out_specs=tuple(there for _ in outs),
        scratch_shapes=[pltpu.VMEM(shape, F32) for shape in outs]
        + [pltpu.VMEM((sum(CHUNKS), w), F32) for w in widths]
        + [
            pltpu.SemaphoreType.DMA((len(widths) * len(CHUNKS),)),
            pltpu.SemaphoreType.DMA((len(outs),)),
        ],
        compiler_params=pltpu.CompilerParams(vmem_limit_bytes=60 * 2**20),
        cost_estimate=pl.CostEstimate(flops=flops, bytes_accessed=16 * 2**20, transcendentals=0),
    )(chosen, *args)


def gather_blocks(value):
    count = lax.axis_size("edge")
    if count & (count - 1) or count > 8:
        return lax.all_gather(value, "edge", axis=0)
    index = lax.axis_index("edge")
    out = value[None]
    step = 1
    while step < count:
        got = lax.ppermute(out, "edge", [(i, i ^ step) for i in range(count)])
        low = (index // step) % 2 == 0
        out = jnp.where(low, jnp.concatenate([out, got]), jnp.concatenate([got, out]))
        step *= 2
    return out


def prefix_in_rows(flags):
    rows, length = flags.shape
    pieces = flags.reshape(rows, length // LANES, LANES)
    upper = (jnp.arange(LANES)[:, None] <= jnp.arange(LANES)[None, :]).astype(F32)
    inner = jnp.einsum("rkl,lm->rkm", pieces, upper, precision=HIGHEST)
    totals = inner[:, :, -1]
    count = length // LANES
    before = (jnp.arange(count)[:, None] < jnp.arange(count)[None, :]).astype(F32)
    offsets = jnp.dot(totals, before, precision=HIGHEST)
    return (inner + offsets[:, :, None]).reshape(rows, length)


def pack_edges(atoms, vectors, species, centres, mask, structures, out):
    count = centres.shape[1]
    for b in range(centres.shape[0]):
        span = slice(b * count, (b + 1) * count)
        vector = vectors[b]
        out[0:3, span] = vector
        out[3:5, span] = species[b].astype(F32)
        out[5:6, span] = (centres[b : b + 1, :] + b * atoms).astype(F32)
        squares = jnp.maximum(jnp.sum(vector * vector, axis=0, keepdims=True), 0.25)
        near = jnp.where(jnp.sqrt(squares) / CUTOFF < 1.0, 1.0, 0.0)
        out[6:7, span] = jnp.where(mask[b : b + 1, :] > 0, near, 0.0)
        out[7:8, span] = (structures[b : b + 1, :] + b * STRUCTS).astype(F32)


def plan_edges(edge_vectors, edge_species, centres, edge_mask, structures):
    batch_count, _, edge_count = edge_vectors.shape
    blocks = lax.axis_size("edge")
    block = lax.axis_index("edge")
    core = lax.axis_index("mp")
    atoms = blocks * ATOM_DEV
    per_block = batch_count * edge_count
    raw = pl.pallas_call(
        partial(pack_edges, atoms), out_shape=jax.ShapeDtypeStruct((8, per_block), F32)
    )(edge_vectors, edge_species, centres, edge_mask, structures)
    gathered = gather_blocks(raw)
    keys = gathered[:, 5].reshape(blocks, batch_count, edge_count)
    alive = gathered[:, 6].reshape(blocks, batch_count, edge_count)
    local = keys - (jnp.arange(batch_count) * atoms)[None, :, None].astype(F32)
    degree = jnp.sum(
        jnp.where(
            local.transpose(1, 0, 2).reshape(batch_count, 1, -1)
            == jnp.arange(atoms, dtype=F32)[None, :, None],
            alive.transpose(1, 0, 2).reshape(batch_count, 1, -1),
            0.0,
        ),
        axis=2,
    )
    spans = batch_count * ATOM_DEV
    degree = degree.reshape(batch_count, blocks, ATOM_DEV).transpose(1, 0, 2).reshape(blocks, spans)
    upper = (jnp.arange(spans)[:, None] <= jnp.arange(spans)[None, :]).astype(F32)
    upto = jnp.dot(degree, upper, precision=HIGHEST)
    start = jnp.zeros((blocks, 1), F32)
    starts = [start]
    for size in CHUNKS:
        for _ in range(2):
            start = jnp.max(jnp.where(upto <= start + size, jnp.maximum(upto, start), start), axis=1, keepdims=True)
            starts.append(start)
    fits = jnp.all(starts[-1] >= upto[:, -1:])
    starts = jnp.concatenate(starts[:-1], axis=1)
    own_before = (upto - degree)[block]
    bin_of = jnp.sum((own_before[:, None] >= starts[block][None, 1:]).astype(F32), axis=1)
    padded = jnp.concatenate([jnp.zeros_like(gathered[:1]), gathered, jnp.zeros_like(gathered[:1])])
    window = lax.dynamic_slice_in_dim(padded, block, 3, 0)
    flat = window.transpose(1, 0, 2).reshape(8, 3 * per_block)
    position = jnp.arange(3 * per_block)
    batch_flat = (position % per_block) // edge_count
    spot = flat[5] - (batch_flat * atoms + block * ATOM_DEV).astype(F32)
    mine = (spot >= 0) & (spot < ATOM_DEV) & (flat[6] > 0.5)
    slot = jnp.where(mine, spot + (batch_flat * ATOM_DEV).astype(F32), -1.0)
    chosen = jnp.sum(
        jnp.where(jnp.arange(spans, dtype=F32)[:, None] == slot[None, :], bin_of[:, None], 0.0), axis=0
    )
    wanted = 2 * jnp.arange(len(CHUNKS)) + core
    picked = (chosen[None, :] == wanted[:, None].astype(F32)) & mine[None, :]
    rank = prefix_in_rows(picked.astype(F32)) - 1.0
    offsets = [sum(CHUNKS[:k]) for k in range(len(CHUNKS))]
    place = jnp.sum(
        jnp.where(picked, rank + jnp.array(offsets, F32)[:, None], 0.0), axis=0
    ) - (1.0 - jnp.sum(picked.astype(F32), axis=0))
    total = sum(CHUNKS)
    hot = (place[None, :] == jnp.arange(total, dtype=F32)[:, None]).astype(F32)
    edges = lax.dot_general(hot, flat, (((1,), (1,)), ((), ())), precision=HIGHEST)
    return fits, edges, place


def tied(first, *others):
    return lax.optimization_barrier((first, others))[0]


def hop(value, distance):
    return lax.ppermute(value, "edge", [(i, i ^ distance) for i in range(8)])


def halves(value, second):
    half = value.shape[0] // 2
    kept = lax.dynamic_slice_in_dim(value, second * half, half, 0)
    return kept, lax.dynamic_slice_in_dim(value, (1 - second) * half, half, 0)


def joined(kept, got, second):
    return jnp.where(second == 0, jnp.concatenate([kept, got]), jnp.concatenate([got, kept]))


def sum_steps(value, outer_hop, inner_hop, wait):
    index = lax.axis_index("edge")
    seconds = {1: index % 2, 2: ((index // 2) ^ (index // 4)) % 2}
    kept, given = halves(value, seconds[outer_hop])
    given = wait(given)
    got = hop(given, outer_hop)
    yield given
    kept, given = halves(kept + wait(got), seconds[inner_hop])
    got = hop(given, inner_hop)
    yield given
    part = kept + wait(got)
    got = hop(part, 6)
    yield part
    part = part + wait(got)
    got = hop(part, inner_hop)
    yield part
    part = joined(part, wait(got), seconds[inner_hop])
    half = part.shape[0]
    got = hop(part, outer_hop)
    yield part
    yield [(part, seconds[outer_hop] * half), (wait(got), (1 - seconds[outer_hop]) * half)]


class BlockSums:
    def __init__(self, plan):
        self.plan, self.steps, self.sums, self.moment = plan, {}, {}, None

    def wait(self, value):
        return value if self.moment is None else tied(value, self.moment)

    def advance(self, matrices, order):
        for piece in order:
            which, first, rows, outer_hop, inner_hop = self.plan[piece]
            if piece not in self.steps:
                value = lax.slice_in_dim(matrices[which], first, first + rows, axis=0)
                self.steps[piece] = sum_steps(value, outer_hop, inner_hop, self.wait)
            given = next(self.steps[piece])
            if isinstance(given, list):
                total = self.sums.get(which, jnp.zeros_like(matrices[which]))
                for part, start in given:
                    total = lax.dynamic_update_slice_in_dim(total, part, first + start, 0)
                self.sums[which] = total
                given = given[1][0]
            self.moment = given


def fast_device(edges, place, others, args):
    (
        edge_vectors, edge_species, centres, edge_mask, structures, energy_cot, embed_in,
        section_head, env_weight, mix_weight, w_in, w_out, read_weight,
    ) = args
    is_first = lax.axis_index("section") == 0
    core = lax.axis_index("mp")
    width = section_head.shape[1]
    half = section_head.shape[2]
    batch_count, _, edge_count = edge_vectors.shape
    chan_count = mix_weight.shape[1]
    gap = LANES - chan_count
    read_left, read_right = read_weight[:half], read_weight[half:]
    read_line = jnp.where(
        core == 0,
        jnp.concatenate([read_left, read_right]),
        jnp.concatenate([read_right, read_left]),
    )[None]
    cot_row = jnp.pad(energy_cot.reshape(1, -1), ((0, 0), (0, LANES - energy_cot.size)))
    lead_flag = jnp.full((8, LANES), 1.0, F32) * (core == 0).astype(F32)
    mix = jnp.pad(mix_weight, ((0, 0), (0, gap), (0, gap)))
    env_w = jnp.pad(env_weight[0], ((0, 0), (0, gap)))
    env_wt = env_w.T
    heads, ins, outs_w = (section_head[0], others[0]), (w_in[0], others[1]), (w_out[0], others[2])
    count = len(CHUNKS)
    offsets = [sum(CHUNKS[:k]) for k in range(count)]
    rows = [edges[o : o + m, 5].reshape(1, -1) for o, m in zip(offsets, CHUNKS)]
    layer_width = width + 2 * LANES

    first_flag = jnp.full((1,), 1, jnp.int32) * is_first.astype(jnp.int32)
    second_flag = 1 - first_flag
    saved, moved = [], []
    for k, m in enumerate(CHUNKS):
        outs = [(m, width + LANES), (m, width), (m, layer_width), (m, width), (m, width)]
        work = 12 * m * width * (3 * width + 384)
        result = on_core(
            partial(first_forward, offsets[k]), outs, work,
            (edges, rows[k], lead_flag, embed_in), (*heads, env_w, *ins, *outs_w), first_flag,
        )
        moved.append(shifted(result[0], "section", 1))
        saved.append(result[1:])
    seconds, returned, firsts = [], [], []
    for k, m in enumerate(CHUNKS):
        outs = [
            (m, width + LANES), (m, layer_width), (m, width), (m, width), (m, width),
            (m, width), (m, width), (m, LANES), (8, width), (3, LANES, LANES), (8, LANES),
        ]
        work = 18 * m * width * (3 * width + 384)
        seconds.append(
            on_core(
                partial(second_both, offsets[k]), outs, work,
                (edges, rows[k], mix, read_line, cot_row),
                (moved[k], env_w, *ins, *outs_w, *heads, env_wt), second_flag,
            )
        )
    outer_work = 6 * sum(CHUNKS) * width * width
    by_hand = lax.axis_size("edge") == 8
    sums = BlockSums(PLAN)
    for k, m in enumerate(CHUNKS):
        arrived = shifted(seconds[k][0], "section", -1)
        if k > 0:
            arrived = tied(arrived, firsts[k - 1][0])
        returned.append(arrived)
        if k == count - 1:
            out_own, out_other = outer_call(
                True, [(half, width)] * 2, (width, width), outer_work, second_flag,
                ([s[3] for s in saved], returned),
                ([s[3] for s in seconds], [s[4] for s in seconds]),
            )
            arrived = tied(arrived, out_other)
            grad_out = out_own + other_core(out_other)
            if by_hand:
                sums.advance([grad_out], EARLY)
        outs = [(m, LANES), (m, width), (m, width), (m, LANES), (16, width)]
        work = 9 * m * width * (3 * width + 384)
        firsts.append(
            on_core(
                partial(first_backward, offsets[k]), outs, work,
                (edges, rows[k], lead_flag, embed_in),
                (saved[k][1], env_w, arrived, *outs_w, saved[k][2], *ins, env_wt, *heads), first_flag,
            )
        )
    in_own, in_other, grad_env = outer_call(
        False, [(layer_width, half)] * 2 + [(width, LANES)], (layer_width, width, LANES), outer_work,
        sums.wait(second_flag),
        ([s[1] for s in saved], [f[2] for f in firsts], [f[3] for f in firsts]),
        ([s[1] for s in seconds], [s[2] for s in seconds], [s[7] for s in seconds]),
    )
    grad_in = in_own + other_core(in_other)
    if by_hand:
        sums.moment = (sums.moment, in_other)
        sums.advance([grad_out], EARLY)
    head_own, head_other = outer_call(
        False, [(width, half)] * 2, (width, width), outer_work, tied(second_flag, in_other, sums.moment),
        ([s[0] for s in saved], [f[1] for f in firsts]),
        ([s[5] for s in seconds], [s[6] for s in seconds]),
    )
    none = jnp.zeros((), F32)
    read_sum = sum(s[8][0] for s in seconds)
    read_sum = jnp.where(
        core == 0, read_sum, jnp.concatenate([read_sum[half:], read_sum[:half]])
    )
    mix_sum = sum(s[9] for s in seconds)[:, :chan_count, :chan_count].reshape(-1, width)
    energy_sum = sum(s[10][0] for s in seconds)
    embed_sum = sum(f[4] for f in firsts)
    small_second = jnp.concatenate(
        [read_sum[None], jnp.pad(energy_sum, (0, width - LANES))[None], mix_sum]
    )
    small_second = jnp.pad(small_second, ((0, 16 - small_second.shape[0]), (0, 0)))
    small = jnp.concatenate(
        [jnp.where(is_first, embed_sum, none), jnp.where(is_first, none, small_second)]
    )
    small = small + lax.ppermute(small, "section", [(0, 1), (1, 0)])
    small = jnp.concatenate([small, grad_env[:, :chan_count].reshape(-1, width)]).reshape(-1, half)
    head_own = jnp.concatenate([head_own, small])
    grad_head = head_own + other_core(jnp.concatenate([head_other, small]))
    total = sum(CHUNKS)
    hot = (place[None, :] == jnp.arange(total, dtype=F32)[:, None]).astype(F32)
    d_vectors = jnp.concatenate([f[0][:, :8] for f in firsts])
    spread = lax.dot_general(d_vectors, hot, (((0,), (0,)), ((), ())), precision=HIGHEST)[:3]
    spread = jnp.where(is_first, spread, none)
    if by_hand:
        matrices = [grad_out, grad_in, grad_head]
        sums.moment = (sums.moment, head_other, grad_in)
        sums.advance(matrices, ORDER[:8])
        spread = sums.wait(spread)
        spread = spread + other_core(spread)
        sums.advance(matrices, ORDER[8:16])
        spread = sums.wait(spread)
        sums.advance(matrices, ORDER[16:])
        grad_out, grad_in, grad_head = (sums.sums[i] for i in range(3))
    else:
        spread = spread + other_core(spread)
        grad_out, grad_in, grad_head = lax.psum((grad_out, grad_in, grad_head), "edge")
    per_block = batch_count * edge_count
    to_left, kept, to_right = (spread[:, i * per_block : (i + 1) * per_block] for i in range(3))
    forces = kept + shifted(to_right, "edge", 1) + shifted(to_left, "edge", -1)
    small = grad_head[width:].reshape(-1, width)
    grad_head = grad_head[:width]
    grad_embed, grad_read = small[:16], small[16]
    energies = small[17, : energy_cot.size].reshape(energy_cot.shape)
    grad_mix = small[18 : 18 + mix_sum.shape[0]].reshape(mix_weight.shape)
    grad_env = small[32:].reshape(width, chan_count)

    forces = jnp.where(is_first, forces, shifted(forces, "section", 1))
    forces = -forces.reshape(3, batch_count, edge_count).transpose(1, 0, 2)
    return (
        energies, forces, grad_embed, grad_head[None], grad_env[None], grad_mix,
        grad_in[None, : w_in.shape[1]], grad_out[None], grad_read,
    )


def per_device(*args):
    section_head, w_in, w_out = args[7], args[10], args[11]
    others = tuple(other_core(m[0]) for m in (section_head, w_in, w_out))
    fits, edges, place = plan_edges(*args[:5])
    results = fast_device(edges, place, others, args)

    def again(state):
        rest, _ = state
        held, rest = lax.optimization_barrier((args, rest))
        return rest - 1, general_device(*held)

    overflow = 1 - fits.astype(jnp.int32)
    return lax.while_loop(lambda state: state[0] > 0, again, (overflow, results))[1]


def solution(mesh):
    placed = (
        P(None, None, "edge"),
        P(None, None, "edge"),
        P(None, "edge"),
        P(None, "edge"),
        P(None, "edge"),
        P(),
        P(),
        P("section", None, "mp"),
        P("section", None, None),
        P(),
        P("section", None, "mp"),
        P("section", "mp", None),
        P(),
    )
    return jax.shard_map(
        per_device,
        mesh=mesh,
        in_specs=placed,
        out_specs=(
            P(),
            P(None, None, "edge"),
            P(),
            P("section", None, "mp"),
            P("section", None, None),
            P(),
            P("section", None, "mp"),
            P("section", "mp", None),
            P(),
        ),
        check_vma=False,
    )
```

```python
from functools import partial

import jax
import jax.numpy as jnp
from jax import lax
from jax.experimental import pallas as pl
from jax.experimental.pallas import tpu as pltpu
from jax.sharding import PartitionSpec as P

NBES = 8
NSPEC = 4
ATOM_DEV = 40
STRUCTS = 16


CUTOFF = 5.0
ENV_SCALE = 0.25
HIGHEST = lax.Precision.HIGHEST
ROOT_THREE = 1.7320508075688772
ROOT_FIVE = 2.23606797749979
ROOT_FIFTEEN = 3.872983346207417


def extended(block, sides, width):
    for axis, dim in sides:
        count = lax.axis_size(axis)
        forward = [(i, i + 1) for i in range(count - 1)]
        backward = [(target, source) for source, target in forward]
        low = lax.ppermute(
            lax.slice_in_dim(block, block.shape[dim] - width, None, axis=dim), axis, forward
        )
        high = lax.ppermute(lax.slice_in_dim(block, 0, width, axis=dim), axis, backward)
        block = jnp.concatenate([low, block, high], axis=dim)
    return block


def shifted(value, axis, steps):
    count = lax.axis_size(axis)
    first, last = (max(0, -steps), min(count, count - steps))
    return lax.ppermute(value, axis, [(source, source + steps) for source in range(first, last)])


def other_core(value):
    return lax.ppermute(value, "mp", [(0, 1), (1, 0)])


def ring_sum(values):
    count = lax.axis_size("edge")

    def step(_, state):
        moving, total = state
        moving = tuple(
            lax.ppermute(v, "edge", [(i, (i + 1) % count) for i in range(count)]) for v in moving
        )
        return moving, tuple(t + v for t, v in zip(total, moving))

    return lax.fori_loop(0, count - 1, step, (tuple(values), tuple(values)))[1]


def matmul(left, right):
    return jnp.dot(left, right, precision=HIGHEST, preferred_element_type=jnp.float32)


def geometry(vectors, edge_live):
    squares = jnp.maximum(jnp.sum(vectors * vectors, axis=0), 0.25)
    length = jnp.sqrt(squares)
    unit_x = vectors[0] / length
    unit_y = vectors[1] / length
    unit_z = vectors[2] / length
    edge_ratio = jnp.minimum(length / CUTOFF, 1.0)
    envelope = (
        1.0 - 28.0 * edge_ratio**6 + 48.0 * edge_ratio**7 - 21.0 * edge_ratio**8
    ) * edge_live
    orders = jnp.arange(1, NBES + 1).astype(jnp.float32)
    bessel = (
        jnp.sqrt(2.0 / CUTOFF)
        * jnp.sin(orders[None, :] * (jnp.pi / CUTOFF) * length[:, None])
        / length[:, None]
    )
    harmonics = jnp.stack(
        [
            jnp.ones_like(unit_x),
            ROOT_THREE * unit_x,
            ROOT_THREE * unit_y,
            ROOT_THREE * unit_z,
            ROOT_FIFTEEN * unit_x * unit_y,
            ROOT_FIFTEEN * unit_y * unit_z,
            0.5 * ROOT_FIVE * (3.0 * unit_z * unit_z - 1.0),
            ROOT_FIFTEEN * unit_x * unit_z,
            0.5 * ROOT_FIFTEEN * (unit_x * unit_x - unit_y * unit_y),
        ],
        axis=1,
    )
    return (harmonics, envelope, bessel)


def couple(edge_tensor, env_flat, mix_weight):
    chan_count = mix_weight.shape[1]
    own_tensor = edge_tensor.reshape(-1, 9, chan_count)
    env_tensor = env_flat.reshape(-1, 9, chan_count)
    paired = own_tensor * env_tensor
    scalars = jnp.concatenate(
        [paired[:, 0], jnp.sum(paired[:, 1:4], axis=1), jnp.sum(paired[:, 4:9], axis=1)], axis=1
    )
    coupled = own_tensor * env_tensor[:, 0:1] + own_tensor[:, 0:1] * env_tensor
    order_zero = jnp.einsum("emc,cd->emd", coupled[:, 0:1], mix_weight[0], precision=HIGHEST)
    order_one = jnp.einsum("emc,cd->emd", coupled[:, 1:4], mix_weight[1], precision=HIGHEST)
    order_two = jnp.einsum("emc,cd->emd", coupled[:, 4:9], mix_weight[2], precision=HIGHEST)
    updated = jnp.concatenate([order_zero, order_one, order_two], axis=1)
    return (scalars, updated.reshape(-1, 9 * chan_count))


def front(bessel, envelope, embed_in, head_local, kinds_hot):
    features = jnp.concatenate([kinds_hot, bessel], axis=1)
    return envelope[:, None] * matmul(jax.nn.silu(matmul(features, embed_in)), head_local)


def contribute(latent_full, harmonics, envelope, env_local, centre_hot):
    weight = matmul(latent_full, env_local)
    contribution = (
        (ENV_SCALE * envelope)[:, None, None] * harmonics[:, :, None] * weight[:, None, :]
    )
    flat_terms = contribution.reshape(weight.shape[0], -1)
    return (weight, matmul(centre_hot.T, flat_terms))


def tensor_step(tensor_full, env_window, weight, harmonics, mix_weight, centre_hot, is_first):
    start_tensor = (harmonics[:, :, None] * weight[:, None, :]).reshape(weight.shape[0], -1)
    edge_tensor = jnp.where(is_first, start_tensor, tensor_full)
    env_flat = matmul(centre_hot, env_window)
    return couple(edge_tensor, env_flat, mix_weight)


def perceptron(latent_full, scalars, in_local, out_local):
    hidden = jax.nn.silu(matmul(jnp.concatenate([latent_full, scalars], axis=1), in_local))
    return matmul(hidden, out_local)


def readout(latent_full, envelope, head_local, read_half):
    return envelope * matmul(jax.nn.silu(matmul(latent_full, head_local)), read_half)


def general_device(
    edge_vectors,
    edge_species,
    centres,
    edge_mask,
    structures,
    energy_cot,
    embed_in,
    section_head,
    env_weight,
    mix_weight,
    w_in,
    w_out,
    read_weight,
):
    section_index = lax.axis_index("section")
    core_index = lax.axis_index("mp")
    edge_index = lax.axis_index("edge")
    is_first = section_index == 0
    last_flag = (section_index == 1).astype(jnp.float32)
    batch_count = edge_vectors.shape[0]
    shard_width = w_out.shape[1]
    tensor_cols = 9 * env_weight.shape[2]
    tensor_half = tensor_cols // 2
    atoms_dev = ATOM_DEV
    head_local = section_head[0]
    env_local = env_weight[0]
    in_local = w_in[0]
    out_local = w_out[0]
    read_half = lax.dynamic_slice_in_dim(read_weight, core_index * shard_width, shard_width, 0)
    core_lead = (core_index == 0).astype(jnp.float32)
    edge_count = edge_vectors.shape[2]
    centre_slots = jnp.arange(3 * atoms_dev)
    labels = jnp.arange(STRUCTS)
    species_range = jnp.arange(NSPEC)
    batch_range = jnp.arange(batch_count)

    def reduce_rims(pieces):
        widened = extended(pieces, (("edge", 0),), atoms_dev)
        return (
            widened[:atoms_dev] + widened[2 * atoms_dev : 3 * atoms_dev] + widened[4 * atoms_dev :]
        )

    def window_rows(totals):
        return extended(totals, (("edge", 0),), atoms_dev)

    def collect(partial_rows):
        width = partial_rows.shape[1] // 2
        own = lax.dynamic_slice_in_dim(partial_rows, core_index * width, width, 1)
        return own + other_core(lax.dynamic_slice_in_dim(partial_rows, (1 - core_index) * width, width, 1))

    def both_halves(half):
        other = other_core(half)
        return jnp.where(
            core_index == 0,
            jnp.concatenate([half, other], axis=1),
            jnp.concatenate([other, half], axis=1),
        )

    def batch_data(batch_index):
        vectors = lax.dynamic_index_in_dim(edge_vectors, batch_index, 0, keepdims=False)
        kind_ids = lax.dynamic_index_in_dim(edge_species, batch_index, 0, keepdims=False)
        owners = lax.dynamic_index_in_dim(centres, batch_index, 0, keepdims=False)
        edge_live = lax.dynamic_index_in_dim(edge_mask, batch_index, 0, keepdims=False).astype(
            jnp.float32
        )
        groups = lax.dynamic_index_in_dim(structures, batch_index, 0, keepdims=False)
        kinds_hot = jnp.concatenate(
            [
                kind_ids[0][:, None] == species_range[None, :],
                kind_ids[1][:, None] == species_range[None, :],
            ],
            axis=1,
        ).astype(jnp.float32)
        local_slot = owners - (edge_index - 1) * atoms_dev
        centre_hot = (local_slot[:, None] == centre_slots[None, :]).astype(jnp.float32)
        group_hot = (groups[:, None] == labels[None, :]).astype(jnp.float32)
        return (vectors, edge_live, kinds_hot, centre_hot, group_hot)

    recv_latent = jnp.zeros((edge_count, shard_width), jnp.float32)
    recv_tensor = jnp.zeros((edge_count, tensor_half), jnp.float32)
    energies = jnp.zeros((batch_count, STRUCTS), jnp.float32)
    kept_state = []
    for step_index in range(batch_count + 1):
        batch_raw = step_index - section_index
        batch_index = jnp.clip(batch_raw, 0, batch_count - 1)
        is_valid = ((batch_raw >= 0) & (batch_raw < batch_count)).astype(jnp.float32)
        vectors, edge_live, kinds_hot, centre_hot, group_hot = batch_data(batch_index)
        harmonics, envelope, bessel = geometry(vectors, edge_live)
        latent_half = lax.cond(
            is_first,
            lambda: front(bessel, envelope, embed_in, head_local, kinds_hot),
            lambda: recv_latent,
        )
        latent_full, tensor_full = (
            both_halves(latent_half),
            both_halves(recv_tensor),
        )
        weight, part_sums = contribute(latent_full, harmonics, envelope, env_local, centre_hot)
        env_window = window_rows(reduce_rims(part_sums))
        scalars, updated = tensor_step(
            tensor_full, env_window, weight, harmonics, mix_weight, centre_hot, is_first
        )
        branch_out = perceptron(latent_full, scalars, in_local, out_local)
        summed = collect(branch_out)
        tensor_own = lax.dynamic_slice_in_dim(updated, core_index * tensor_half, tensor_half, 1)
        next_half = latent_half + summed
        recv_latent, recv_tensor = shifted((next_half, tensor_own), "section", 1)
        next_full = both_halves(next_half)
        edge_energy = readout(next_full, envelope, head_local, read_half)
        batch_slot = (batch_range == batch_index).astype(jnp.float32) * is_valid * last_flag
        energies = (
            energies
            + batch_slot[:, None] * jnp.dot(edge_energy, group_hot, precision=HIGHEST)[None, :]
        )
        kept_state.append((latent_full, tensor_full, env_window, next_full))
    kept_latent = jnp.stack([entry[0] for entry in kept_state])
    kept_tensor = jnp.stack([entry[1] for entry in kept_state])
    kept_window = jnp.stack([entry[2] for entry in kept_state])
    kept_next = jnp.stack([entry[3] for entry in kept_state])
    grad_head = jnp.zeros_like(head_local)
    grad_env = jnp.zeros_like(env_local)
    grad_in = jnp.zeros_like(in_local)
    grad_out = jnp.zeros_like(out_local)
    grad_mix = jnp.zeros_like(mix_weight)
    grad_embed = jnp.zeros_like(embed_in)
    grad_read = jnp.zeros_like(read_half)
    forces = jnp.zeros((batch_count, 3, edge_count), jnp.float32)
    recv_grad = jnp.zeros((edge_count, shard_width), jnp.float32)
    recv_tgrad = jnp.zeros((edge_count, tensor_half), jnp.float32)
    for step_index in range(batch_count + 1):
        batch_raw = step_index - 1 + section_index
        batch_index = jnp.clip(batch_raw, 0, batch_count - 1)
        is_valid = ((batch_raw >= 0) & (batch_raw < batch_count)).astype(jnp.float32)
        saved_index = jnp.clip(batch_raw + section_index, 0, batch_count)
        latent_full = lax.dynamic_index_in_dim(kept_latent, saved_index, 0, keepdims=False)
        tensor_full = lax.dynamic_index_in_dim(kept_tensor, saved_index, 0, keepdims=False)
        env_window = lax.dynamic_index_in_dim(kept_window, saved_index, 0, keepdims=False)
        next_full = lax.dynamic_index_in_dim(kept_next, saved_index, 0, keepdims=False)
        vectors, edge_live, kinds_hot, centre_hot, group_hot = batch_data(batch_index)
        (harmonics, envelope, bessel), geometry_pull = jax.vjp(
            partial(geometry, edge_live=edge_live), vectors
        )
        batch_cot = lax.dynamic_index_in_dim(energy_cot, batch_index, 0, keepdims=False)
        energy_rows = jnp.dot(group_hot, batch_cot, precision=HIGHEST) * (is_valid * last_flag)
        _, read_pull = jax.vjp(readout, next_full, envelope, head_local, read_half)
        d_next_read, d_env_read, g_head_read, g_read = read_pull(energy_rows)
        d_next_half = jnp.where(is_first, recv_grad, collect(d_next_read))
        d_out_full, d_updated = (
            both_halves(d_next_half),
            both_halves(recv_tgrad),
        )
        (weight, part_sums), contribute_pull = jax.vjp(
            partial(contribute, centre_hot=centre_hot), latent_full, harmonics, envelope, env_local
        )
        (scalars, updated), tensor_pull = jax.vjp(
            partial(tensor_step, centre_hot=centre_hot, is_first=is_first),
            tensor_full,
            env_window,
            weight,
            harmonics,
            mix_weight,
        )
        _, perceptron_pull = jax.vjp(perceptron, latent_full, scalars, in_local, out_local)
        d_latent_mlp, d_scalar_part, g_in, g_out = perceptron_pull(d_out_full)
        d_scalars = d_scalar_part + other_core(d_scalar_part)
        d_tensor, d_window, d_weight, d_harm_tensor, g_mix = tensor_pull((d_scalars, d_updated))
        d_parts = window_rows(reduce_rims(d_window))
        d_latent_env, d_harm_env, d_envelope_env, g_env = contribute_pull((d_weight, d_parts))
        d_latent_own = (
            collect(d_latent_mlp)
            + lax.dynamic_slice_in_dim(d_latent_env, core_index * shard_width, shard_width, 1)
            + d_next_half
        )
        d_tensor_own = lax.dynamic_slice_in_dim(d_tensor, core_index * tensor_half, tensor_half, 1)
        recv_grad, recv_tgrad = shifted((d_latent_own, d_tensor_own), "section", -1)

        def front_pull(cotangent):
            _, pull_back = jax.vjp(
                partial(front, kinds_hot=kinds_hot), bessel, envelope, embed_in, head_local
            )
            return pull_back(cotangent)

        def front_none(cotangent):
            return (
                jnp.zeros_like(bessel),
                jnp.zeros_like(envelope),
                jnp.zeros_like(embed_in),
                jnp.zeros_like(head_local),
            )

        d_bessel, d_envelope_front, g_embed, g_head_front = lax.cond(
            is_first, front_pull, front_none, d_latent_own
        )
        d_harmonics = core_lead * (d_harm_tensor + d_harm_env)
        d_envelope = core_lead * d_envelope_env + d_env_read + d_envelope_front
        d_vectors = geometry_pull((d_harmonics, d_envelope, d_bessel))[0]
        batch_slot = (batch_range == batch_index).astype(jnp.float32) * is_valid
        forces = forces + batch_slot[:, None, None] * d_vectors[None]
        grad_head = grad_head + is_valid * (g_head_read + g_head_front)
        grad_env = grad_env + is_valid * g_env
        grad_in = grad_in + is_valid * g_in
        grad_out = grad_out + is_valid * g_out
        grad_mix = grad_mix + is_valid * g_mix
        grad_embed = grad_embed + is_valid * g_embed
        grad_read = grad_read + is_valid * g_read
    grad_head, grad_env, grad_in, grad_out = ring_sum((grad_head, grad_env, grad_in, grad_out))
    read_full = lax.dynamic_update_slice_in_dim(
        jnp.zeros_like(read_weight), grad_read, core_index * shard_width, 0
    )
    chip_sums = [v + other_core(v) for v in (energies, grad_embed, core_lead * grad_mix, read_full, forces)]
    energies, grad_embed, grad_mix, read_full, forces = (
        v + lax.ppermute(v, "section", [(0, 1), (1, 0)]) for v in chip_sums
    )
    energies, grad_embed, grad_mix, read_full = ring_sum((energies, grad_embed, grad_mix, read_full))
    return (
        energies,
        -forces,
        grad_embed,
        grad_head[None],
        grad_env[None],
        grad_mix,
        grad_in[None],
        grad_out[None],
        read_full,
    )


CHUNKS = (128, 192, 160)
PLAN = (
    (0, 0, 256, 2, 1), (0, 256, 256, 1, 2), (1, 0, 640, 1, 2), (1, 640, 640, 1, 2), (2, 0, 608, 2, 1),
    (2, 608, 608, 1, 2),
)
EARLY = (0, 1)
ORDER = (
    0, 2, 4, 5, 2, 1, 2, 4, 3, 1, 5, 0, 4, 3, 2, 5, 1, 3, 4, 2, 5, 3, 0, 5, 3, 4, 2, 1, 5, 0, 3, 4,
)
LANES = 128
F32 = jnp.float32
BF16 = jnp.bfloat16
BESSEL_SCALE = (2.0 / CUTOFF) ** 0.5
ANGLE = 3.141592653589793 / CUTOFF


def dot_nn(left, right):
    return jnp.dot(left, right, preferred_element_type=F32)


def dot_nt(left, right):
    return lax.dot_general(left, right, (((1,), (1,)), ((), ())), preferred_element_type=F32)


def dot_tn(left, right):
    return lax.dot_general(left, right, (((0,), (0,)), ((), ())), preferred_element_type=F32)


def split_two(value):
    high = value.astype(BF16)
    return high, (value - high.astype(F32)).astype(BF16)


def split_three(value):
    high = value.astype(BF16)
    rest = value - high.astype(F32)
    middle = rest.astype(BF16)
    return high, middle, (rest - middle.astype(F32)).astype(BF16)


def six_pass(left, right):
    rows = left.shape[0]
    high, middle, low = split_three(left)
    three = dot_nn(jnp.concatenate([high, middle, low], axis=0), right[0])
    two = dot_nn(jnp.concatenate([high, middle], axis=0), right[1])
    small = three[2 * rows :] + two[rows:] + dot_nn(high, right[2])
    return three[:rows] + (three[rows : 2 * rows] + two[:rows] + small)


def three_pass(dot, left, right):
    rows = left.shape[0]
    high, low = split_two(left)
    both = dot(jnp.concatenate([high, low], axis=0), right[0])
    return both[:rows] + both[rows:] + dot(high, right[1])


def three_pass_tn(left, right):
    left_high, left_low = split_two(left)
    right_high, right_low = split_two(right)
    return dot_tn(
        jnp.concatenate([left_high, left_low, left_high], axis=0),
        jnp.concatenate([right_high, right_high, right_low], axis=0),
    )


def sigmoid(value):
    return 1.0 / (1.0 + jnp.exp(-value))


def order_of(component):
    return 0 if component == 0 else (1 if component < 4 else 2)


def same_sum(same, parts):
    high, middle, low = split_three(jnp.concatenate(parts, axis=1))
    summed = dot_nn(same, high) + (dot_nn(same, middle) + dot_nn(same, low))
    return [summed[:, LANES * m : LANES * (m + 1)] for m in range(len(parts))]


def place_columns(columns, first, width=LANES):
    lane = lax.broadcasted_iota(jnp.int32, (columns[0].shape[0], width), 1)
    out = jnp.zeros((columns[0].shape[0], width), F32)
    for i, column in enumerate(columns):
        out = jnp.where(lane == first + i, column, out)
    return out


def waves(length):
    turn = length * ANGLE - 1.5707963267948966
    square = turn * turn
    even, odd, term_even, term_odd = 1.0, 1.0, 1.0, 1.0
    coefficients_even, coefficients_odd = [], []
    for n in range(1, 9):
        term_even = -term_even / ((2 * n - 1) * (2 * n))
        term_odd = -term_odd / ((2 * n) * (2 * n + 1))
        coefficients_even.append(term_even)
        coefficients_odd.append(term_odd)
    even = jnp.full_like(turn, coefficients_even[-1])
    odd = jnp.full_like(turn, coefficients_odd[-1])
    for n in range(6, -1, -1):
        even = even * square + coefficients_even[n]
        odd = odd * square + coefficients_odd[n]
    sines = {1: even * square + 1.0}
    cosines = {1: -turn * (odd * square + 1.0)}
    for total, left, right in ((2, 1, 1), (3, 2, 1), (4, 2, 2), (5, 4, 1), (6, 4, 2), (7, 4, 3), (8, 4, 4)):
        sines[total] = sines[left] * cosines[right] + cosines[left] * sines[right]
        cosines[total] = cosines[left] * cosines[right] - sines[left] * sines[right]
    return [sines[k] for k in range(1, 9)], [cosines[k] for k in range(1, 9)]


def edge_values(edges, key_row, first, rows, full):
    block = edges[first : first + rows, :]
    vector = [block[:, i : i + 1] for i in range(3)]
    live = block[:, 6:7]
    squares = vector[0] * vector[0] + vector[1] * vector[1] + vector[2] * vector[2]
    length = jnp.sqrt(jnp.maximum(squares, 0.25))
    ux, uy, uz = (v / length for v in vector)
    ratio = jnp.minimum(length / CUTOFF, 1.0)
    second = ratio * ratio
    sixth = second * second * second
    envelope = (1.0 - 28.0 * sixth + 48.0 * (sixth * ratio) - 21.0 * (sixth * second)) * live
    harmonics = [
        jnp.ones_like(ux),
        ROOT_THREE * ux,
        ROOT_THREE * uy,
        ROOT_THREE * uz,
        ROOT_FIFTEEN * ux * uy,
        ROOT_FIFTEEN * uy * uz,
        0.5 * ROOT_FIVE * (3.0 * uz * uz - 1.0),
        ROOT_FIFTEEN * ux * uz,
        0.5 * ROOT_FIFTEEN * (ux * ux - uy * uy),
    ]
    same = jnp.where(block[:, 5:6] == key_row, 1.0, 0.0).astype(BF16)
    g = dict(
        env=envelope, harm=harmonics, same=same, squares=squares, length=length, ratio=ratio,
        unit=(ux, uy, uz), live=live, group=block[:, 7:8],
    )
    if full:
        sines, g["cosines"] = waves(length)
        g["bessel"] = [BESSEL_SCALE * value / length for value in sines]
        lane = lax.broadcasted_iota(jnp.int32, (rows, 16), 1).astype(F32)
        kinds = jnp.where(
            lane < NSPEC,
            jnp.where(block[:, 3:4] == lane, live, 0.0),
            jnp.where(block[:, 4:5] + NSPEC == lane, live, 0.0),
        )
        g["feat"] = kinds + place_columns(g["bessel"], 2 * NSPEC, 16)
    return g


def vector_pull(g, d_bessel, d_harm, d_envelope):
    ux, uy, uz = g["unit"]
    length, ratio = g["length"], g["ratio"]
    dx = ROOT_THREE * d_harm[1] + ROOT_FIFTEEN * (uy * d_harm[4] + uz * d_harm[7] + ux * d_harm[8])
    dy = ROOT_THREE * d_harm[2] + ROOT_FIFTEEN * (ux * d_harm[4] + uz * d_harm[5] - uy * d_harm[8])
    dz = (
        ROOT_THREE * d_harm[3]
        + ROOT_FIFTEEN * (uy * d_harm[5] + ux * d_harm[7])
        + (3.0 * ROOT_FIVE) * uz * d_harm[6]
    )
    left = 1.0 - ratio
    fourth = (ratio * ratio) * (ratio * ratio)
    d_length = (-168.0 / CUTOFF) * (fourth * ratio) * (left * left) * g["live"] * d_envelope
    d_length = d_length - (dx * ux + dy * uy + dz * uz) / length
    for k in range(NBES):
        slope = (BESSEL_SCALE * ANGLE * (k + 1)) * g["cosines"][k] - g["bessel"][k]
        d_length = d_length + d_bessel[k] * (slope / length)
    bound = jnp.where(g["squares"] > 0.25, 1.0, jnp.where(g["squares"] == 0.25, 0.5, 0.0))
    d_length = d_length * bound
    return [d / length + d_length * u for d, u in ((dx, ux), (dy, uy), (dz, uz))]


def env_terms(g, weight):
    scaled = ENV_SCALE * g["env"] * weight
    return same_sum(g["same"], [y * scaled for y in g["harm"]])


def pack_scalars(tensor, env):
    sums = [tensor[0] * env[0], tensor[1] * env[1], tensor[4] * env[4]]
    for m in (2, 3):
        sums[1] = sums[1] + tensor[m] * env[m]
    for m in (5, 6, 7, 8):
        sums[2] = sums[2] + tensor[m] * env[m]
    return jnp.concatenate([sums[0] + pltpu.roll(sums[1], 64, 1), sums[2]], axis=1)


def unpack_scalars(packed):
    first = packed[:, :LANES]
    return [first, pltpu.roll(first, 64, 1), packed[:, LANES:]]


def swap_order(lead, left, right):
    return jnp.where(lead, left, right), jnp.where(lead, right, left)


def env_pull(g, weight, d_env):
    d_terms = same_sum(g["same"], d_env)
    d_weight, d_harm, inner = None, [], None
    for m in range(9):
        part = g["harm"][m] * d_terms[m]
        d_weight = part if m == 0 else d_weight + part
        d_harm.append(jnp.sum(weight * d_terms[m], axis=1, keepdims=True))
        step = g["harm"][m] * d_harm[m]
        inner = step if m == 0 else inner + step
    scale = ENV_SCALE * g["env"]
    return scale * d_weight, [scale * d for d in d_harm], ENV_SCALE * inner


class Fetched:
    def __init__(self, source, buffer, semaphore):
        rows = source.shape[0]
        self.buffer, self.shape = buffer, buffer.shape
        target = buffer if rows == buffer.shape[0] else buffer.at[pl.ds(0, rows)]
        self.copy = pltpu.make_async_copy(source, target, semaphore)
        self.copy.start()
        self.arrived, self.pieces = False, {}
        if rows < buffer.shape[0]:
            buffer[rows:, :] = jnp.zeros((buffer.shape[0] - rows, buffer.shape[1]), F32)

    def __getitem__(self, where):
        if not self.arrived:
            self.copy.wait()
            self.arrived = True
        return self.buffer[where]

    def split(self, parts):
        if parts not in self.pieces:
            value = self[...]
            self.pieces[parts] = split_three(value) if parts == 3 else split_two(value)
        return self.pieces[parts]


class Stored:
    def __init__(self, target, buffer, semaphore):
        self.target, self.buffer, self.semaphore = target, buffer, semaphore
        self.shape, self.copy = buffer.shape, None

    def __setitem__(self, where, value):
        self.buffer[where] = value
        if where is Ellipsis:
            self.send()

    def __getitem__(self, where):
        return self.buffer[where]

    def send(self):
        self.copy = pltpu.make_async_copy(self.buffer, self.target, self.semaphore)
        self.copy.start()


def forward_pair(value, own, other):
    return [six_pass(value, own.split(3)), six_pass(value, other.split(3))]


def backward_pair(value, own, other, parts):
    return [three_pass(dot_nt, value, own.split(parts)), three_pass(dot_nt, value, other.split(parts))]


def first_forward(
    first, edges, key_row, lead_flag, embed,
    head_o, head_x, env_w, in_o, in_x, out_o, out_x,
    sent, soft_out, layer_in, slope_out, hidden,
):
    rows = sent.shape[0]
    lead = lead_flag[0:1, 0:1] > 0.5
    g = edge_values(edges, key_row[...], first, rows, True)
    pre = six_pass(g["feat"], split_three(embed[...]))
    soft = pre * sigmoid(pre)
    soft_out[...] = soft
    own, other = forward_pair(soft, head_o, head_x)
    latent = g["env"] * jnp.concatenate(swap_order(lead, own, other), axis=1)
    weight = six_pass(latent, env_w.split(3))
    env = env_terms(g, weight)
    scalars = pack_scalars([y * weight for y in g["harm"]], env)
    full = jnp.concatenate([latent, scalars], axis=1)
    layer_in[...] = full
    pre = jnp.concatenate(forward_pair(full, in_o, in_x), axis=1)
    gate = sigmoid(pre)
    slope_out[...] = gate * (1.0 + pre * (1.0 - gate))
    hid = pre * gate
    hidden[...] = hid
    half = hid.shape[1] // 2
    width = latent.shape[1]
    sent[:, :width] = (
        latent + six_pass(hid[:, :half], out_o.split(3)) + six_pass(hid[:, half:], out_x.split(3))
    )
    sent[:, width:] = weight
    sent.send()


def second_both(
    first, edges, key_row, mix, read, cot_row,
    arrived, env_w, in_o, in_x, out_o, out_x, head_o, head_x, env_wt,
    back, layer_in, d_pre_hidden, hidden, d_latent_out, latent_out, d_pre_read, d_weight_out,
    read_grad, mix_grad, energy_out,
):
    rows = back.shape[0]
    width = arrived.shape[1] - LANES
    half = width // 2
    g = edge_values(edges, key_row[...], first, rows, False)
    lane = lax.broadcasted_iota(jnp.int32, (rows, LANES), 1).astype(F32)
    group_hot = jnp.where(g["group"] == lane, g["live"], 0.0)
    cot = jnp.sum(group_hot * cot_row[...], axis=1, keepdims=True)
    mixes = [split_three(mix[i]) for i in range(3)]
    latent = arrived[:, :width]
    weight_first = arrived[:, width:]
    env_first = env_terms(g, weight_first)
    start = [y * weight_first for y in g["harm"]]
    coupled = [start[m] * env_first[0] + start[0] * env_first[m] for m in range(9)]
    members = ((0,), (1, 2, 3), (4, 5, 6, 7, 8))
    tensor = []
    for order in range(3):
        mixed = six_pass(jnp.concatenate([coupled[m] for m in members[order]], axis=0), mixes[order])
        tensor += [mixed[rows * i : rows * (i + 1)] for i in range(len(members[order]))]
    weight = six_pass(latent, env_w.split(3))
    env = env_terms(g, weight)
    full = jnp.concatenate([latent, pack_scalars(tensor, env)], axis=1)
    layer_in[...] = full
    pre = jnp.concatenate(forward_pair(full, in_o, in_x), axis=1)
    gate = sigmoid(pre)
    slope = gate * (1.0 + pre * (1.0 - gate))
    hid = pre * gate
    hidden[...] = hid
    latent_next = (
        latent + six_pass(hid[:, :half], out_o.split(3)) + six_pass(hid[:, half:], out_x.split(3))
    )
    latent_out[...] = latent_next
    pre_read = jnp.concatenate(forward_pair(latent_next, head_o, head_x), axis=1)
    gate = sigmoid(pre_read)
    soft = pre_read * gate
    line = read[...]
    inner = jnp.sum(soft * line, axis=1, keepdims=True)
    energy_out[...] = jnp.broadcast_to(
        jnp.sum(group_hot * (g["env"] * inner), axis=0, keepdims=True), energy_out.shape
    )
    scaled_cot = cot * g["env"]
    read_grad[...] = jnp.broadcast_to(
        jnp.sum(scaled_cot * soft, axis=0, keepdims=True), read_grad.shape
    )
    d_envelope = cot * inner
    d_read = scaled_cot * line * (gate * (1.0 + pre_read * (1.0 - gate)))
    d_pre_read[...] = d_read
    d_latent_out[...] = three_pass(dot_nt, d_read[:, :half], head_o.split(3)) + three_pass(
        dot_nt, d_read[:, half:], head_x.split(3)
    )
    d_hid = jnp.concatenate(backward_pair(d_latent_out[...], out_o, out_x, 3), axis=1)
    d_pre = d_hid * slope
    d_pre_hidden[...] = d_pre
    d_full = three_pass(dot_nt, d_pre[:, :half], in_o.split(3)) + three_pass(
        dot_nt, d_pre[:, half:], in_x.split(3)
    )
    d_scalars = unpack_scalars(d_full[:, width:])
    d_tensor = [d_scalars[order_of(m)] * env[m] for m in range(9)]
    d_env = [d_scalars[order_of(m)] * tensor[m] for m in range(9)]
    d_weight, d_harm, d_more = env_pull(g, weight, d_env)
    d_envelope = d_envelope + d_more
    d_weight_out[...] = d_weight
    back[:, :width] = (
        three_pass(dot_nn, d_weight_out[...], env_wt.split(2))
        + d_latent_out[...]
        + d_full[:, :width]
    )
    d_coupled = []
    for order in range(3):
        joined = jnp.concatenate([d_tensor[m] for m in members[order]], axis=0)
        mix_grad[order] = three_pass_tn(
            jnp.concatenate([coupled[m] for m in members[order]], axis=0), joined
        )
        mixed = three_pass(dot_nt, joined, mixes[order])
        d_coupled += [mixed[rows * i : rows * (i + 1)] for i in range(len(members[order]))]
    mix_grad.send()
    d_env_first = [d_coupled[m] * start[0] for m in range(9)]
    d_start = [d_coupled[m] * env_first[0] for m in range(9)]
    for m in range(9):
        d_env_first[0] = d_env_first[0] + d_coupled[m] * start[m]
        d_start[0] = d_start[0] + d_coupled[m] * env_first[m]
    d_first, d_harm_first, d_more = env_pull(g, weight_first, d_env_first)
    for m in range(9):
        d_first = d_first + g["harm"][m] * d_start[m]
        d_harm[m] = (
            d_harm[m]
            + d_harm_first[m]
            + jnp.sum(weight_first * d_start[m], axis=1, keepdims=True)
        )
    d_envelope = d_envelope + d_more
    back[:, width:] = d_first + place_columns(d_harm + [d_envelope], 64)
    back.send()


def first_backward(
    first, edges, key_row, lead_flag, embed,
    layer_in, env_w, arrived, out_o, out_x, slope_in, in_o, in_x, env_wt, head_o, head_x,
    d_vector, d_head, d_pre_hidden, d_weight_out, embed_grad,
):
    rows = arrived.shape[0]
    width = arrived.shape[1] - LANES
    half = width // 2
    lead = lead_flag[0:1, 0:1] > 0.5
    g = edge_values(edges, key_row[...], first, rows, True)
    embed_pair = split_two(embed[...])
    latent = layer_in[:, :width]
    weight = three_pass(dot_nn, latent, env_w.split(2))
    env = env_terms(g, weight)
    extra = arrived[:, width:]
    lane = lax.broadcasted_iota(jnp.int32, extra.shape, 1)
    d_weight = jnp.where(lane < 64, extra, 0.0)
    d_harm = [extra[:, 64 + m : 65 + m] for m in range(9)]
    d_envelope = extra[:, 73:74]
    d_hid = jnp.concatenate(backward_pair(arrived[:, :width], out_o, out_x, 2), axis=1)
    d_pre = d_hid * slope_in[...]
    d_pre_hidden[...] = d_pre
    d_full = three_pass(dot_nt, d_pre[:, :half], in_o.split(2)) + three_pass(
        dot_nt, d_pre[:, half:], in_x.split(2)
    )
    d_scalars = unpack_scalars(d_full[:, width:])
    d_start = [d_scalars[order_of(m)] * env[m] for m in range(9)]
    d_env = [d_scalars[order_of(m)] * (g["harm"][m] * weight) for m in range(9)]
    d_more_weight, d_more_harm, d_more = env_pull(g, weight, d_env)
    d_weight = d_weight + d_more_weight
    d_envelope = d_envelope + d_more
    for m in range(9):
        d_weight = d_weight + g["harm"][m] * d_start[m]
        d_harm[m] = (
            d_harm[m] + d_more_harm[m] + jnp.sum(weight * d_start[m], axis=1, keepdims=True)
        )
    d_weight_out[...] = d_weight
    d_latent = (
        three_pass(dot_nn, d_weight_out[...], env_wt.split(2))
        + arrived[:, :width]
        + d_full[:, :width]
    )
    d_own, d_other = swap_order(lead, d_latent[:, :half], d_latent[:, half:])
    d_head[:, :half] = g["env"] * d_own
    d_head[:, half:] = g["env"] * d_other
    d_head.send()
    d_soft = three_pass(dot_nt, d_own, head_o.split(2)) + three_pass(dot_nt, d_other, head_x.split(2))
    pre = three_pass(dot_nn, g["feat"], embed_pair)
    gate = sigmoid(pre)
    d_envelope = d_envelope + jnp.sum(pre * gate * d_soft, axis=1, keepdims=True)
    d_pre = g["env"] * d_soft * (gate * (1.0 + pre * (1.0 - gate)))
    d_feat = three_pass(dot_nt, d_pre, embed_pair)
    embed_grad[...] = three_pass_tn(g["feat"], d_pre)
    d_bessel = [d_feat[:, 2 * NSPEC + k : 2 * NSPEC + 1 + k] for k in range(NBES)]
    d_vector[...] = place_columns(vector_pull(g, d_bessel, d_harm, d_envelope), 0)


def outer_sum(split_left, chosen, *refs):
    count = len(CHUNKS)
    extra = len(refs) > 4 * count + 8
    kinds = 3 if extra else 2
    sources = [
        [refs[(kinds * side + i) * count : (kinds * side + i + 1) * count] for i in range(kinds)]
        for side in range(2)
    ]
    rest = refs[2 * kinds * count :]
    outs = [Stored(rest[i], rest[kinds + i], rest[-1].at[i]) for i in range(kinds)]
    buffers = rest[2 * kinds : 3 * kinds]
    semaphores = rest[-2]

    def copies(side):
        for i in range(kinds):
            start = 0
            for k, source in enumerate(sources[side][i]):
                rows, columns = source.shape[0], buffers[i].shape[1]
                yield pltpu.make_async_copy(
                    source.at[:, pl.ds(0, columns)],
                    buffers[i].at[pl.ds(start, rows)],
                    semaphores.at[i * count + k],
                )
                start += rows

    for side in range(2):

        @pl.when(chosen[0] == side)
        def _(side=side):
            for copy in copies(side):
                copy.start()

    for copy in copies(0):
        copy.wait()
    left_high, left_low = split_two(buffers[0][...])
    right_high, right_low = split_two(buffers[1][...])
    left = jnp.concatenate([left_high, left_low, left_high], axis=0)
    right = jnp.concatenate([right_high, right_high, right_low], axis=0)
    if split_left:
        half = left.shape[1] // 2
        outs[1][...] = dot_tn(left[:, half:], right)
        outs[0][...] = dot_tn(left[:, :half], right)
    else:
        half = right.shape[1] // 2
        outs[1][...] = dot_tn(left, right[:, half:])
        outs[0][...] = dot_tn(left, right[:, :half])
    if extra:
        right_high, right_low = split_two(buffers[2][...])
        right = jnp.concatenate([right_high, right_high, right_low], axis=0)
        outs[2][...] = dot_tn(left[:, : outs[2].shape[0]], right)
    for out in outs:
        out.copy.wait()


def on_core(body, outs, flops, args, fetched, chosen):
    here = pl.BlockSpec(memory_space=pltpu.VMEM)
    there = pl.BlockSpec(memory_space=pl.ANY)
    pad = 2 * LANES
    tall = [(m.shape[0] + pad - 1) // pad * pad if m.shape[0] > pad else m.shape[0] for m in fetched]
    scratch = [pltpu.VMEM((rows, m.shape[1]), F32) for rows, m in zip(tall, fetched)]
    scratch += [pltpu.VMEM(shape, F32) for shape in outs]
    scratch.append(pltpu.SemaphoreType.DMA((len(fetched),)))
    scratch.append(pltpu.SemaphoreType.DMA((len(outs),)))

    def guarded(flag, *refs):
        @pl.when(flag[0] == 1)
        def _():
            small, rest = refs[: len(args)], refs[len(args) :]
            sources, rest = rest[: len(fetched)], rest[len(fetched) :]
            targets, rest = rest[: len(outs)], rest[len(outs) :]
            buffers, rest = rest[: len(fetched)], rest[len(fetched) :]
            kept, (arrivals, departures) = rest[: len(outs)], rest[len(outs) :]
            inputs = [Fetched(s, b, arrivals.at[i]) for i, (s, b) in enumerate(zip(sources, buffers))]
            outputs = [Stored(t, b, departures.at[i]) for i, (t, b) in enumerate(zip(targets, kept))]
            body(*small, *inputs, *outputs)
            for output in outputs:
                output.copy.wait()

    return pl.pallas_call(
        guarded,
        out_shape=tuple(jax.ShapeDtypeStruct(shape, F32) for shape in outs),
        in_specs=[pl.BlockSpec(memory_space=pltpu.SMEM)] + [here] * len(args) + [there] * len(fetched),
        out_specs=tuple(there for _ in outs),
        scratch_shapes=scratch,
        compiler_params=pltpu.CompilerParams(vmem_limit_bytes=60 * 2**20),
        cost_estimate=pl.CostEstimate(flops=flops, bytes_accessed=16 * 2**20, transcendentals=0),
    )(chosen, *args, *fetched)


def outer_call(split_left, outs, widths, flops, chosen, first, second):
    there = pl.BlockSpec(memory_space=pl.ANY)
    args = [array for side in (first, second) for factor in side for array in factor]
    return pl.pallas_call(
        partial(outer_sum, split_left),
        out_shape=tuple(jax.ShapeDtypeStruct(shape, F32) for shape in outs),
        in_specs=[pl.BlockSpec(memory_space=pltpu.SMEM)] + [there] * len(args),
        out_specs=tuple(there for _ in outs),
        scratch_shapes=[pltpu.VMEM(shape, F32) for shape in outs]
        + [pltpu.VMEM((sum(CHUNKS), w), F32) for w in widths]
        + [
            pltpu.SemaphoreType.DMA((len(widths) * len(CHUNKS),)),
            pltpu.SemaphoreType.DMA((len(outs),)),
        ],
        compiler_params=pltpu.CompilerParams(vmem_limit_bytes=60 * 2**20),
        cost_estimate=pl.CostEstimate(flops=flops, bytes_accessed=16 * 2**20, transcendentals=0),
    )(chosen, *args)


def gather_blocks(value):
    count = lax.axis_size("edge")
    if count & (count - 1) or count > 8:
        return lax.all_gather(value, "edge", axis=0)
    index = lax.axis_index("edge")
    out = value[None]
    step = 1
    while step < count:
        got = lax.ppermute(out, "edge", [(i, i ^ step) for i in range(count)])
        low = (index // step) % 2 == 0
        out = jnp.where(low, jnp.concatenate([out, got]), jnp.concatenate([got, out]))
        step *= 2
    return out


def prefix_in_rows(flags):
    rows, length = flags.shape
    pieces = flags.reshape(rows, length // LANES, LANES)
    upper = (jnp.arange(LANES)[:, None] <= jnp.arange(LANES)[None, :]).astype(F32)
    inner = jnp.einsum("rkl,lm->rkm", pieces, upper, precision=HIGHEST)
    totals = inner[:, :, -1]
    count = length // LANES
    before = (jnp.arange(count)[:, None] < jnp.arange(count)[None, :]).astype(F32)
    offsets = jnp.dot(totals, before, precision=HIGHEST)
    return (inner + offsets[:, :, None]).reshape(rows, length)


def pack_edges(atoms, vectors, species, centres, mask, structures, out):
    count = centres.shape[1]
    for b in range(centres.shape[0]):
        span = slice(b * count, (b + 1) * count)
        vector = vectors[b]
        out[0:3, span] = vector
        out[3:5, span] = species[b].astype(F32)
        out[5:6, span] = (centres[b : b + 1, :] + b * atoms).astype(F32)
        squares = jnp.maximum(jnp.sum(vector * vector, axis=0, keepdims=True), 0.25)
        near = jnp.where(jnp.sqrt(squares) / CUTOFF < 1.0, 1.0, 0.0)
        out[6:7, span] = jnp.where(mask[b : b + 1, :] > 0, near, 0.0)
        out[7:8, span] = (structures[b : b + 1, :] + b * STRUCTS).astype(F32)


def plan_edges(edge_vectors, edge_species, centres, edge_mask, structures):
    batch_count, _, edge_count = edge_vectors.shape
    blocks = lax.axis_size("edge")
    block = lax.axis_index("edge")
    core = lax.axis_index("mp")
    atoms = blocks * ATOM_DEV
    per_block = batch_count * edge_count
    raw = pl.pallas_call(
        partial(pack_edges, atoms), out_shape=jax.ShapeDtypeStruct((8, per_block), F32)
    )(edge_vectors, edge_species, centres, edge_mask, structures)
    gathered = gather_blocks(raw)
    keys = gathered[:, 5].reshape(blocks, batch_count, edge_count)
    alive = gathered[:, 6].reshape(blocks, batch_count, edge_count)
    local = keys - (jnp.arange(batch_count) * atoms)[None, :, None].astype(F32)
    degree = jnp.sum(
        jnp.where(
            local.transpose(1, 0, 2).reshape(batch_count, 1, -1)
            == jnp.arange(atoms, dtype=F32)[None, :, None],
            alive.transpose(1, 0, 2).reshape(batch_count, 1, -1),
            0.0,
        ),
        axis=2,
    )
    spans = batch_count * ATOM_DEV
    degree = degree.reshape(batch_count, blocks, ATOM_DEV).transpose(1, 0, 2).reshape(blocks, spans)
    upper = (jnp.arange(spans)[:, None] <= jnp.arange(spans)[None, :]).astype(F32)
    upto = jnp.dot(degree, upper, precision=HIGHEST)
    start = jnp.zeros((blocks, 1), F32)
    starts = [start]
    for size in CHUNKS:
        for _ in range(2):
            start = jnp.max(jnp.where(upto <= start + size, jnp.maximum(upto, start), start), axis=1, keepdims=True)
            starts.append(start)
    fits = jnp.all(starts[-1] >= upto[:, -1:])
    starts = jnp.concatenate(starts[:-1], axis=1)
    own_before = (upto - degree)[block]
    bin_of = jnp.sum((own_before[:, None] >= starts[block][None, 1:]).astype(F32), axis=1)
    padded = jnp.concatenate([jnp.zeros_like(gathered[:1]), gathered, jnp.zeros_like(gathered[:1])])
    window = lax.dynamic_slice_in_dim(padded, block, 3, 0)
    flat = window.transpose(1, 0, 2).reshape(8, 3 * per_block)
    position = jnp.arange(3 * per_block)
    batch_flat = (position % per_block) // edge_count
    spot = flat[5] - (batch_flat * atoms + block * ATOM_DEV).astype(F32)
    mine = (spot >= 0) & (spot < ATOM_DEV) & (flat[6] > 0.5)
    slot = jnp.where(mine, spot + (batch_flat * ATOM_DEV).astype(F32), -1.0)
    chosen = jnp.sum(
        jnp.where(jnp.arange(spans, dtype=F32)[:, None] == slot[None, :], bin_of[:, None], 0.0), axis=0
    )
    wanted = 2 * jnp.arange(len(CHUNKS)) + core
    picked = (chosen[None, :] == wanted[:, None].astype(F32)) & mine[None, :]
    rank = prefix_in_rows(picked.astype(F32)) - 1.0
    offsets = [sum(CHUNKS[:k]) for k in range(len(CHUNKS))]
    place = jnp.sum(
        jnp.where(picked, rank + jnp.array(offsets, F32)[:, None], 0.0), axis=0
    ) - (1.0 - jnp.sum(picked.astype(F32), axis=0))
    total = sum(CHUNKS)
    hot = (place[None, :] == jnp.arange(total, dtype=F32)[:, None]).astype(F32)
    edges = lax.dot_general(hot, flat, (((1,), (1,)), ((), ())), precision=HIGHEST)
    return fits, edges, place


def tied(first, *others):
    return lax.optimization_barrier((first, others))[0]


def hop(value, distance):
    return lax.ppermute(value, "edge", [(i, i ^ distance) for i in range(8)])


def halves(value, second):
    half = value.shape[0] // 2
    kept = lax.dynamic_slice_in_dim(value, second * half, half, 0)
    return kept, lax.dynamic_slice_in_dim(value, (1 - second) * half, half, 0)


def joined(kept, got, second):
    return jnp.where(second == 0, jnp.concatenate([kept, got]), jnp.concatenate([got, kept]))


def sum_steps(value, outer_hop, inner_hop, wait):
    index = lax.axis_index("edge")
    seconds = {1: index % 2, 2: ((index // 2) ^ (index // 4)) % 2}
    kept, given = halves(value, seconds[outer_hop])
    given = wait(given)
    got = hop(given, outer_hop)
    yield given
    kept, given = halves(kept + wait(got), seconds[inner_hop])
    got = hop(given, inner_hop)
    yield given
    part = kept + wait(got)
    got = hop(part, 6)
    yield part
    part = part + wait(got)
    got = hop(part, inner_hop)
    yield part
    part = joined(part, wait(got), seconds[inner_hop])
    half = part.shape[0]
    got = hop(part, outer_hop)
    yield part
    yield [(part, seconds[outer_hop] * half), (wait(got), (1 - seconds[outer_hop]) * half)]


class BlockSums:
    def __init__(self, plan):
        self.plan, self.steps, self.sums, self.moment = plan, {}, {}, None

    def wait(self, value):
        return value if self.moment is None else tied(value, self.moment)

    def advance(self, matrices, order):
        for piece in order:
            which, first, rows, outer_hop, inner_hop = self.plan[piece]
            if piece not in self.steps:
                value = lax.slice_in_dim(matrices[which], first, first + rows, axis=0)
                self.steps[piece] = sum_steps(value, outer_hop, inner_hop, self.wait)
            given = next(self.steps[piece])
            if isinstance(given, list):
                total = self.sums.get(which, jnp.zeros_like(matrices[which]))
                for part, start in given:
                    total = lax.dynamic_update_slice_in_dim(total, part, first + start, 0)
                self.sums[which] = total
                given = given[1][0]
            self.moment = given


def fast_device(edges, place, others, args):
    (
        edge_vectors, edge_species, centres, edge_mask, structures, energy_cot, embed_in,
        section_head, env_weight, mix_weight, w_in, w_out, read_weight,
    ) = args
    is_first = lax.axis_index("section") == 0
    core = lax.axis_index("mp")
    width = section_head.shape[1]
    half = section_head.shape[2]
    batch_count, _, edge_count = edge_vectors.shape
    chan_count = mix_weight.shape[1]
    gap = LANES - chan_count
    read_left, read_right = read_weight[:half], read_weight[half:]
    read_line = jnp.where(
        core == 0,
        jnp.concatenate([read_left, read_right]),
        jnp.concatenate([read_right, read_left]),
    )[None]
    cot_row = jnp.pad(energy_cot.reshape(1, -1), ((0, 0), (0, LANES - energy_cot.size)))
    lead_flag = jnp.full((8, LANES), 1.0, F32) * (core == 0).astype(F32)
    mix = jnp.pad(mix_weight, ((0, 0), (0, gap), (0, gap)))
    env_w = jnp.pad(env_weight[0], ((0, 0), (0, gap)))
    env_wt = env_w.T
    heads, ins, outs_w = (section_head[0], others[0]), (w_in[0], others[1]), (w_out[0], others[2])
    count = len(CHUNKS)
    offsets = [sum(CHUNKS[:k]) for k in range(count)]
    rows = [edges[o : o + m, 5].reshape(1, -1) for o, m in zip(offsets, CHUNKS)]
    layer_width = width + 2 * LANES

    first_flag = jnp.full((1,), 1, jnp.int32) * is_first.astype(jnp.int32)
    second_flag = 1 - first_flag
    saved, moved = [], []
    for k, m in enumerate(CHUNKS):
        outs = [(m, width + LANES), (m, width), (m, layer_width), (m, width), (m, width)]
        work = 12 * m * width * (3 * width + 384)
        result = on_core(
            partial(first_forward, offsets[k]), outs, work,
            (edges, rows[k], lead_flag, embed_in), (*heads, env_w, *ins, *outs_w), first_flag,
        )
        moved.append(shifted(result[0], "section", 1))
        saved.append(result[1:])
    seconds, returned, firsts = [], [], []
    for k, m in enumerate(CHUNKS):
        outs = [
            (m, width + LANES), (m, layer_width), (m, width), (m, width), (m, width),
            (m, width), (m, width), (m, LANES), (8, width), (3, LANES, LANES), (8, LANES),
        ]
        work = 18 * m * width * (3 * width + 384)
        seconds.append(
            on_core(
                partial(second_both, offsets[k]), outs, work,
                (edges, rows[k], mix, read_line, cot_row),
                (moved[k], env_w, *ins, *outs_w, *heads, env_wt), second_flag,
            )
        )
    outer_work = 6 * sum(CHUNKS) * width * width
    by_hand = lax.axis_size("edge") == 8
    sums = BlockSums(PLAN)
    for k, m in enumerate(CHUNKS):
        arrived = shifted(seconds[k][0], "section", -1)
        if k > 0:
            arrived = tied(arrived, firsts[k - 1][0])
        returned.append(arrived)
        if k == count - 1:
            out_own, out_other = outer_call(
                True, [(half, width)] * 2, (width, width), outer_work, second_flag,
                ([s[3] for s in saved], returned),
                ([s[3] for s in seconds], [s[4] for s in seconds]),
            )
            arrived = tied(arrived, out_other)
            grad_out = out_own + other_core(out_other)
            if by_hand:
                sums.advance([grad_out], EARLY)
        outs = [(m, LANES), (m, width), (m, width), (m, LANES), (16, width)]
        work = 9 * m * width * (3 * width + 384)
        firsts.append(
            on_core(
                partial(first_backward, offsets[k]), outs, work,
                (edges, rows[k], lead_flag, embed_in),
                (saved[k][1], env_w, arrived, *outs_w, saved[k][2], *ins, env_wt, *heads), first_flag,
            )
        )
    in_own, in_other, grad_env = outer_call(
        False, [(layer_width, half)] * 2 + [(width, LANES)], (layer_width, width, LANES), outer_work,
        sums.wait(second_flag),
        ([s[1] for s in saved], [f[2] for f in firsts], [f[3] for f in firsts]),
        ([s[1] for s in seconds], [s[2] for s in seconds], [s[7] for s in seconds]),
    )
    grad_in = in_own + other_core(in_other)
    if by_hand:
        sums.moment = (sums.moment, in_other)
        sums.advance([grad_out], EARLY)
    head_own, head_other = outer_call(
        False, [(width, half)] * 2, (width, width), outer_work, tied(second_flag, in_other, sums.moment),
        ([s[0] for s in saved], [f[1] for f in firsts]),
        ([s[5] for s in seconds], [s[6] for s in seconds]),
    )
    none = jnp.zeros((), F32)
    read_sum = sum(s[8][0] for s in seconds)
    read_sum = jnp.where(
        core == 0, read_sum, jnp.concatenate([read_sum[half:], read_sum[:half]])
    )
    mix_sum = sum(s[9] for s in seconds)[:, :chan_count, :chan_count].reshape(-1, width)
    energy_sum = sum(s[10][0] for s in seconds)
    embed_sum = sum(f[4] for f in firsts)
    small_second = jnp.concatenate(
        [read_sum[None], jnp.pad(energy_sum, (0, width - LANES))[None], mix_sum]
    )
    small_second = jnp.pad(small_second, ((0, 16 - small_second.shape[0]), (0, 0)))
    small = jnp.concatenate(
        [jnp.where(is_first, embed_sum, none), jnp.where(is_first, none, small_second)]
    )
    small = sums.wait(small)
    small = small + lax.ppermute(small, "section", [(0, 1), (1, 0)])
    small = jnp.concatenate([small, grad_env[:, :chan_count].reshape(-1, width)]).reshape(-1, half)
    head_own = jnp.concatenate([head_own, small])
    grad_head = head_own + other_core(jnp.concatenate([head_other, small]))
    total = sum(CHUNKS)
    hot = (place[None, :] == jnp.arange(total, dtype=F32)[:, None]).astype(F32)
    d_vectors = jnp.concatenate([f[0][:, :8] for f in firsts])
    spread = lax.dot_general(d_vectors, hot, (((0,), (0,)), ((), ())), precision=HIGHEST)[:3]
    spread = jnp.where(is_first, spread, none)
    if by_hand:
        matrices = [grad_out, grad_in, grad_head]
        sums.moment = (sums.moment, head_other, grad_in)
        sums.advance(matrices, ORDER[:8])
        spread = sums.wait(spread)
        spread = spread + other_core(spread)
        sums.advance(matrices, ORDER[8:16])
        spread = sums.wait(spread)
        sums.advance(matrices, ORDER[16:])
        grad_out, grad_in, grad_head = (sums.sums[i] for i in range(3))
    else:
        spread = spread + other_core(spread)
        grad_out, grad_in, grad_head = lax.psum((grad_out, grad_in, grad_head), "edge")
    per_block = batch_count * edge_count
    to_left, kept, to_right = (spread[:, i * per_block : (i + 1) * per_block] for i in range(3))
    forces = kept + shifted(to_right, "edge", 1) + shifted(to_left, "edge", -1)
    small = grad_head[width:].reshape(-1, width)
    grad_head = grad_head[:width]
    grad_embed, grad_read = small[:16], small[16]
    energies = small[17, : energy_cot.size].reshape(energy_cot.shape)
    grad_mix = small[18 : 18 + mix_sum.shape[0]].reshape(mix_weight.shape)
    grad_env = small[32:].reshape(width, chan_count)

    forces = jnp.where(is_first, forces, shifted(forces, "section", 1))
    forces = -forces.reshape(3, batch_count, edge_count).transpose(1, 0, 2)
    return (
        energies, forces, grad_embed, grad_head[None], grad_env[None], grad_mix,
        grad_in[None, : w_in.shape[1]], grad_out[None], grad_read,
    )


def per_device(*args):
    section_head, w_in, w_out = args[7], args[10], args[11]
    others = tuple(other_core(m[0]) for m in (section_head, w_in, w_out))
    fits, edges, place = plan_edges(*args[:5])
    results = fast_device(edges, place, others, args)

    def again(state):
        rest, _ = state
        held, rest = lax.optimization_barrier((args, rest))
        return rest - 1, general_device(*held)

    overflow = 1 - fits.astype(jnp.int32)
    return lax.while_loop(lambda state: state[0] > 0, again, (overflow, results))[1]


def solution(mesh):
    placed = (
        P(None, None, "edge"),
        P(None, None, "edge"),
        P(None, "edge"),
        P(None, "edge"),
        P(None, "edge"),
        P(),
        P(),
        P("section", None, "mp"),
        P("section", None, None),
        P(),
        P("section", None, "mp"),
        P("section", "mp", None),
        P(),
    )
    return jax.shard_map(
        per_device,
        mesh=mesh,
        in_specs=placed,
        out_specs=(
            P(),
            P(None, None, "edge"),
            P(),
            P("section", None, "mp"),
            P("section", None, None),
            P(),
            P("section", None, "mp"),
            P("section", "mp", None),
            P(),
        ),
        check_vma=False,
    )
```

```python
from functools import partial

import jax
import jax.numpy as jnp
from jax import lax
from jax.experimental import pallas as pl
from jax.experimental.pallas import tpu as pltpu
from jax.sharding import PartitionSpec as P

NBES = 8
NSPEC = 4
ATOM_DEV = 40
STRUCTS = 16


CUTOFF = 5.0
ENV_SCALE = 0.25
HIGHEST = lax.Precision.HIGHEST
ROOT_THREE = 1.7320508075688772
ROOT_FIVE = 2.23606797749979
ROOT_FIFTEEN = 3.872983346207417


def extended(block, sides, width):
    for axis, dim in sides:
        count = lax.axis_size(axis)
        forward = [(i, i + 1) for i in range(count - 1)]
        backward = [(target, source) for source, target in forward]
        low = lax.ppermute(
            lax.slice_in_dim(block, block.shape[dim] - width, None, axis=dim), axis, forward
        )
        high = lax.ppermute(lax.slice_in_dim(block, 0, width, axis=dim), axis, backward)
        block = jnp.concatenate([low, block, high], axis=dim)
    return block


def shifted(value, axis, steps):
    count = lax.axis_size(axis)
    first, last = (max(0, -steps), min(count, count - steps))
    return lax.ppermute(value, axis, [(source, source + steps) for source in range(first, last)])


def other_core(value):
    return lax.ppermute(value, "mp", [(0, 1), (1, 0)])


def ring_sum(values):
    count = lax.axis_size("edge")

    def step(_, state):
        moving, total = state
        moving = tuple(
            lax.ppermute(v, "edge", [(i, (i + 1) % count) for i in range(count)]) for v in moving
        )
        return moving, tuple(t + v for t, v in zip(total, moving))

    return lax.fori_loop(0, count - 1, step, (tuple(values), tuple(values)))[1]


def matmul(left, right):
    return jnp.dot(left, right, precision=HIGHEST, preferred_element_type=jnp.float32)


def geometry(vectors, edge_live):
    squares = jnp.maximum(jnp.sum(vectors * vectors, axis=0), 0.25)
    length = jnp.sqrt(squares)
    unit_x = vectors[0] / length
    unit_y = vectors[1] / length
    unit_z = vectors[2] / length
    edge_ratio = jnp.minimum(length / CUTOFF, 1.0)
    envelope = (
        1.0 - 28.0 * edge_ratio**6 + 48.0 * edge_ratio**7 - 21.0 * edge_ratio**8
    ) * edge_live
    orders = jnp.arange(1, NBES + 1).astype(jnp.float32)
    bessel = (
        jnp.sqrt(2.0 / CUTOFF)
        * jnp.sin(orders[None, :] * (jnp.pi / CUTOFF) * length[:, None])
        / length[:, None]
    )
    harmonics = jnp.stack(
        [
            jnp.ones_like(unit_x),
            ROOT_THREE * unit_x,
            ROOT_THREE * unit_y,
            ROOT_THREE * unit_z,
            ROOT_FIFTEEN * unit_x * unit_y,
            ROOT_FIFTEEN * unit_y * unit_z,
            0.5 * ROOT_FIVE * (3.0 * unit_z * unit_z - 1.0),
            ROOT_FIFTEEN * unit_x * unit_z,
            0.5 * ROOT_FIFTEEN * (unit_x * unit_x - unit_y * unit_y),
        ],
        axis=1,
    )
    return (harmonics, envelope, bessel)


def couple(edge_tensor, env_flat, mix_weight):
    chan_count = mix_weight.shape[1]
    own_tensor = edge_tensor.reshape(-1, 9, chan_count)
    env_tensor = env_flat.reshape(-1, 9, chan_count)
    paired = own_tensor * env_tensor
    scalars = jnp.concatenate(
        [paired[:, 0], jnp.sum(paired[:, 1:4], axis=1), jnp.sum(paired[:, 4:9], axis=1)], axis=1
    )
    coupled = own_tensor * env_tensor[:, 0:1] + own_tensor[:, 0:1] * env_tensor
    order_zero = jnp.einsum("emc,cd->emd", coupled[:, 0:1], mix_weight[0], precision=HIGHEST)
    order_one = jnp.einsum("emc,cd->emd", coupled[:, 1:4], mix_weight[1], precision=HIGHEST)
    order_two = jnp.einsum("emc,cd->emd", coupled[:, 4:9], mix_weight[2], precision=HIGHEST)
    updated = jnp.concatenate([order_zero, order_one, order_two], axis=1)
    return (scalars, updated.reshape(-1, 9 * chan_count))


def front(bessel, envelope, embed_in, head_local, kinds_hot):
    features = jnp.concatenate([kinds_hot, bessel], axis=1)
    return envelope[:, None] * matmul(jax.nn.silu(matmul(features, embed_in)), head_local)


def contribute(latent_full, harmonics, envelope, env_local, centre_hot):
    weight = matmul(latent_full, env_local)
    contribution = (
        (ENV_SCALE * envelope)[:, None, None] * harmonics[:, :, None] * weight[:, None, :]
    )
    flat_terms = contribution.reshape(weight.shape[0], -1)
    return (weight, matmul(centre_hot.T, flat_terms))


def tensor_step(tensor_full, env_window, weight, harmonics, mix_weight, centre_hot, is_first):
    start_tensor = (harmonics[:, :, None] * weight[:, None, :]).reshape(weight.shape[0], -1)
    edge_tensor = jnp.where(is_first, start_tensor, tensor_full)
    env_flat = matmul(centre_hot, env_window)
    return couple(edge_tensor, env_flat, mix_weight)


def perceptron(latent_full, scalars, in_local, out_local):
    hidden = jax.nn.silu(matmul(jnp.concatenate([latent_full, scalars], axis=1), in_local))
    return matmul(hidden, out_local)


def readout(latent_full, envelope, head_local, read_half):
    return envelope * matmul(jax.nn.silu(matmul(latent_full, head_local)), read_half)


def general_device(
    edge_vectors,
    edge_species,
    centres,
    edge_mask,
    structures,
    energy_cot,
    embed_in,
    section_head,
    env_weight,
    mix_weight,
    w_in,
    w_out,
    read_weight,
):
    section_index = lax.axis_index("section")
    core_index = lax.axis_index("mp")
    edge_index = lax.axis_index("edge")
    is_first = section_index == 0
    last_flag = (section_index == 1).astype(jnp.float32)
    batch_count = edge_vectors.shape[0]
    shard_width = w_out.shape[1]
    tensor_cols = 9 * env_weight.shape[2]
    tensor_half = tensor_cols // 2
    atoms_dev = ATOM_DEV
    head_local = section_head[0]
    env_local = env_weight[0]
    in_local = w_in[0]
    out_local = w_out[0]
    read_half = lax.dynamic_slice_in_dim(read_weight, core_index * shard_width, shard_width, 0)
    core_lead = (core_index == 0).astype(jnp.float32)
    edge_count = edge_vectors.shape[2]
    centre_slots = jnp.arange(3 * atoms_dev)
    labels = jnp.arange(STRUCTS)
    species_range = jnp.arange(NSPEC)
    batch_range = jnp.arange(batch_count)

    def reduce_rims(pieces):
        widened = extended(pieces, (("edge", 0),), atoms_dev)
        return (
            widened[:atoms_dev] + widened[2 * atoms_dev : 3 * atoms_dev] + widened[4 * atoms_dev :]
        )

    def window_rows(totals):
        return extended(totals, (("edge", 0),), atoms_dev)

    def collect(partial_rows):
        width = partial_rows.shape[1] // 2
        own = lax.dynamic_slice_in_dim(partial_rows, core_index * width, width, 1)
        return own + other_core(lax.dynamic_slice_in_dim(partial_rows, (1 - core_index) * width, width, 1))

    def both_halves(half):
        other = other_core(half)
        return jnp.where(
            core_index == 0,
            jnp.concatenate([half, other], axis=1),
            jnp.concatenate([other, half], axis=1),
        )

    def batch_data(batch_index):
        vectors = lax.dynamic_index_in_dim(edge_vectors, batch_index, 0, keepdims=False)
        kind_ids = lax.dynamic_index_in_dim(edge_species, batch_index, 0, keepdims=False)
        owners = lax.dynamic_index_in_dim(centres, batch_index, 0, keepdims=False)
        edge_live = lax.dynamic_index_in_dim(edge_mask, batch_index, 0, keepdims=False).astype(
            jnp.float32
        )
        groups = lax.dynamic_index_in_dim(structures, batch_index, 0, keepdims=False)
        kinds_hot = jnp.concatenate(
            [
                kind_ids[0][:, None] == species_range[None, :],
                kind_ids[1][:, None] == species_range[None, :],
            ],
            axis=1,
        ).astype(jnp.float32)
        local_slot = owners - (edge_index - 1) * atoms_dev
        centre_hot = (local_slot[:, None] == centre_slots[None, :]).astype(jnp.float32)
        group_hot = (groups[:, None] == labels[None, :]).astype(jnp.float32)
        return (vectors, edge_live, kinds_hot, centre_hot, group_hot)

    recv_latent = jnp.zeros((edge_count, shard_width), jnp.float32)
    recv_tensor = jnp.zeros((edge_count, tensor_half), jnp.float32)
    energies = jnp.zeros((batch_count, STRUCTS), jnp.float32)
    kept_state = []
    for step_index in range(batch_count + 1):
        batch_raw = step_index - section_index
        batch_index = jnp.clip(batch_raw, 0, batch_count - 1)
        is_valid = ((batch_raw >= 0) & (batch_raw < batch_count)).astype(jnp.float32)
        vectors, edge_live, kinds_hot, centre_hot, group_hot = batch_data(batch_index)
        harmonics, envelope, bessel = geometry(vectors, edge_live)
        latent_half = lax.cond(
            is_first,
            lambda: front(bessel, envelope, embed_in, head_local, kinds_hot),
            lambda: recv_latent,
        )
        latent_full, tensor_full = (
            both_halves(latent_half),
            both_halves(recv_tensor),
        )
        weight, part_sums = contribute(latent_full, harmonics, envelope, env_local, centre_hot)
        env_window = window_rows(reduce_rims(part_sums))
        scalars, updated = tensor_step(
            tensor_full, env_window, weight, harmonics, mix_weight, centre_hot, is_first
        )
        branch_out = perceptron(latent_full, scalars, in_local, out_local)
        summed = collect(branch_out)
        tensor_own = lax.dynamic_slice_in_dim(updated, core_index * tensor_half, tensor_half, 1)
        next_half = latent_half + summed
        recv_latent, recv_tensor = shifted((next_half, tensor_own), "section", 1)
        next_full = both_halves(next_half)
        edge_energy = readout(next_full, envelope, head_local, read_half)
        batch_slot = (batch_range == batch_index).astype(jnp.float32) * is_valid * last_flag
        energies = (
            energies
            + batch_slot[:, None] * jnp.dot(edge_energy, group_hot, precision=HIGHEST)[None, :]
        )
        kept_state.append((latent_full, tensor_full, env_window, next_full))
    kept_latent = jnp.stack([entry[0] for entry in kept_state])
    kept_tensor = jnp.stack([entry[1] for entry in kept_state])
    kept_window = jnp.stack([entry[2] for entry in kept_state])
    kept_next = jnp.stack([entry[3] for entry in kept_state])
    grad_head = jnp.zeros_like(head_local)
    grad_env = jnp.zeros_like(env_local)
    grad_in = jnp.zeros_like(in_local)
    grad_out = jnp.zeros_like(out_local)
    grad_mix = jnp.zeros_like(mix_weight)
    grad_embed = jnp.zeros_like(embed_in)
    grad_read = jnp.zeros_like(read_half)
    forces = jnp.zeros((batch_count, 3, edge_count), jnp.float32)
    recv_grad = jnp.zeros((edge_count, shard_width), jnp.float32)
    recv_tgrad = jnp.zeros((edge_count, tensor_half), jnp.float32)
    for step_index in range(batch_count + 1):
        batch_raw = step_index - 1 + section_index
        batch_index = jnp.clip(batch_raw, 0, batch_count - 1)
        is_valid = ((batch_raw >= 0) & (batch_raw < batch_count)).astype(jnp.float32)
        saved_index = jnp.clip(batch_raw + section_index, 0, batch_count)
        latent_full = lax.dynamic_index_in_dim(kept_latent, saved_index, 0, keepdims=False)
        tensor_full = lax.dynamic_index_in_dim(kept_tensor, saved_index, 0, keepdims=False)
        env_window = lax.dynamic_index_in_dim(kept_window, saved_index, 0, keepdims=False)
        next_full = lax.dynamic_index_in_dim(kept_next, saved_index, 0, keepdims=False)
        vectors, edge_live, kinds_hot, centre_hot, group_hot = batch_data(batch_index)
        (harmonics, envelope, bessel), geometry_pull = jax.vjp(
            partial(geometry, edge_live=edge_live), vectors
        )
        batch_cot = lax.dynamic_index_in_dim(energy_cot, batch_index, 0, keepdims=False)
        energy_rows = jnp.dot(group_hot, batch_cot, precision=HIGHEST) * (is_valid * last_flag)
        _, read_pull = jax.vjp(readout, next_full, envelope, head_local, read_half)
        d_next_read, d_env_read, g_head_read, g_read = read_pull(energy_rows)
        d_next_half = jnp.where(is_first, recv_grad, collect(d_next_read))
        d_out_full, d_updated = (
            both_halves(d_next_half),
            both_halves(recv_tgrad),
        )
        (weight, part_sums), contribute_pull = jax.vjp(
            partial(contribute, centre_hot=centre_hot), latent_full, harmonics, envelope, env_local
        )
        (scalars, updated), tensor_pull = jax.vjp(
            partial(tensor_step, centre_hot=centre_hot, is_first=is_first),
            tensor_full,
            env_window,
            weight,
            harmonics,
            mix_weight,
        )
        _, perceptron_pull = jax.vjp(perceptron, latent_full, scalars, in_local, out_local)
        d_latent_mlp, d_scalar_part, g_in, g_out = perceptron_pull(d_out_full)
        d_scalars = d_scalar_part + other_core(d_scalar_part)
        d_tensor, d_window, d_weight, d_harm_tensor, g_mix = tensor_pull((d_scalars, d_updated))
        d_parts = window_rows(reduce_rims(d_window))
        d_latent_env, d_harm_env, d_envelope_env, g_env = contribute_pull((d_weight, d_parts))
        d_latent_own = (
            collect(d_latent_mlp)
            + lax.dynamic_slice_in_dim(d_latent_env, core_index * shard_width, shard_width, 1)
            + d_next_half
        )
        d_tensor_own = lax.dynamic_slice_in_dim(d_tensor, core_index * tensor_half, tensor_half, 1)
        recv_grad, recv_tgrad = shifted((d_latent_own, d_tensor_own), "section", -1)

        def front_pull(cotangent):
            _, pull_back = jax.vjp(
                partial(front, kinds_hot=kinds_hot), bessel, envelope, embed_in, head_local
            )
            return pull_back(cotangent)

        def front_none(cotangent):
            return (
                jnp.zeros_like(bessel),
                jnp.zeros_like(envelope),
                jnp.zeros_like(embed_in),
                jnp.zeros_like(head_local),
            )

        d_bessel, d_envelope_front, g_embed, g_head_front = lax.cond(
            is_first, front_pull, front_none, d_latent_own
        )
        d_harmonics = core_lead * (d_harm_tensor + d_harm_env)
        d_envelope = core_lead * d_envelope_env + d_env_read + d_envelope_front
        d_vectors = geometry_pull((d_harmonics, d_envelope, d_bessel))[0]
        batch_slot = (batch_range == batch_index).astype(jnp.float32) * is_valid
        forces = forces + batch_slot[:, None, None] * d_vectors[None]
        grad_head = grad_head + is_valid * (g_head_read + g_head_front)
        grad_env = grad_env + is_valid * g_env
        grad_in = grad_in + is_valid * g_in
        grad_out = grad_out + is_valid * g_out
        grad_mix = grad_mix + is_valid * g_mix
        grad_embed = grad_embed + is_valid * g_embed
        grad_read = grad_read + is_valid * g_read
    grad_head, grad_env, grad_in, grad_out = ring_sum((grad_head, grad_env, grad_in, grad_out))
    read_full = lax.dynamic_update_slice_in_dim(
        jnp.zeros_like(read_weight), grad_read, core_index * shard_width, 0
    )
    chip_sums = [v + other_core(v) for v in (energies, grad_embed, core_lead * grad_mix, read_full, forces)]
    energies, grad_embed, grad_mix, read_full, forces = (
        v + lax.ppermute(v, "section", [(0, 1), (1, 0)]) for v in chip_sums
    )
    energies, grad_embed, grad_mix, read_full = ring_sum((energies, grad_embed, grad_mix, read_full))
    return (
        energies,
        -forces,
        grad_embed,
        grad_head[None],
        grad_env[None],
        grad_mix,
        grad_in[None],
        grad_out[None],
        read_full,
    )


CHUNKS = (128, 192, 160)
PLAN = (
    (0, 0, 256, 2, 1), (0, 256, 256, 1, 2), (1, 0, 640, 1, 2), (1, 640, 640, 1, 2), (2, 0, 608, 2, 1),
    (2, 608, 608, 1, 2),
)
EARLY = (0, 1)
ORDER = (
    0, 2, 4, 5, 2, 1, 2, 4, 3, 1, 5, 0, 4, 3, 2, 5, 1, 3, 4, 2, 5, 3, 0, 5, 3, 4, 2, 1, 5, 0, 3, 4,
)
LANES = 128
F32 = jnp.float32
BF16 = jnp.bfloat16
BESSEL_SCALE = (2.0 / CUTOFF) ** 0.5
ANGLE = 3.141592653589793 / CUTOFF


def dot_nn(left, right):
    return jnp.dot(left, right, preferred_element_type=F32)


def dot_nt(left, right):
    return lax.dot_general(left, right, (((1,), (1,)), ((), ())), preferred_element_type=F32)


def dot_tn(left, right):
    return lax.dot_general(left, right, (((0,), (0,)), ((), ())), preferred_element_type=F32)


def split_two(value):
    high = value.astype(BF16)
    return high, (value - high.astype(F32)).astype(BF16)


def split_three(value):
    high = value.astype(BF16)
    rest = value - high.astype(F32)
    middle = rest.astype(BF16)
    return high, middle, (rest - middle.astype(F32)).astype(BF16)


def six_pass(left, right):
    rows = left.shape[0]
    high, middle, low = split_three(left)
    three = dot_nn(jnp.concatenate([high, middle, low], axis=0), right[0])
    two = dot_nn(jnp.concatenate([high, middle], axis=0), right[1])
    small = three[2 * rows :] + two[rows:] + dot_nn(high, right[2])
    return three[:rows] + (three[rows : 2 * rows] + two[:rows] + small)


def three_pass(dot, left, right):
    rows = left.shape[0]
    high, low = split_two(left)
    both = dot(jnp.concatenate([high, low], axis=0), right[0])
    return both[:rows] + both[rows:] + dot(high, right[1])


def three_pass_tn(left, right):
    left_high, left_low = split_two(left)
    right_high, right_low = split_two(right)
    return dot_tn(
        jnp.concatenate([left_high, left_low, left_high], axis=0),
        jnp.concatenate([right_high, right_high, right_low], axis=0),
    )


def sigmoid(value):
    return 1.0 / (1.0 + jnp.exp(-value))


def order_of(component):
    return 0 if component == 0 else (1 if component < 4 else 2)


def same_sum(same, parts, split=split_three):
    pieces = split(jnp.concatenate(parts, axis=1))
    summed = dot_nn(same, pieces[-1])
    for piece in pieces[-2::-1]:
        summed = dot_nn(same, piece) + summed
    return [summed[:, LANES * m : LANES * (m + 1)] for m in range(len(parts))]


def place_columns(columns, first, width=LANES):
    lane = lax.broadcasted_iota(jnp.int32, (columns[0].shape[0], width), 1)
    out = jnp.zeros((columns[0].shape[0], width), F32)
    for i, column in enumerate(columns):
        out = jnp.where(lane == first + i, column, out)
    return out


def waves(length):
    turn = length * ANGLE - 1.5707963267948966
    square = turn * turn
    even, odd, term_even, term_odd = 1.0, 1.0, 1.0, 1.0
    coefficients_even, coefficients_odd = [], []
    for n in range(1, 9):
        term_even = -term_even / ((2 * n - 1) * (2 * n))
        term_odd = -term_odd / ((2 * n) * (2 * n + 1))
        coefficients_even.append(term_even)
        coefficients_odd.append(term_odd)
    even = jnp.full_like(turn, coefficients_even[-1])
    odd = jnp.full_like(turn, coefficients_odd[-1])
    for n in range(6, -1, -1):
        even = even * square + coefficients_even[n]
        odd = odd * square + coefficients_odd[n]
    sines = {1: even * square + 1.0}
    cosines = {1: -turn * (odd * square + 1.0)}
    for total, left, right in ((2, 1, 1), (3, 2, 1), (4, 2, 2), (5, 4, 1), (6, 4, 2), (7, 4, 3), (8, 4, 4)):
        sines[total] = sines[left] * cosines[right] + cosines[left] * sines[right]
        cosines[total] = cosines[left] * cosines[right] - sines[left] * sines[right]
    return [sines[k] for k in range(1, 9)], [cosines[k] for k in range(1, 9)]


def edge_values(edges, key_row, first, rows, full):
    block = edges[first : first + rows, :]
    vector = [block[:, i : i + 1] for i in range(3)]
    live = block[:, 6:7]
    squares = vector[0] * vector[0] + vector[1] * vector[1] + vector[2] * vector[2]
    length = jnp.sqrt(jnp.maximum(squares, 0.25))
    ux, uy, uz = (v / length for v in vector)
    ratio = jnp.minimum(length / CUTOFF, 1.0)
    second = ratio * ratio
    sixth = second * second * second
    envelope = (1.0 - 28.0 * sixth + 48.0 * (sixth * ratio) - 21.0 * (sixth * second)) * live
    harmonics = [
        jnp.ones_like(ux),
        ROOT_THREE * ux,
        ROOT_THREE * uy,
        ROOT_THREE * uz,
        ROOT_FIFTEEN * ux * uy,
        ROOT_FIFTEEN * uy * uz,
        0.5 * ROOT_FIVE * (3.0 * uz * uz - 1.0),
        ROOT_FIFTEEN * ux * uz,
        0.5 * ROOT_FIFTEEN * (ux * ux - uy * uy),
    ]
    same = jnp.where(block[:, 5:6] == key_row, 1.0, 0.0).astype(BF16)
    g = dict(
        env=envelope, harm=harmonics, same=same, squares=squares, length=length, ratio=ratio,
        unit=(ux, uy, uz), live=live, group=block[:, 7:8],
    )
    if full:
        sines, g["cosines"] = waves(length)
        g["bessel"] = [BESSEL_SCALE * value / length for value in sines]
        lane = lax.broadcasted_iota(jnp.int32, (rows, 16), 1).astype(F32)
        kinds = jnp.where(
            lane < NSPEC,
            jnp.where(block[:, 3:4] == lane, live, 0.0),
            jnp.where(block[:, 4:5] + NSPEC == lane, live, 0.0),
        )
        g["feat"] = kinds + place_columns(g["bessel"], 2 * NSPEC, 16)
    return g


def vector_pull(g, d_bessel, d_harm, d_envelope):
    ux, uy, uz = g["unit"]
    length, ratio = g["length"], g["ratio"]
    dx = ROOT_THREE * d_harm[1] + ROOT_FIFTEEN * (uy * d_harm[4] + uz * d_harm[7] + ux * d_harm[8])
    dy = ROOT_THREE * d_harm[2] + ROOT_FIFTEEN * (ux * d_harm[4] + uz * d_harm[5] - uy * d_harm[8])
    dz = (
        ROOT_THREE * d_harm[3]
        + ROOT_FIFTEEN * (uy * d_harm[5] + ux * d_harm[7])
        + (3.0 * ROOT_FIVE) * uz * d_harm[6]
    )
    left = 1.0 - ratio
    fourth = (ratio * ratio) * (ratio * ratio)
    d_length = (-168.0 / CUTOFF) * (fourth * ratio) * (left * left) * g["live"] * d_envelope
    d_length = d_length - (dx * ux + dy * uy + dz * uz) / length
    for k in range(NBES):
        slope = (BESSEL_SCALE * ANGLE * (k + 1)) * g["cosines"][k] - g["bessel"][k]
        d_length = d_length + d_bessel[k] * (slope / length)
    bound = jnp.where(g["squares"] > 0.25, 1.0, jnp.where(g["squares"] == 0.25, 0.5, 0.0))
    d_length = d_length * bound
    return [d / length + d_length * u for d, u in ((dx, ux), (dy, uy), (dz, uz))]


def env_terms(g, weight):
    scaled = ENV_SCALE * g["env"] * weight
    return same_sum(g["same"], [y * scaled for y in g["harm"]])


def pack_scalars(tensor, env):
    sums = [tensor[0] * env[0], tensor[1] * env[1], tensor[4] * env[4]]
    for m in (2, 3):
        sums[1] = sums[1] + tensor[m] * env[m]
    for m in (5, 6, 7, 8):
        sums[2] = sums[2] + tensor[m] * env[m]
    return jnp.concatenate([sums[0] + pltpu.roll(sums[1], 64, 1), sums[2]], axis=1)


def unpack_scalars(packed):
    first = packed[:, :LANES]
    return [first, pltpu.roll(first, 64, 1), packed[:, LANES:]]


def swap_order(lead, left, right):
    return jnp.where(lead, left, right), jnp.where(lead, right, left)


def env_pull(g, weight, d_env):
    d_terms = same_sum(g["same"], d_env, split_two)
    d_weight, d_harm, inner = None, [], None
    for m in range(9):
        part = g["harm"][m] * d_terms[m]
        d_weight = part if m == 0 else d_weight + part
        d_harm.append(jnp.sum(weight * d_terms[m], axis=1, keepdims=True))
        step = g["harm"][m] * d_harm[m]
        inner = step if m == 0 else inner + step
    scale = ENV_SCALE * g["env"]
    return scale * d_weight, [scale * d for d in d_harm], ENV_SCALE * inner


class Fetched:
    def __init__(self, source, buffer, semaphore):
        rows = source.shape[0]
        self.buffer, self.shape = buffer, buffer.shape
        target = buffer if rows == buffer.shape[0] else buffer.at[pl.ds(0, rows)]
        self.copy = pltpu.make_async_copy(source, target, semaphore)
        self.copy.start()
        self.arrived, self.pieces = False, {}
        if rows < buffer.shape[0]:
            buffer[rows:, :] = jnp.zeros((buffer.shape[0] - rows, buffer.shape[1]), F32)

    def __getitem__(self, where):
        if not self.arrived:
            self.copy.wait()
            self.arrived = True
        return self.buffer[where]

    def split(self, parts):
        if parts not in self.pieces:
            value = self[...]
            self.pieces[parts] = split_three(value) if parts == 3 else split_two(value)
        return self.pieces[parts]


class Stored:
    def __init__(self, target, buffer, semaphore):
        self.target, self.buffer, self.semaphore = target, buffer, semaphore
        self.shape, self.copy = buffer.shape, None

    def __setitem__(self, where, value):
        self.buffer[where] = value
        if where is Ellipsis:
            self.send()

    def __getitem__(self, where):
        return self.buffer[where]

    def send(self):
        self.copy = pltpu.make_async_copy(self.buffer, self.target, self.semaphore)
        self.copy.start()


def forward_pair(value, own, other):
    return [six_pass(value, own.split(3)), six_pass(value, other.split(3))]


def backward_pair(value, own, other, parts):
    return [three_pass(dot_nt, value, own.split(parts)), three_pass(dot_nt, value, other.split(parts))]


def first_forward(
    first, edges, key_row, lead_flag, embed,
    head_o, head_x, env_w, in_o, in_x, out_o, out_x,
    sent, soft_out, layer_in, slope_out, hidden,
):
    rows = sent.shape[0]
    lead = lead_flag[0:1, 0:1] > 0.5
    g = edge_values(edges, key_row[...], first, rows, True)
    pre = six_pass(g["feat"], split_three(embed[...]))
    soft = pre * sigmoid(pre)
    soft_out[...] = soft
    own, other = forward_pair(soft, head_o, head_x)
    latent = g["env"] * jnp.concatenate(swap_order(lead, own, other), axis=1)
    weight = six_pass(latent, env_w.split(3))
    env = env_terms(g, weight)
    scalars = pack_scalars([y * weight for y in g["harm"]], env)
    full = jnp.concatenate([latent, scalars], axis=1)
    layer_in[...] = full
    pre = jnp.concatenate(forward_pair(full, in_o, in_x), axis=1)
    gate = sigmoid(pre)
    slope_out[...] = gate * (1.0 + pre * (1.0 - gate))
    hid = pre * gate
    hidden[...] = hid
    half = hid.shape[1] // 2
    width = latent.shape[1]
    sent[:, :width] = (
        latent + six_pass(hid[:, :half], out_o.split(3)) + six_pass(hid[:, half:], out_x.split(3))
    )
    sent[:, width:] = weight
    sent.send()


def second_both(
    first, edges, key_row, mix, read, cot_row,
    arrived, env_w, in_o, in_x, out_o, out_x, head_o, head_x, env_wt,
    back, layer_in, d_pre_hidden, hidden, d_latent_out, latent_out, d_pre_read, d_weight_out,
    read_grad, mix_grad, energy_out,
):
    rows = back.shape[0]
    width = arrived.shape[1] - LANES
    half = width // 2
    g = edge_values(edges, key_row[...], first, rows, False)
    lane = lax.broadcasted_iota(jnp.int32, (rows, LANES), 1).astype(F32)
    group_hot = jnp.where(g["group"] == lane, g["live"], 0.0)
    cot = jnp.sum(group_hot * cot_row[...], axis=1, keepdims=True)
    mixes = [split_three(mix[i]) for i in range(3)]
    latent = arrived[:, :width]
    weight_first = arrived[:, width:]
    env_first = env_terms(g, weight_first)
    start = [y * weight_first for y in g["harm"]]
    coupled = [start[m] * env_first[0] + start[0] * env_first[m] for m in range(9)]
    members = ((0,), (1, 2, 3), (4, 5, 6, 7, 8))
    tensor = []
    for order in range(3):
        mixed = six_pass(jnp.concatenate([coupled[m] for m in members[order]], axis=0), mixes[order])
        tensor += [mixed[rows * i : rows * (i + 1)] for i in range(len(members[order]))]
    weight = six_pass(latent, env_w.split(3))
    env = env_terms(g, weight)
    full = jnp.concatenate([latent, pack_scalars(tensor, env)], axis=1)
    layer_in[...] = full
    pre = jnp.concatenate(forward_pair(full, in_o, in_x), axis=1)
    gate = sigmoid(pre)
    slope = gate * (1.0 + pre * (1.0 - gate))
    hid = pre * gate
    hidden[...] = hid
    latent_next = (
        latent + six_pass(hid[:, :half], out_o.split(3)) + six_pass(hid[:, half:], out_x.split(3))
    )
    latent_out[...] = latent_next
    pre_read = jnp.concatenate(forward_pair(latent_next, head_o, head_x), axis=1)
    gate = sigmoid(pre_read)
    soft = pre_read * gate
    line = read[...]
    inner = jnp.sum(soft * line, axis=1, keepdims=True)
    energy_out[...] = jnp.broadcast_to(
        jnp.sum(group_hot * (g["env"] * inner), axis=0, keepdims=True), energy_out.shape
    )
    scaled_cot = cot * g["env"]
    read_grad[...] = jnp.broadcast_to(
        jnp.sum(scaled_cot * soft, axis=0, keepdims=True), read_grad.shape
    )
    d_envelope = cot * inner
    d_read = scaled_cot * line * (gate * (1.0 + pre_read * (1.0 - gate)))
    d_pre_read[...] = d_read
    d_latent_out[...] = three_pass(dot_nt, d_read[:, :half], head_o.split(3)) + three_pass(
        dot_nt, d_read[:, half:], head_x.split(3)
    )
    d_hid = jnp.concatenate(backward_pair(d_latent_out[...], out_o, out_x, 3), axis=1)
    d_pre = d_hid * slope
    d_pre_hidden[...] = d_pre
    d_full = three_pass(dot_nt, d_pre[:, :half], in_o.split(3)) + three_pass(
        dot_nt, d_pre[:, half:], in_x.split(3)
    )
    d_scalars = unpack_scalars(d_full[:, width:])
    d_tensor = [d_scalars[order_of(m)] * env[m] for m in range(9)]
    d_env = [d_scalars[order_of(m)] * tensor[m] for m in range(9)]
    d_weight, d_harm, d_more = env_pull(g, weight, d_env)
    d_envelope = d_envelope + d_more
    d_weight_out[...] = d_weight
    back[:, :width] = (
        three_pass(dot_nn, d_weight_out[...], env_wt.split(2))
        + d_latent_out[...]
        + d_full[:, :width]
    )
    d_coupled = []
    for order in range(3):
        joined = jnp.concatenate([d_tensor[m] for m in members[order]], axis=0)
        mix_grad[order] = three_pass_tn(
            jnp.concatenate([coupled[m] for m in members[order]], axis=0), joined
        )
        mixed = three_pass(dot_nt, joined, mixes[order])
        d_coupled += [mixed[rows * i : rows * (i + 1)] for i in range(len(members[order]))]
    mix_grad.send()
    d_env_first = [d_coupled[m] * start[0] for m in range(9)]
    d_start = [d_coupled[m] * env_first[0] for m in range(9)]
    for m in range(9):
        d_env_first[0] = d_env_first[0] + d_coupled[m] * start[m]
        d_start[0] = d_start[0] + d_coupled[m] * env_first[m]
    d_first, d_harm_first, d_more = env_pull(g, weight_first, d_env_first)
    for m in range(9):
        d_first = d_first + g["harm"][m] * d_start[m]
        d_harm[m] = (
            d_harm[m]
            + d_harm_first[m]
            + jnp.sum(weight_first * d_start[m], axis=1, keepdims=True)
        )
    d_envelope = d_envelope + d_more
    back[:, width:] = d_first + place_columns(d_harm + [d_envelope], 64)
    back.send()


def first_backward(
    first, edges, key_row, lead_flag, embed,
    layer_in, env_w, arrived, out_o, out_x, slope_in, in_o, in_x, env_wt, head_o, head_x,
    d_vector, d_head, d_pre_hidden, d_weight_out, embed_grad,
):
    rows = arrived.shape[0]
    width = arrived.shape[1] - LANES
    half = width // 2
    lead = lead_flag[0:1, 0:1] > 0.5
    g = edge_values(edges, key_row[...], first, rows, True)
    embed_pair = split_two(embed[...])
    latent = layer_in[:, :width]
    weight = three_pass(dot_nn, latent, env_w.split(2))
    env = env_terms(g, weight)
    extra = arrived[:, width:]
    lane = lax.broadcasted_iota(jnp.int32, extra.shape, 1)
    d_weight = jnp.where(lane < 64, extra, 0.0)
    d_harm = [extra[:, 64 + m : 65 + m] for m in range(9)]
    d_envelope = extra[:, 73:74]
    d_hid = jnp.concatenate(backward_pair(arrived[:, :width], out_o, out_x, 2), axis=1)
    d_pre = d_hid * slope_in[...]
    d_pre_hidden[...] = d_pre
    d_full = three_pass(dot_nt, d_pre[:, :half], in_o.split(2)) + three_pass(
        dot_nt, d_pre[:, half:], in_x.split(2)
    )
    d_scalars = unpack_scalars(d_full[:, width:])
    d_start = [d_scalars[order_of(m)] * env[m] for m in range(9)]
    d_env = [d_scalars[order_of(m)] * (g["harm"][m] * weight) for m in range(9)]
    d_more_weight, d_more_harm, d_more = env_pull(g, weight, d_env)
    d_weight = d_weight + d_more_weight
    d_envelope = d_envelope + d_more
    for m in range(9):
        d_weight = d_weight + g["harm"][m] * d_start[m]
        d_harm[m] = (
            d_harm[m] + d_more_harm[m] + jnp.sum(weight * d_start[m], axis=1, keepdims=True)
        )
    d_weight_out[...] = d_weight
    d_latent = (
        three_pass(dot_nn, d_weight_out[...], env_wt.split(2))
        + arrived[:, :width]
        + d_full[:, :width]
    )
    d_own, d_other = swap_order(lead, d_latent[:, :half], d_latent[:, half:])
    d_head[:, :half] = g["env"] * d_own
    d_head[:, half:] = g["env"] * d_other
    d_head.send()
    d_soft = three_pass(dot_nt, d_own, head_o.split(2)) + three_pass(dot_nt, d_other, head_x.split(2))
    pre = three_pass(dot_nn, g["feat"], embed_pair)
    gate = sigmoid(pre)
    d_envelope = d_envelope + jnp.sum(pre * gate * d_soft, axis=1, keepdims=True)
    d_pre = g["env"] * d_soft * (gate * (1.0 + pre * (1.0 - gate)))
    d_feat = three_pass(dot_nt, d_pre, embed_pair)
    embed_grad[...] = three_pass_tn(g["feat"], d_pre)
    d_bessel = [d_feat[:, 2 * NSPEC + k : 2 * NSPEC + 1 + k] for k in range(NBES)]
    d_vector[...] = place_columns(vector_pull(g, d_bessel, d_harm, d_envelope), 0)


def outer_sum(split_left, chosen, *refs):
    count = len(CHUNKS)
    extra = len(refs) > 4 * count + 8
    kinds = 3 if extra else 2
    sources = [
        [refs[(kinds * side + i) * count : (kinds * side + i + 1) * count] for i in range(kinds)]
        for side in range(2)
    ]
    rest = refs[2 * kinds * count :]
    outs = [Stored(rest[i], rest[kinds + i], rest[-1].at[i]) for i in range(kinds)]
    buffers = rest[2 * kinds : 3 * kinds]
    semaphores = rest[-2]

    def copies(side):
        for i in range(kinds):
            start = 0
            for k, source in enumerate(sources[side][i]):
                rows, columns = source.shape[0], buffers[i].shape[1]
                yield pltpu.make_async_copy(
                    source.at[:, pl.ds(0, columns)],
                    buffers[i].at[pl.ds(start, rows)],
                    semaphores.at[i * count + k],
                )
                start += rows

    for side in range(2):

        @pl.when(chosen[0] == side)
        def _(side=side):
            for copy in copies(side):
                copy.start()

    for copy in copies(0):
        copy.wait()
    left_high, left_low = split_two(buffers[0][...])
    right_high, right_low = split_two(buffers[1][...])
    left = jnp.concatenate([left_high, left_low, left_high], axis=0)
    right = jnp.concatenate([right_high, right_high, right_low], axis=0)
    if split_left:
        half = left.shape[1] // 2
        outs[1][...] = dot_tn(left[:, half:], right)
        outs[0][...] = dot_tn(left[:, :half], right)
    else:
        half = right.shape[1] // 2
        outs[1][...] = dot_tn(left, right[:, half:])
        outs[0][...] = dot_tn(left, right[:, :half])
    if extra:
        right_high, right_low = split_two(buffers[2][...])
        right = jnp.concatenate([right_high, right_high, right_low], axis=0)
        outs[2][...] = dot_tn(left[:, : outs[2].shape[0]], right)
    for out in outs:
        out.copy.wait()


def on_core(body, outs, flops, args, fetched, chosen):
    here = pl.BlockSpec(memory_space=pltpu.VMEM)
    there = pl.BlockSpec(memory_space=pl.ANY)
    pad = 2 * LANES
    tall = [(m.shape[0] + pad - 1) // pad * pad if m.shape[0] > pad else m.shape[0] for m in fetched]
    scratch = [pltpu.VMEM((rows, m.shape[1]), F32) for rows, m in zip(tall, fetched)]
    scratch += [pltpu.VMEM(shape, F32) for shape in outs]
    scratch.append(pltpu.SemaphoreType.DMA((len(fetched),)))
    scratch.append(pltpu.SemaphoreType.DMA((len(outs),)))

    def guarded(flag, *refs):
        @pl.when(flag[0] == 1)
        def _():
            small, rest = refs[: len(args)], refs[len(args) :]
            sources, rest = rest[: len(fetched)], rest[len(fetched) :]
            targets, rest = rest[: len(outs)], rest[len(outs) :]
            buffers, rest = rest[: len(fetched)], rest[len(fetched) :]
            kept, (arrivals, departures) = rest[: len(outs)], rest[len(outs) :]
            inputs = [Fetched(s, b, arrivals.at[i]) for i, (s, b) in enumerate(zip(sources, buffers))]
            outputs = [Stored(t, b, departures.at[i]) for i, (t, b) in enumerate(zip(targets, kept))]
            body(*small, *inputs, *outputs)
            for output in outputs:
                output.copy.wait()

    return pl.pallas_call(
        guarded,
        out_shape=tuple(jax.ShapeDtypeStruct(shape, F32) for shape in outs),
        in_specs=[pl.BlockSpec(memory_space=pltpu.SMEM)] + [here] * len(args) + [there] * len(fetched),
        out_specs=tuple(there for _ in outs),
        scratch_shapes=scratch,
        compiler_params=pltpu.CompilerParams(vmem_limit_bytes=60 * 2**20),
        cost_estimate=pl.CostEstimate(flops=flops, bytes_accessed=16 * 2**20, transcendentals=0),
    )(chosen, *args, *fetched)


def outer_call(split_left, outs, widths, flops, chosen, first, second):
    there = pl.BlockSpec(memory_space=pl.ANY)
    args = [array for side in (first, second) for factor in side for array in factor]
    return pl.pallas_call(
        partial(outer_sum, split_left),
        out_shape=tuple(jax.ShapeDtypeStruct(shape, F32) for shape in outs),
        in_specs=[pl.BlockSpec(memory_space=pltpu.SMEM)] + [there] * len(args),
        out_specs=tuple(there for _ in outs),
        scratch_shapes=[pltpu.VMEM(shape, F32) for shape in outs]
        + [pltpu.VMEM((sum(CHUNKS), w), F32) for w in widths]
        + [
            pltpu.SemaphoreType.DMA((len(widths) * len(CHUNKS),)),
            pltpu.SemaphoreType.DMA((len(outs),)),
        ],
        compiler_params=pltpu.CompilerParams(vmem_limit_bytes=60 * 2**20),
        cost_estimate=pl.CostEstimate(flops=flops, bytes_accessed=16 * 2**20, transcendentals=0),
    )(chosen, *args)


def gather_blocks(value):
    count = lax.axis_size("edge")
    if count & (count - 1) or count > 8:
        return lax.all_gather(value, "edge", axis=0)
    index = lax.axis_index("edge")
    out = value[None]
    step = 1
    while step < count:
        got = lax.ppermute(out, "edge", [(i, i ^ step) for i in range(count)])
        low = (index // step) % 2 == 0
        out = jnp.where(low, jnp.concatenate([out, got]), jnp.concatenate([got, out]))
        step *= 2
    return out


def prefix_in_rows(flags):
    rows, length = flags.shape
    pieces = flags.reshape(rows, length // LANES, LANES)
    upper = (jnp.arange(LANES)[:, None] <= jnp.arange(LANES)[None, :]).astype(F32)
    inner = jnp.einsum("rkl,lm->rkm", pieces, upper, precision=HIGHEST)
    totals = inner[:, :, -1]
    count = length // LANES
    before = (jnp.arange(count)[:, None] < jnp.arange(count)[None, :]).astype(F32)
    offsets = jnp.dot(totals, before, precision=HIGHEST)
    return (inner + offsets[:, :, None]).reshape(rows, length)


def pack_edges(atoms, vectors, species, centres, mask, structures, out):
    count = centres.shape[1]
    for b in range(centres.shape[0]):
        span = slice(b * count, (b + 1) * count)
        vector = vectors[b]
        out[0:3, span] = vector
        out[3:5, span] = species[b].astype(F32)
        out[5:6, span] = (centres[b : b + 1, :] + b * atoms).astype(F32)
        squares = jnp.maximum(jnp.sum(vector * vector, axis=0, keepdims=True), 0.25)
        near = jnp.where(jnp.sqrt(squares) / CUTOFF < 1.0, 1.0, 0.0)
        out[6:7, span] = jnp.where(mask[b : b + 1, :] > 0, near, 0.0)
        out[7:8, span] = (structures[b : b + 1, :] + b * STRUCTS).astype(F32)


def plan_edges(edge_vectors, edge_species, centres, edge_mask, structures):
    batch_count, _, edge_count = edge_vectors.shape
    blocks = lax.axis_size("edge")
    block = lax.axis_index("edge")
    core = lax.axis_index("mp")
    atoms = blocks * ATOM_DEV
    per_block = batch_count * edge_count
    raw = pl.pallas_call(
        partial(pack_edges, atoms), out_shape=jax.ShapeDtypeStruct((8, per_block), F32)
    )(edge_vectors, edge_species, centres, edge_mask, structures)
    gathered = gather_blocks(raw)
    keys = gathered[:, 5].reshape(blocks, batch_count, edge_count)
    alive = gathered[:, 6].reshape(blocks, batch_count, edge_count)
    local = keys - (jnp.arange(batch_count) * atoms)[None, :, None].astype(F32)
    degree = jnp.sum(
        jnp.where(
            local.transpose(1, 0, 2).reshape(batch_count, 1, -1)
            == jnp.arange(atoms, dtype=F32)[None, :, None],
            alive.transpose(1, 0, 2).reshape(batch_count, 1, -1),
            0.0,
        ),
        axis=2,
    )
    spans = batch_count * ATOM_DEV
    degree = degree.reshape(batch_count, blocks, ATOM_DEV).transpose(1, 0, 2).reshape(blocks, spans)
    upper = (jnp.arange(spans)[:, None] <= jnp.arange(spans)[None, :]).astype(F32)
    upto = jnp.dot(degree, upper, precision=HIGHEST)
    start = jnp.zeros((blocks, 1), F32)
    starts = [start]
    for size in CHUNKS:
        for _ in range(2):
            start = jnp.max(jnp.where(upto <= start + size, jnp.maximum(upto, start), start), axis=1, keepdims=True)
            starts.append(start)
    fits = jnp.all(starts[-1] >= upto[:, -1:])
    starts = jnp.concatenate(starts[:-1], axis=1)
    own_before = (upto - degree)[block]
    bin_of = jnp.sum((own_before[:, None] >= starts[block][None, 1:]).astype(F32), axis=1)
    padded = jnp.concatenate([jnp.zeros_like(gathered[:1]), gathered, jnp.zeros_like(gathered[:1])])
    window = lax.dynamic_slice_in_dim(padded, block, 3, 0)
    flat = window.transpose(1, 0, 2).reshape(8, 3 * per_block)
    position = jnp.arange(3 * per_block)
    batch_flat = (position % per_block) // edge_count
    spot = flat[5] - (batch_flat * atoms + block * ATOM_DEV).astype(F32)
    mine = (spot >= 0) & (spot < ATOM_DEV) & (flat[6] > 0.5)
    slot = jnp.where(mine, spot + (batch_flat * ATOM_DEV).astype(F32), -1.0)
    chosen = jnp.sum(
        jnp.where(jnp.arange(spans, dtype=F32)[:, None] == slot[None, :], bin_of[:, None], 0.0), axis=0
    )
    wanted = 2 * jnp.arange(len(CHUNKS)) + core
    picked = (chosen[None, :] == wanted[:, None].astype(F32)) & mine[None, :]
    rank = prefix_in_rows(picked.astype(F32)) - 1.0
    offsets = [sum(CHUNKS[:k]) for k in range(len(CHUNKS))]
    place = jnp.sum(
        jnp.where(picked, rank + jnp.array(offsets, F32)[:, None], 0.0), axis=0
    ) - (1.0 - jnp.sum(picked.astype(F32), axis=0))
    total = sum(CHUNKS)
    hot = (place[None, :] == jnp.arange(total, dtype=F32)[:, None]).astype(F32)
    edges = lax.dot_general(hot, flat, (((1,), (1,)), ((), ())), precision=HIGHEST)
    return fits, edges, place


def tied(first, *others):
    return lax.optimization_barrier((first, others))[0]


def hop(value, distance):
    return lax.ppermute(value, "edge", [(i, i ^ distance) for i in range(8)])


def halves(value, second):
    half = value.shape[0] // 2
    kept = lax.dynamic_slice_in_dim(value, second * half, half, 0)
    return kept, lax.dynamic_slice_in_dim(value, (1 - second) * half, half, 0)


def joined(kept, got, second):
    return jnp.where(second == 0, jnp.concatenate([kept, got]), jnp.concatenate([got, kept]))


def sum_steps(value, outer_hop, inner_hop, wait):
    index = lax.axis_index("edge")
    seconds = {1: index % 2, 2: ((index // 2) ^ (index // 4)) % 2}
    kept, given = halves(value, seconds[outer_hop])
    given = wait(given)
    got = hop(given, outer_hop)
    yield given
    kept, given = halves(kept + wait(got), seconds[inner_hop])
    got = hop(given, inner_hop)
    yield given
    part = kept + wait(got)
    got = hop(part, 6)
    yield part
    part = part + wait(got)
    got = hop(part, inner_hop)
    yield part
    part = joined(part, wait(got), seconds[inner_hop])
    half = part.shape[0]
    got = hop(part, outer_hop)
    yield part
    yield [(part, seconds[outer_hop] * half), (wait(got), (1 - seconds[outer_hop]) * half)]


class BlockSums:
    def __init__(self, plan):
        self.plan, self.steps, self.sums, self.moment = plan, {}, {}, None

    def wait(self, value):
        return value if self.moment is None else tied(value, self.moment)

    def advance(self, matrices, order):
        for piece in order:
            which, first, rows, outer_hop, inner_hop = self.plan[piece]
            if piece not in self.steps:
                value = lax.slice_in_dim(matrices[which], first, first + rows, axis=0)
                self.steps[piece] = sum_steps(value, outer_hop, inner_hop, self.wait)
            given = next(self.steps[piece])
            if isinstance(given, list):
                total = self.sums.get(which, jnp.zeros_like(matrices[which]))
                for part, start in given:
                    total = lax.dynamic_update_slice_in_dim(total, part, first + start, 0)
                self.sums[which] = total
                given = given[1][0]
            self.moment = given


def fast_device(edges, place, others, args):
    (
        edge_vectors, edge_species, centres, edge_mask, structures, energy_cot, embed_in,
        section_head, env_weight, mix_weight, w_in, w_out, read_weight,
    ) = args
    is_first = lax.axis_index("section") == 0
    core = lax.axis_index("mp")
    width = section_head.shape[1]
    half = section_head.shape[2]
    batch_count, _, edge_count = edge_vectors.shape
    chan_count = mix_weight.shape[1]
    gap = LANES - chan_count
    read_left, read_right = read_weight[:half], read_weight[half:]
    read_line = jnp.where(
        core == 0,
        jnp.concatenate([read_left, read_right]),
        jnp.concatenate([read_right, read_left]),
    )[None]
    cot_row = jnp.pad(energy_cot.reshape(1, -1), ((0, 0), (0, LANES - energy_cot.size)))
    lead_flag = jnp.full((8, LANES), 1.0, F32) * (core == 0).astype(F32)
    mix = jnp.pad(mix_weight, ((0, 0), (0, gap), (0, gap)))
    env_w = jnp.pad(env_weight[0], ((0, 0), (0, gap)))
    env_wt = env_w.T
    heads, ins, outs_w = (section_head[0], others[0]), (w_in[0], others[1]), (w_out[0], others[2])
    count = len(CHUNKS)
    offsets = [sum(CHUNKS[:k]) for k in range(count)]
    rows = [edges[o : o + m, 5].reshape(1, -1) for o, m in zip(offsets, CHUNKS)]
    layer_width = width + 2 * LANES

    first_flag = jnp.full((1,), 1, jnp.int32) * is_first.astype(jnp.int32)
    second_flag = 1 - first_flag
    saved, moved = [], []
    for k, m in enumerate(CHUNKS):
        outs = [(m, width + LANES), (m, width), (m, layer_width), (m, width), (m, width)]
        work = 12 * m * width * (3 * width + 384)
        result = on_core(
            partial(first_forward, offsets[k]), outs, work,
            (edges, rows[k], lead_flag, embed_in), (*heads, env_w, *ins, *outs_w), first_flag,
        )
        moved.append(shifted(result[0], "section", 1))
        saved.append(result[1:])
    seconds, returned, firsts = [], [], []
    for k, m in enumerate(CHUNKS):
        outs = [
            (m, width + LANES), (m, layer_width), (m, width), (m, width), (m, width),
            (m, width), (m, width), (m, LANES), (8, width), (3, LANES, LANES), (8, LANES),
        ]
        work = 18 * m * width * (3 * width + 384)
        seconds.append(
            on_core(
                partial(second_both, offsets[k]), outs, work,
                (edges, rows[k], mix, read_line, cot_row),
                (moved[k], env_w, *ins, *outs_w, *heads, env_wt), second_flag,
            )
        )
    outer_work = 6 * sum(CHUNKS) * width * width
    by_hand = lax.axis_size("edge") == 8
    sums = BlockSums(PLAN)
    for k, m in enumerate(CHUNKS):
        arrived = shifted(seconds[k][0], "section", -1)
        if k > 0:
            arrived = tied(arrived, firsts[k - 1][0])
        returned.append(arrived)
        if k == count - 1:
            out_own, out_other = outer_call(
                True, [(half, width)] * 2, (width, width), outer_work, second_flag,
                ([s[3] for s in saved], returned),
                ([s[3] for s in seconds], [s[4] for s in seconds]),
            )
            arrived = tied(arrived, out_other)
            grad_out = out_own + other_core(out_other)
            if by_hand:
                sums.advance([grad_out], EARLY)
        outs = [(m, LANES), (m, width), (m, width), (m, LANES), (16, width)]
        work = 9 * m * width * (3 * width + 384)
        firsts.append(
            on_core(
                partial(first_backward, offsets[k]), outs, work,
                (edges, rows[k], lead_flag, embed_in),
                (saved[k][1], env_w, arrived, *outs_w, saved[k][2], *ins, env_wt, *heads), first_flag,
            )
        )
    in_own, in_other, grad_env = outer_call(
        False, [(layer_width, half)] * 2 + [(width, LANES)], (layer_width, width, LANES), outer_work,
        sums.wait(second_flag),
        ([s[1] for s in saved], [f[2] for f in firsts], [f[3] for f in firsts]),
        ([s[1] for s in seconds], [s[2] for s in seconds], [s[7] for s in seconds]),
    )
    grad_in = in_own + other_core(in_other)
    if by_hand:
        sums.moment = (sums.moment, in_other)
        sums.advance([grad_out], EARLY)
    head_own, head_other = outer_call(
        False, [(width, half)] * 2, (width, width), outer_work, tied(second_flag, in_other, sums.moment),
        ([s[0] for s in saved], [f[1] for f in firsts]),
        ([s[5] for s in seconds], [s[6] for s in seconds]),
    )
    none = jnp.zeros((), F32)
    read_sum = sum(s[8][0] for s in seconds)
    read_sum = jnp.where(
        core == 0, read_sum, jnp.concatenate([read_sum[half:], read_sum[:half]])
    )
    mix_sum = sum(s[9] for s in seconds)[:, :chan_count, :chan_count].reshape(-1, width)
    energy_sum = sum(s[10][0] for s in seconds)
    embed_sum = sum(f[4] for f in firsts)
    small_second = jnp.concatenate(
        [read_sum[None], jnp.pad(energy_sum, (0, width - LANES))[None], mix_sum]
    )
    small_second = jnp.pad(small_second, ((0, 16 - small_second.shape[0]), (0, 0)))
    small = jnp.concatenate(
        [jnp.where(is_first, embed_sum, none), jnp.where(is_first, none, small_second)]
    )
    small = sums.wait(small)
    small = small + lax.ppermute(small, "section", [(0, 1), (1, 0)])
    small = jnp.concatenate([small, grad_env[:, :chan_count].reshape(-1, width)]).reshape(-1, half)
    head_own = jnp.concatenate([head_own, small])
    grad_head = head_own + other_core(jnp.concatenate([head_other, small]))
    total = sum(CHUNKS)
    hot = (place[None, :] == jnp.arange(total, dtype=F32)[:, None]).astype(F32)
    d_vectors = jnp.concatenate([f[0][:, :8] for f in firsts])
    spread = lax.dot_general(d_vectors, hot, (((0,), (0,)), ((), ())), precision=HIGHEST)[:3]
    spread = jnp.where(is_first, spread, none)
    if by_hand:
        matrices = [grad_out, grad_in, grad_head]
        sums.moment = (sums.moment, head_other, grad_in)
        sums.advance(matrices, ORDER[:8])
        spread = sums.wait(spread)
        spread = spread + other_core(spread)
        sums.advance(matrices, ORDER[8:16])
        spread = sums.wait(spread)
        sums.advance(matrices, ORDER[16:])
        grad_out, grad_in, grad_head = (sums.sums[i] for i in range(3))
    else:
        spread = spread + other_core(spread)
        grad_out, grad_in, grad_head = lax.psum((grad_out, grad_in, grad_head), "edge")
    per_block = batch_count * edge_count
    to_left, kept, to_right = (spread[:, i * per_block : (i + 1) * per_block] for i in range(3))
    forces = kept + shifted(to_right, "edge", 1) + shifted(to_left, "edge", -1)
    small = grad_head[width:].reshape(-1, width)
    grad_head = grad_head[:width]
    grad_embed, grad_read = small[:16], small[16]
    energies = small[17, : energy_cot.size].reshape(energy_cot.shape)
    grad_mix = small[18 : 18 + mix_sum.shape[0]].reshape(mix_weight.shape)
    grad_env = small[32:].reshape(width, chan_count)

    forces = jnp.where(is_first, forces, shifted(forces, "section", 1))
    forces = -forces.reshape(3, batch_count, edge_count).transpose(1, 0, 2)
    return (
        energies, forces, grad_embed, grad_head[None], grad_env[None], grad_mix,
        grad_in[None, : w_in.shape[1]], grad_out[None], grad_read,
    )


def per_device(*args):
    section_head, w_in, w_out = args[7], args[10], args[11]
    others = tuple(other_core(m[0]) for m in (section_head, w_in, w_out))
    fits, edges, place = plan_edges(*args[:5])
    results = fast_device(edges, place, others, args)

    def again(state):
        rest, _ = state
        held, rest = lax.optimization_barrier((args, rest))
        return rest - 1, general_device(*held)

    overflow = 1 - fits.astype(jnp.int32)
    return lax.while_loop(lambda state: state[0] > 0, again, (overflow, results))[1]


def solution(mesh):
    placed = (
        P(None, None, "edge"),
        P(None, None, "edge"),
        P(None, "edge"),
        P(None, "edge"),
        P(None, "edge"),
        P(),
        P(),
        P("section", None, "mp"),
        P("section", None, None),
        P(),
        P("section", None, "mp"),
        P("section", "mp", None),
        P(),
    )
    return jax.shard_map(
        per_device,
        mesh=mesh,
        in_specs=placed,
        out_specs=(
            P(),
            P(None, None, "edge"),
            P(),
            P("section", None, "mp"),
            P("section", None, None),
            P(),
            P("section", None, "mp"),
            P("section", "mp", None),
            P(),
        ),
        check_vma=False,
    )
```
